128 devices in a mesh: dp: 16 (over y_lo, z, core), mp: 8 (over y_hi, x).
Axes of the slice: x: 4, y: 4 (y_hi: 2, y_lo: 2; y = y_hi * 2 + y_lo), z: 4, core: 2. Of those that a mesh axis runs over, the one named last changes fastest.
Arguments:
- tokens: bfloat16 [16, 8, 256, 1536], P('dp', None, 'mp'), may hold values from -6 to 6
- seq_len: int32 [16], P('dp'), may hold values from 1024 to 2048, as said below
- norm_gain: float32 [1536], replicated, may hold values from 0.5 to 1.5
- main_weight: bfloat16 [1536, 2, 3072], P('dp', None, 'mp'), may hold values from -0.15625 to 0.15625
- side_weight: bfloat16 [1536, 304], P('dp'), may hold values from -0.15625 to 0.15625
- side_terms: float32 [5, 256], replicated, as said below
- channel_terms: float32 [6, 3072], P(None, 'mp'), as said below
- head_terms: float32 [3, 48], P(None, 'mp'), as said below
- output_weight: bfloat16 [3072, 1536], P('mp', 'dp'), may hold values from -0.109375 to 0.109375
- cotangent: bfloat16 [16, 8, 256, 1536], P('dp', None, 'mp'), may hold values from -6 to 6
Outputs:
- layer_out: bfloat16 [16, 8, 256, 1536], P('dp', None, 'mp')
- token_grad: float32 [16, 8, 256, 1536], P('dp', None, 'mp')
- norm_gain_grad: float32 [1536], replicated
- main_weight_grad: float32 [1536, 2, 3072], P('dp', None, 'mp')
- side_weight_grad: float32 [1536, 304], P('dp')
- side_terms_grad: float32 [5, 256], replicated
- channel_terms_grad: float32 [6, 3072], P(None, 'mp')
- head_terms_grad: float32 [3, 48], P(None, 'mp')
- output_weight_grad: float32 [3072, 1536], P('mp', 'dp')
The draws below stay inside these ranges and needn't reach their ends.
Inputs may be any that keep to these rules, and one draw needn't show every extreme that they name: `seq_len`: lengths of the sequences; one buffer is full and one is half full in every draw. `side_terms`: taps and biases of order one. `channel_terms`: taps and biases of order one, then gains near one. `head_terms`: step biases below zero, log rates of order one, skip factors near one.
All inputs are finite; a program needn't handle non-finite values.
Results may differ from the reference program's by a relative error of at most 0.02.
Values may be sent and summed in bfloat16 or wider, within the bound.
A program may use at most 192 MiB of HBM per device.

```python
import jax
import jax.numpy as jnp
from jax import lax

D = 1536
HEADS = 48
STATE = 128
CONV = 4
CL = 256
STRETCHES = 8
INNER = 3072
SIDE = 304
N_DP = 16


def draw_seq_len(key, part):
    key = jax.random.fold_in(key, 11)
    first, second = jax.random.split(key)
    total = STRETCHES * CL
    lengths = jax.random.randint(first, (N_DP,), total // 2, total + 1)
    order = jax.random.permutation(second, N_DP)
    lengths = lengths.at[order[0]].set(total)
    lengths = lengths.at[order[1]].set(total // 2)
    return lengths.astype(jnp.int32)


def draw_side_terms(key, part):
    key = jax.random.fold_in(key, 17)
    first, second = jax.random.split(key)
    taps = 0.5 * jax.random.normal(first, (CONV, 2 * STATE), jnp.float32)
    bias = 0.3 * jax.random.normal(second, (1, 2 * STATE), jnp.float32)
    return jnp.concatenate([taps, bias], 0)


def draw_channel_terms(key, part):
    key = jax.random.fold_in(key, 19)
    first, second, third = jax.random.split(key, 3)
    taps = 0.5 * jax.random.normal(first, (CONV, INNER), jnp.float32)
    bias = 0.3 * jax.random.normal(second, (1, INNER), jnp.float32)
    gain = 1.0 + jax.random.uniform(third, (1, INNER), jnp.float32, -0.4, 0.4)
    return jnp.concatenate([taps, bias, gain], 0)


def draw_head_terms(key, part):
    key = jax.random.fold_in(key, 23)
    first, second, third = jax.random.split(key, 3)
    bias = jax.random.uniform(first, (1, HEADS), jnp.float32, -4.0, -1.0)
    rate = jax.random.uniform(second, (1, HEADS), jnp.float32, -0.7, 2.8)
    skip = jax.random.uniform(third, (1, HEADS), jnp.float32, 0.5, 1.5)
    return jnp.concatenate([bias, rate, skip], 0)


def levels(rng, extent, cuts, least, top_value):
    loudness = 1.0
    for axis_at, shards_of in cuts:
        steps = jax.random.uniform(jax.random.fold_in(jax.random.fold_in(rng, 6), axis_at), (shards_of,), jnp.float32, least / len(cuts), top_value / len(cuts))
        loudness = loudness * jnp.repeat(jnp.exp(steps), extent[axis_at] // shards_of).reshape((-1,) + (1,) * (len(extent) - 1 - axis_at))
    return loudness


def bell_draw(own_key, extent, deviation, bound, cuts=(), kind=jnp.bfloat16):
    drawn = jax.random.normal(own_key, extent, jnp.float32) * deviation
    if len(cuts) > 0:
        drawn = levels(own_key, extent, cuts, -0.22, 0.18) * drawn
    return jnp.clip(drawn, min=-bound, max=bound).astype(kind)


def setup_inputs(seed: int = 0) -> dict:
    splits = jax.random.split(jax.random.key(seed), 11)
    return {
        "tokens": bell_draw(splits[0], (N_DP, STRETCHES, CL, D), 1.0, 6.0, ((0, 16), (2, 8))),
        "seq_len": draw_seq_len(jax.random.fold_in(splits[10], 71), 0),
        "norm_gain": jnp.clip(1.0 + 0.1 * jax.random.normal(splits[2], (D,), jnp.float32), 0.5, 1.5),
        "main_weight": bell_draw(splits[3], (D, 2, INNER), D ** -0.5, 0.15625, ((0, 16), (2, 8))),
        "side_weight": bell_draw(splits[4], (D, SIDE), D ** -0.5, 0.15625, ((0, 16),)),
        "side_terms": draw_side_terms(jax.random.fold_in(splits[10], 71), 0),
        "channel_terms": draw_channel_terms(jax.random.fold_in(splits[10], 71), 0),
        "head_terms": draw_head_terms(jax.random.fold_in(splits[10], 71), 0),
        "output_weight": bell_draw(splits[8], (INNER, D), INNER ** -0.5, 0.109375, ((0, 8), (1, 16))),
        "cotangent": bell_draw(splits[9], (N_DP, STRETCHES, CL, D), 1.0, 6.0, ((0, 16), (2, 8))),
    }


@jax.custom_vjp
def low(v):
    return lax.optimization_barrier(v.astype(jnp.bfloat16)).astype(jnp.float32)

@jax.custom_vjp
def low_back(v):
    return v

def low_keep(v):
    return (low(v), None)

def low_pass(kept, grad):
    return (grad,)

def back_keep(v):
    return (v, None)

def back_low(kept, grad):
    return (low(grad),)
low.defvjp(low_keep, low_pass)
low_back.defvjp(back_keep, back_low)
epsilon = 1e-05
highest = lax.Precision.HIGHEST

def causal_conv(series, terms):
    count = series.shape[0]
    padded = jnp.concatenate([jnp.zeros((CONV - 1, series.shape[1]), series.dtype), series], 0)
    total = terms[CONV] + jnp.zeros_like(series)
    for k in range(CONV):
        total = total + terms[k] * padded[k:k + count]
    return jax.nn.silu(total)

def block_step(decay, state, block):
    values, steps, keys, queries = block
    logs = jnp.cumsum(steps * decay, axis=0)
    order = jnp.arange(values.shape[0])
    lower = (order[:, None] >= order[None, :])[:, :, None]
    gaps = logs[:, None, :] - logs[None, :, :]
    weights = jnp.where(lower, jnp.exp(jnp.where(lower, gaps, 0.0)), 0.0)
    intersection = jnp.dot(queries, keys.T, precision=highest)
    mixing = weights * intersection[:, :, None] * steps[None, :, :]
    inner = jnp.einsum('tsh,shp->thp', mixing, values, precision=highest)
    carried = jnp.exp(logs)[:, :, None] * jnp.einsum('tn,hpn->thp', queries, state, precision=highest)
    tails = jnp.exp(logs[-1][None, :] - logs) * steps
    update = jnp.einsum('sh,shp,sn->hpn', tails, values, keys, precision=highest)
    state = jnp.exp(logs[-1])[:, None, None] * state + update
    return (state, inner + carried)

def state_scan(values, steps, decay, keys, queries, skip):
    count, heads, width = values.shape
    blocks = count // CL
    parts = (values.reshape(blocks, CL, heads, width), steps.reshape(blocks, CL, heads), keys.reshape(blocks, CL, -1), queries.reshape(blocks, CL, -1))
    start = jnp.zeros((heads, width, keys.shape[1]), values.dtype)
    stepper = jax.checkpoint(partial_step(decay))
    final, outputs = lax.scan(stepper, start, parts)
    return outputs.reshape(count, heads, width) + skip[None, :, None] * values

def partial_step(decay):

    def stepper(state, block):
        return block_step(decay, state, block)
    return stepper

def mixer(gates, inputs, keys_raw, step_raw, side_terms, channel_terms, head_terms):
    count = inputs.shape[0]
    heads = head_terms.shape[1]
    state_size = side_terms.shape[1] // 2
    values = causal_conv(inputs, channel_terms[:CONV + 1]).reshape(count, heads, -1)
    both_keys = causal_conv(keys_raw, side_terms)
    steps = jax.nn.softplus(step_raw + head_terms[0])
    decay = -jnp.exp(head_terms[1])
    scanned = state_scan(values, steps, decay, both_keys[:, :state_size], both_keys[:, state_size:], head_terms[2])
    return scanned.reshape(count, -1) * jax.nn.silu(gates)

def layer(seq, valid, main_weight, side_weight, output_weight, norm_gain, side_terms, channel_terms, head_terms):
    count = seq.shape[0]
    scale = lax.rsqrt(lax.optimization_barrier(jnp.mean(seq * seq, axis=-1, keepdims=True)) + epsilon)
    normed = low(seq * scale * norm_gain)
    both = low_back(jnp.dot(normed, main_weight.reshape(D, 2 * INNER), precision=highest)).reshape(count, 2, INNER)
    small = low_back(jnp.dot(normed, side_weight, precision=highest))
    mixed = mixer(both[:, 0], both[:, 1], small[:, :2 * STATE], small[:, 2 * STATE:], side_terms, channel_terms, head_terms)
    rnorm = lax.rsqrt(lax.optimization_barrier(jnp.mean(mixed * mixed, axis=-1, keepdims=True)) + epsilon)
    gated = low(mixed * rnorm * channel_terms[CONV + 1])
    branch = low_back(jnp.dot(gated, output_weight, precision=highest))
    return seq + valid[:, None] * branch

def reference(tokens, seq_len, norm_gain, main_weight, side_weight, side_terms, channel_terms, head_terms, output_weight, cotangent):
    count = STRETCHES * CL
    params = (main_weight.astype(jnp.float32), side_weight.astype(jnp.float32), output_weight.astype(jnp.float32), norm_gain, side_terms, channel_terms, head_terms)

    def one(totals, block):
        seq, length, grad_out = block
        seq_float = seq.reshape(count, D).astype(jnp.float32)
        valid = (jnp.arange(count) < length).astype(jnp.float32)

        def forward(inputs, weights):
            return layer(inputs, valid, *weights)
        result, pull = jax.vjp(forward, seq_float, params)
        grad_seq, grad_params = pull(grad_out.reshape(count, D).astype(jnp.float32))
        totals = jax.tree.map(jnp.add, totals, grad_params)
        return (totals, (result.astype(jnp.bfloat16).reshape(STRETCHES, CL, D), grad_seq.reshape(STRETCHES, CL, D)))
    zeros = jax.tree.map(jnp.zeros_like, params)
    totals, (outputs, grads) = lax.scan(one, zeros, (tokens, seq_len, cotangent))
    main_grad, side_grad, output_grad, gain_grad, side_terms_grad, channel_grad, head_grad = totals
    return (outputs, grads, gain_grad, main_grad, side_grad, side_terms_grad, channel_grad, head_grad, output_grad)
```

```python
import functools

import jax
import jax.numpy as jnp
from jax import lax
from jax.experimental import pallas as pl
from jax.experimental.pallas import tpu as pltpu
from jax.sharding import PartitionSpec as P

f32, bf16 = jnp.float32, jnp.bfloat16
CONV, D, INNER = 4, 1536, 3072
L, N, PW, IN, HD = 256, 128, 64, 384, 6
BLOCKS, GROUP, PIECE, DP = 8, 8, 32, 16
COLS = 2 * IN + 3 * N
MIX = IN + 2 * N
MESH = pl.DeviceIdType.MESH
VMEM_BYTES = 60 * 2**20
epsilon = 1e-05
NEG = -1e30

def mm(a, b):
    return lax.dot_general(a, b, (((1,), (0,)), ((), ())), preferred_element_type=f32)
def mm_nt(a, b):
    return lax.dot_general(a, b, (((1,), (1,)), ((), ())), preferred_element_type=f32)
def mm_tn(a, b):
    return lax.dot_general(a, b, (((0,), (0,)), ((), ())), preferred_element_type=f32)

def thirds(x):
    hi = x.astype(bf16)
    rest = x - hi.astype(f32)
    mid = rest.astype(bf16)
    return hi, mid, (rest - mid.astype(f32)).astype(bf16)

def exact_left(mask, x):
    a, b, c = thirds(x)
    return mm(mask, a) + mm(mask, b) + mm(mask, c)

def exact_right(x, mask):
    a, b, c = thirds(x)
    return mm(a, mask) + mm(b, mask) + mm(c, mask)

def sigmoid(x):
    return 1.0 / (1.0 + jnp.exp(-x))

def softplus(x):
    return jnp.maximum(x, 0.0) + jnp.log1p(jnp.exp(-jnp.abs(x)))

def tri(lower):
    r = lax.broadcasted_iota(jnp.int32, (L, L), 0)
    c = lax.broadcasted_iota(jnp.int32, (L, L), 1)
    return jnp.where((r >= c) if lower else (r <= c), 1.0, 0.0).astype(bf16)

def spread(cols, low):
    out = []
    for j in range(3):
        a = jnp.broadcast_to(cols[:, 2 * j : 2 * j + 1], (cols.shape[0], 128))
        b = jnp.broadcast_to(cols[:, 2 * j + 1 : 2 * j + 2], (cols.shape[0], 128))
        out.append(jnp.where(low, a, b))
    return jnp.concatenate(out, 1)

def conv_pre(window, taps):
    total = taps[4:5]
    for k in range(4):
        total = total + taps[k : k + 1] * window[5 + k : 5 + k + L]
    return total

def low_lanes(rows):
    return lax.broadcasted_iota(jnp.int32, (rows, 128), 1) < 64

def head_quantities(dt_raw, heads):
    pre = dt_raw + heads[0:1]
    dt = softplus(pre)
    logs = exact_left(tri(True), dt * heads[1:2])
    return pre, dt, logs

def half_mask(t):
    rows = 128
    r = lax.broadcasted_iota(jnp.int32, (rows, 128 * (t + 1)), 0) + 128 * t
    c = lax.broadcasted_iota(jnp.int32, (rows, 128 * (t + 1)), 1)
    return r >= c

def weights_of(logs, logs_t, h, t):
    w = 128 * (t + 1)
    col = jnp.broadcast_to(logs[128 * t : 128 * (t + 1), h : h + 1], (128, 128))
    if t:
        col = jnp.concatenate([col, col], 1)
    gap = col - logs_t[h : h + 1, :w]
    return jnp.exp(jnp.where(half_mask(t), gap, NEG))

def fwd_block(window, gates, dt_raw, taps, heads, skip, state):
    low = low_lanes(L)
    total = conv_pre(window, taps)
    act = total * sigmoid(total)
    x, b, c = act[:, :IN], act[:, IN : IN + N].astype(bf16), act[:, IN + N :].astype(bf16)
    pre, dt, logs = head_quantities(dt_raw, heads)
    logs_t = logs.T
    dt_l, logs_l = spread(dt, low), spread(logs, low)
    xd = (dt_l * x).astype(bf16)
    g = mm_nt(c, b)
    half_low = low_lanes(128)
    rows = [[], []]
    zero = jnp.zeros((), bf16)
    for j in range(3):
        pair = xd[:, 128 * j : 128 * (j + 1)]
        own = (jnp.where(low, pair, zero), jnp.where(low, zero, pair))
        for t in range(2):
            w = 128 * (t + 1)
            total_y = 0.0
            for e in range(2):
                m = weights_of(logs, logs_t, 2 * j + e, t) * g[128 * t : 128 * (t + 1), :w]
                total_y = total_y + mm(m.astype(bf16), own[e][:w])
            rows[t].append(total_y)
    intra = jnp.concatenate([jnp.concatenate(r, 1) for r in rows], 0)
    scan = intra + jnp.exp(logs_l) * mm(c, state.astype(bf16))
    last = logs_l[L - 1 : L]
    tails = jnp.exp(last - logs_l)
    state = jnp.exp(last) * state + mm_tn(b, (tails * xd.astype(f32)).astype(bf16))
    mixed = (scan + skip * x) * (gates * sigmoid(gates))
    return scan, mixed, state

def bwd_block(window, gates, dt_raw, taps, heads, skip, gain, state, state_next, scan, rnorm, products, g_gated, d_state, after):
    low = low_lanes(L)
    total = conv_pre(window, taps)
    sig = sigmoid(total)
    act = total * sig
    d_act = sig + act * (1.0 - sig)
    x, b, c = act[:, :IN], act[:, IN : IN + N].astype(bf16), act[:, IN + N :].astype(bf16)
    pre, dt, logs = head_quantities(dt_raw, heads)
    logs_t = logs.T
    dt_l, logs_l = spread(dt, low), spread(logs, low)
    xd = (dt_l * x).astype(bf16)
    xdf = xd.astype(f32)
    gsig = sigmoid(gates)
    gate = gates * gsig
    y = scan + skip * x
    mixed = y * gate
    g_mixed = rnorm * (g_gated * gain) - mixed * (rnorm * rnorm * rnorm * products * (1.0 / 3072.0))
    gain_sum = jnp.sum(g_gated * mixed * rnorm, axis=0, keepdims=True)
    dy = g_mixed * gate
    d_gates = g_mixed * y * (gsig + gate * (1.0 - gsig))
    skip_sum = jnp.sum(dy * x, axis=0, keepdims=True)
    dyb = dy.astype(bf16)
    g = mm_nt(c, b)
    zero = jnp.zeros((), bf16)
    dg = [0.0, 0.0]
    parts = []
    for j in range(3):
        pair_x = xd[:, 128 * j : 128 * (j + 1)]
        pair_y = dyb[:, 128 * j : 128 * (j + 1)]
        own = (jnp.where(low, pair_y, zero), jnp.where(low, zero, pair_y))
        upper, lower = 0.0, 0.0
        for e in range(2):
            for t in range(2):
                w = 128 * (t + 1)
                wt = weights_of(logs, logs_t, 2 * j + e, t)
                mine = own[e][128 * t : 128 * (t + 1)]
                dm = mm_nt(mine, pair_x[:w])
                dg[t] = dg[t] + dm * wt
                m = (wt * g[128 * t : 128 * (t + 1), :w]).astype(bf16)
                back = mm_tn(m, mine)
                upper = upper + back[:128]
                if t:
                    lower = lower + back[128:]
        parts.append(jnp.concatenate([upper, lower], 0))
    d_intra = jnp.concatenate(parts, 1)
    e_l = jnp.exp(logs_l)
    last = logs_l[L - 1 : L]
    tails = jnp.exp(last - logs_l)
    sb = state.astype(bf16)
    dsb = d_state.astype(bf16)
    edy = (e_l * dy).astype(bf16)
    txd = (tails * xdf).astype(bf16)
    v = mm(b, dsb)
    dxd = d_intra + tails * v
    dg0, dg1 = dg[0].astype(bf16), dg[1].astype(bf16)
    dc = mm_nt(edy, sb) + jnp.concatenate([mm(dg0, b[:128]), mm(dg1, b)], 0)
    first = mm_tn(dg0, c[:128])
    second = mm_tn(dg1, c[128:])
    db = mm_nt(txd, dsb) + jnp.concatenate([first + second[:128], second[128:]], 0)
    z = dyb.astype(f32) * scan - xdf * d_intra - txd.astype(f32) * v
    boundary = jnp.sum(state_next * dsb.astype(f32), axis=0, keepdims=True)
    row = lax.broadcasted_iota(jnp.int32, (L, IN), 0)
    z = jnp.where(row == L - 1, z + boundary, z)
    r = lax.broadcasted_iota(jnp.int32, (IN, 128), 0)
    cc = lax.broadcasted_iota(jnp.int32, (IN, 128), 1)
    fold = jnp.where((r // PW) == cc, 1.0, 0.0).astype(bf16)
    dl = exact_right(z, fold)
    g_adt = exact_left(tri(False), dl)
    direct = exact_right(x * dxd, fold)
    d_pre = (direct + heads[1:2] * g_adt) * sigmoid(pre)
    decay_sum = jnp.sum(dt * g_adt, axis=0, keepdims=True)
    bias_sum = jnp.sum(d_pre, axis=0, keepdims=True)
    d_state = jnp.exp(last) * d_state + mm_tn(c, edy)
    dx = dt_l * dxd + skip * dy
    g_pre = jnp.concatenate([dx, db, dc], 1) * d_act
    longer = jnp.concatenate([g_pre, after], 0)
    d_raw = 0.0
    tap_sums = []
    for k in range(4):
        d_raw = d_raw + taps[k : k + 1] * longer[3 - k : 3 - k + L]
        tap_sums.append(jnp.sum(g_pre * window[5 + k : 5 + k + L], axis=0, keepdims=True))
    tap_sums.append(jnp.sum(g_pre, axis=0, keepdims=True))
    g_all = jnp.concatenate([d_gates.astype(bf16), d_raw.astype(bf16), d_pre.astype(bf16)], 1)
    return g_all, d_state, g_pre[:8], (jnp.concatenate(tap_sums, 0), gain_sum, skip_sum, decay_sum, bias_sum)


class Place:
    def __init__(self):
        self.dp, self.mp = lax.axis_index("dp"), lax.axis_index("mp")
        self.hi, self.x = self.mp // 4, self.mp % 4
        self.ylo, self.z, self.core = self.dp // 8, (self.dp // 2) % 4, self.dp % 2
        self.right = (self.dp, self.hi * 4 + (self.x + 1) % 4)
        self.left = (self.dp, self.hi * 4 + (self.x + 3) % 4)
        self.across = (self.dp, (1 - self.hi) * 4 + self.x)
        self.mate = (self.dp + 1 - 2 * self.core, self.mp)
        self.beside = (self.at(1 - self.ylo, self.z, self.core), self.mp)
        self.along = [(self.at(self.ylo, (self.z + k) % 4, self.core), self.mp) for k in (1, 2, 3)]
        self.group = [(self.dp, (self.mp + k) % GROUP) for k in range(1, GROUP)]
        self.copies = [((self.dp + k) % DP, self.mp) for k in range(1, DP)]

    def at(self, ylo, z, core):
        return ylo * 8 + z * 2 + core


def meet(peers):
    barrier = pltpu.get_barrier_semaphore()
    for peer in peers:
        pl.semaphore_signal(barrier, inc=1, device_id=peer, device_id_type=MESH)
    pl.semaphore_wait(barrier, len(peers))


class Sender:
    def __init__(self, send_sem, recv_sem):
        self.send_sem, self.recv_sem, self.count, self.started = send_sem, recv_sem, 0, []

    def __call__(self, source, target, peer):
        k = self.count
        self.count += 1
        copy = pltpu.make_async_remote_copy(
            src_ref=source,
            dst_ref=target,
            send_sem=self.send_sem.at[k],
            recv_sem=self.recv_sem.at[k],
            device_id=peer,
            device_id_type=MESH,
        )
        copy.start()
        self.started.append(copy)
        return copy

    def drain(self):
        for copy in self.started:
            copy.wait_send()


def gather_steps(send, place, buf):
    hi, x, me = place.hi, place.x, place.mp
    lx, rx, ox = hi * 4 + (x + 3) % 4, hi * 4 + (x + 1) % 4, hi * 4 + (x + 2) % 4
    flip = (1 - hi) * 4
    lxy, rxy, ym = flip + (x + 3) % 4, flip + (x + 1) % 4, flip + x
    right, left, across = place.right, place.left, place.across

    def go(slot, g, h, to):
        part = buf.at[pl.ds(4 * g + 2 * h, 2), slot]
        return send(part, part, to)

    c = [go(me, 1, 0, across), go(me, 1, 1, across)]
    a = [go(me, 0, 0, right), go(me, 0, 1, left), go(me, 0, 1, right), go(me, 0, 0, left)]
    b = [go(me, 1, 0, right), go(me, 1, 1, left), go(me, 1, 1, right), go(me, 1, 0, left)]
    y = [go(me, 0, 0, across), go(me, 0, 1, across)]
    yield
    a[0].wait_recv()
    f = [go(lx, 0, 0, right)]
    y.append(go(lx, 0, 0, across))
    a[1].wait_recv()
    f.append(go(rx, 0, 1, left))
    y.append(go(rx, 0, 1, across))
    yield
    a[2].wait_recv()
    y.append(go(lx, 0, 1, across))
    a[3].wait_recv()
    y.append(go(rx, 0, 0, across))
    yield
    b[0].wait_recv()
    k = [go(lx, 1, 0, right)]
    b[1].wait_recv()
    k.append(go(rx, 1, 1, left))
    c[0].wait_recv()
    c[1].wait_recv()
    d = [go(ym, 1, 0, right), go(ym, 1, 1, left), go(ym, 1, 1, right), go(ym, 1, 0, left)]
    yield
    f[0].wait_recv()
    y.append(go(ox, 0, 0, across))
    f[1].wait_recv()
    y.append(go(ox, 0, 1, across))
    yield
    d[0].wait_recv()
    e = [go(lxy, 1, 0, right)]
    d[1].wait_recv()
    e.append(go(rxy, 1, 1, left))
    yield
    for copy in [b[2], b[3], d[2], d[3]] + k + e + y:
        copy.wait_recv()


def weight_steps(send, place, buf):
    own, other = place.dp, place.at(1 - place.ylo, place.z, place.core)
    one = send(buf.at[own], buf.at[own], place.beside)
    mates = [send(buf.at[own], buf.at[own], place.mate)]
    near = [send(buf.at[own], buf.at[own], peer) for peer in place.along]
    yield
    one.wait_recv()
    mates.append(send(buf.at[other], buf.at[other], place.mate))
    far = [send(buf.at[other], buf.at[other], peer) for peer in place.along]
    yield
    for k in range(3):
        near[k].wait_recv()
        slot = place.at(place.ylo, (place.z + 3 - k) % 4, place.core)
        mates.append(send(buf.at[slot], buf.at[slot], place.mate))
    yield
    for k in range(3):
        far[k].wait_recv()
        slot = place.at(1 - place.ylo, (place.z + 3 - k) % 4, place.core)
        mates.append(send(buf.at[slot], buf.at[slot], place.mate))
    yield
    for copy in mates:
        copy.wait_recv()


def add_into(buf, first, slot, other, where, count):
    def body(i, carry):
        total = buf[first + i, slot].astype(f32) + other[where(i)].astype(f32)
        buf[first + i, slot] = total.astype(bf16)
        return carry

    lax.fori_loop(0, count, body, 0)


def scatter_steps(send, place, buf, y_in, x_in, xx_in, t_out, t_in, total):
    hi, x = place.hi, place.x
    right, left, across = place.right, place.left, place.across
    order = [(x + 2) % 4, (x + 1) % 4, (x + 3) % 4, x]
    mine, theirs = hi * 4, (1 - hi) * 4

    def first_hop(k, base, side):
        slot = side + order[0]
        return [
            send(buf.at[pl.ds(base, 2), slot], x_in.at[k, 0], right),
            send(buf.at[pl.ds(base + 2, 2), slot], x_in.at[k, 1], left),
        ]

    def second_hop(k, base, side, hops):
        hops[0].wait_recv()
        add_into(buf, base, side + order[1], x_in, lambda i: (k, 0, i), 2)
        one = send(buf.at[pl.ds(base, 4), side + order[1]], xx_in.at[k, 0], right)
        hops[1].wait_recv()
        add_into(buf, base + 2, side + order[2], x_in, lambda i: (k, 1, i), 2)
        return [one, send(buf.at[pl.ds(base, 4), side + order[2]], xx_in.at[k, 1], left)]

    def three(k, base, side, i):
        return (
            buf[base + i, side + x].astype(f32)
            + xx_in[k, 0, i].astype(f32)
            + xx_in[k, 1, i].astype(f32)
        )

    ahead = []
    for k in range(4):
        ahead.append(send(buf.at[pl.ds(0, 4), theirs + order[k]], y_in.at[k], across))
    hop_t = first_hop(1, 4, theirs)
    hop_m = first_hop(2, 4, mine)
    yield
    two_t = second_hop(1, 4, theirs, hop_t)
    yield
    ahead[0].wait_recv()
    add_into(buf, 0, mine + order[0], y_in, lambda i: (0, i), 4)
    hop_a = first_hop(0, 0, mine)
    two_m = second_hop(2, 4, mine, hop_m)
    yield
    for copy in two_t:
        copy.wait_recv()

    def give(i, carry):
        t_out[i] = three(1, 4, theirs, i).astype(bf16)
        return carry

    lax.fori_loop(0, 4, give, 0)
    last = send(t_out, t_in, across)
    yield
    for k in range(1, 4):
        ahead[k].wait_recv()
        add_into(buf, 0, mine + order[k], y_in, lambda i, k=k: (k, i), 4)
    two_a = second_hop(0, 0, mine, hop_a)
    yield
    for copy in two_m + [last]:
        copy.wait_recv()

    def keep_b(i, carry):
        total[4 + i] = three(2, 4, mine, i) + t_in[i].astype(f32)
        return carry

    lax.fori_loop(0, 4, keep_b, 0)
    yield
    for copy in two_a:
        copy.wait_recv()

    def keep_a(i, carry):
        total[i] = three(0, 0, mine, i)
        return carry

    lax.fori_loop(0, 4, keep_a, 0)


SCATTER_SCRATCH = [
    pltpu.VMEM((4, 4, PIECE, D), bf16),
    pltpu.VMEM((3, 2, 2, PIECE, D), bf16),
    pltpu.VMEM((3, 2, 4, PIECE, D), bf16),
    pltpu.VMEM((4, PIECE, D), bf16),
    pltpu.VMEM((4, PIECE, D), bf16),
]


def finish(steps):
    for _ in steps:
        pass


def rows(block, count=L):
    return pl.ds(pl.multiple_of(block * count, count), count)


def pick(columns, block):
    lane = lax.broadcasted_iota(jnp.int32, columns.shape, 1)
    return jnp.sum(jnp.where(lane == block, columns, 0.0), axis=1, keepdims=True)


def gather_kernel(normed, weights, grad, whole, full, back, send_sem, recv_sem, local_sem):
    place = Place()
    own = [
        pltpu.make_async_copy(normed, whole.at[:, place.mp], local_sem.at[0]),
        pltpu.make_async_copy(weights, full.at[place.dp], local_sem.at[1]),
        pltpu.make_async_copy(grad, back.at[:, place.mp], local_sem.at[2]),
    ]
    for copy in own:
        copy.start()
    meet([place.right, place.left, place.across, place.mate, place.beside] + place.along)
    for copy in own:
        copy.wait()
    send = Sender(send_sem, recv_sem)
    plans = [gather_steps(send, place, whole), weight_steps(send, place, full)]
    for _ in range(2):
        for plan in plans:
            next(plan)
    for plan in plans:
        finish(plan)
    finish(gather_steps(send, place, back))
    send.drain()


def forward_kernel(
    whole, weights, back, taps, heads, skip, gain,
    raw, gates, steps, scan, mixed, states, g_gated, sums,
    squares, state, inbox, send_sem, recv_sem,
):
    place = Place()
    meet(place.group)
    raw[pl.ds(0, 8)] = jnp.zeros((8, MIX), f32)
    state[...] = jnp.zeros((N, IN), f32)
    squares[...] = jnp.zeros((L, 128), f32)
    lane = lax.broadcasted_iota(jnp.int32, (L, 128), 1)

    def body(i, carry):
        at = rows(i)
        both = mm(whole[at], weights[:, :COLS])
        gates[at] = both[:, :IN]
        steps[at] = both[:, IN + MIX :]
        raw[pl.ds(pl.multiple_of(i * L + 8, 8), L)] = both[:, IN : IN + MIX]
        states[i] = state[...]
        window = raw[pl.ds(pl.multiple_of(i * L, 8), L + 8)]
        inner, out, after = fwd_block(
            window, gates[at], steps[at], taps[...], heads[...], skip[...], state[...]
        )
        scan[at] = inner
        mixed[at] = out
        state[...] = after
        back_out = mm(back[at], weights[:, COLS:])
        g_gated[at] = back_out
        square = jnp.sum(out * out, axis=1, keepdims=True)
        product = jnp.sum(back_out * gain[...] * out, axis=1, keepdims=True)
        kept = squares[...]
        squares[...] = jnp.where(lane == i, square, jnp.where(lane == i + 8, product, kept))
        return carry

    lax.fori_loop(0, BLOCKS, body, 0)
    states[BLOCKS] = state[...]
    inbox[place.mp] = squares[...].T[:16]
    send = Sender(send_sem, recv_sem)
    copies = [send(inbox.at[place.mp], inbox.at[place.mp], peer) for peer in place.group]
    for copy in copies:
        copy.wait_recv()
    send.drain()
    total = inbox[0]
    for k in range(1, GROUP):
        total = total + inbox[k]
    top = lax.rsqrt(total[:8] * (1.0 / INNER) + epsilon)
    sums[...] = jnp.concatenate([top, total[8:], jnp.zeros((112, L), f32)], 0).T


def backward_kernel(
    raw, gates, steps, scan, mixed, states, g_gated, sums, weights, taps, heads, skip, gain,
    g_all, gated, branch, totals,
    parts, y_in, x_in, xx_in, t_out, t_in, d_state, after, send_sem, recv_sem,
):
    place = Place()
    meet([place.right, place.left, place.across])

    def spread_out(i, carry):
        at = rows(i)
        scale = pick(sums[...], i)
        rounded = (mixed[at] * scale * gain[...]).astype(bf16)
        gated[at] = rounded
        parts[i] = mm_nt(rounded, weights[:, COLS:]).astype(bf16).reshape(GROUP, PIECE, D)
        return carry

    lax.fori_loop(0, BLOCKS, spread_out, 0)
    send = Sender(send_sem, recv_sem)
    plan = scatter_steps(send, place, parts, y_in, x_in, xx_in, t_out, t_in, branch)
    next(plan)
    d_state[...] = jnp.zeros((N, IN), f32)
    after[...] = jnp.zeros((8, MIX), f32)
    totals[...] = jnp.zeros((16, MIX), f32)

    def body(j, carry):
        i = BLOCKS - 1 - j
        at = rows(i)
        window = raw[pl.ds(pl.multiple_of(i * L, 8), L + 8)]
        g, ds, top, found = bwd_block(
            window, gates[at], steps[at], taps[...], heads[...], skip[...], gain[...],
            states[i], states[i + 1], scan[at], pick(sums[...], i), pick(sums[...], i + 8),
            g_gated[at], d_state[...], after[...],
        )
        g_all[at] = g
        d_state[...] = ds
        after[...] = top
        tap_sums, gain_sum, skip_sum, decay_sum, bias_sum = found
        blank = jnp.zeros((1, MIX - IN), f32)
        fill = jnp.zeros((1, MIX - 2 * N), f32)
        totals[...] += jnp.concatenate(
            [
                tap_sums,
                jnp.concatenate([gain_sum, blank], 1),
                jnp.concatenate([skip_sum, blank], 1),
                jnp.concatenate([decay_sum, bias_sum, fill], 1),
                jnp.zeros((8, MIX), f32),
            ],
            0,
        )
        return carry

    run_between(body, plan)
    finish(plan)
    send.drain()


def run_between(body, plan):
    lax.fori_loop(0, BLOCKS, body, 0)


def last_kernel(
    whole, back, gated, g_all, weights, tokens, scale, grad_out, norm_gain, totals,
    token_grad, gain_grad, mine_grad, side_grad, shared_sums, copy_sums,
    parts, y_in, x_in, xx_in, t_out, t_in, summed, grads, core_in, z_in, y_out, w_in,
    inbox, side_box, sums_box, gain_box, gain_all, send_sem, recv_sem,
):
    place = Place()
    meet(place.group + place.copies)
    send = Sender(send_sem, recv_sem)

    sums_box[place.dp] = totals[...]
    early = [send(sums_box.at[place.dp], sums_box.at[place.dp], peer) for peer in place.copies]

    def spread_out(i, carry):
        at = rows(i)
        parts[i] = mm_nt(g_all[at], weights[:, :COLS]).astype(bf16).reshape(GROUP, PIECE, D)
        return carry

    lax.fori_loop(0, BLOCKS, spread_out, 0)
    plan = scatter_steps(send, place, parts, y_in, x_in, xx_in, t_out, t_in, summed)
    next(plan)

    def product(i, carry):
        lanes = pl.ds(pl.multiple_of(i * 384, 128), 384)
        left = mm_tn(whole[:, lanes], g_all[...]).astype(bf16).reshape(2, 2, 96, COLS)
        right = mm_tn(back[:, lanes], gated[...]).astype(bf16).reshape(2, 2, 96, IN)
        for k in range(2):
            grads[2 * i + k, :, :, :COLS] = left[k]
            grads[2 * i + k, :, :, COLS:] = right[k]
        return carry

    lax.fori_loop(0, 4, product, 0)
    swap = send(grads.at[:, 1 - place.core], core_in, place.mate)
    next(plan)
    swap.wait_recv()

    def fold(i, carry):
        total = grads[i, place.core].astype(f32) + core_in[i].astype(f32)
        grads[i, place.core] = total.astype(bf16)
        return carry

    lax.fori_loop(0, 8, fold, 0)
    hops = []
    for k in range(3):
        z = (place.z + k + 1) % 4
        for y in range(2):
            hops.append(send(grads.at[4 * y + z, place.core], z_in.at[k, y], place.along[k]))
    next(plan)
    next(plan)
    for hop in hops:
        hop.wait_recv()

    def joined(y):
        total = grads[4 * y + place.z, place.core].astype(f32)
        for k in range(3):
            total = total + z_in[k, y].astype(f32)
        return total

    y_out[...] = joined(1 - place.ylo).astype(bf16)
    cross = send(y_out, w_in, place.beside)
    next(plan)
    cross.wait_recv()
    mine = joined(place.ylo) + w_in[...].astype(f32)
    mine_grad[...] = mine
    side_box[place.mp] = mine[:, 2 * IN : COLS].astype(bf16)
    sides = [send(side_box.at[place.mp], side_box.at[place.mp], peer) for peer in place.group]
    for copy in early:
        copy.wait_recv()
    copied = sums_box[0]
    for k in range(1, DP):
        copied = copied + sums_box[k]
    copy_sums[...] = copied
    inbox[place.mp] = copied[:8, IN:]
    shares = [send(inbox.at[place.mp], inbox.at[place.mp], peer) for peer in place.group]
    finish(plan)

    gain_row = norm_gain[...]
    gain_sum = jnp.zeros((1, D), f32)
    for i in range(BLOCKS):
        x = tokens[i].astype(f32)
        s = scale[i]
        g = summed[i]
        dot = jnp.sum(g * gain_row * x, axis=1, keepdims=True)
        token_grad[i] = grad_out[i].astype(f32) + s * gain_row * g - x * (s * s * s * dot * (1.0 / D))
        gain_sum = gain_sum + jnp.sum(g * x * s, axis=0, keepdims=True)
    gain_box[place.mp] = jnp.concatenate([gain_sum, jnp.zeros((7, D), f32)], 0)
    gains = [send(gain_box.at[place.mp], gain_box.at[place.mp], peer) for peer in place.group]

    for copy in sides + shares:
        copy.wait_recv()
    both, steps = 0.0, 0.0
    lane = lax.broadcasted_iota(jnp.int32, (N, N), 1)
    source = lax.broadcasted_iota(jnp.int32, (N, N), 0)
    shared = inbox[0]
    for k in range(GROUP):
        piece = side_box[k]
        both = both + piece[:, : 2 * N].astype(f32)
        spot = jnp.where((lane == source + HD * k) & (source < HD), 1.0, 0.0).astype(bf16)
        steps = steps + mm(piece[:, 2 * N :], spot)
        if k:
            shared = shared + inbox[k]
    side_grad[...] = jnp.concatenate([both, steps], 1)
    shared_sums[...] = shared
    for copy in gains:
        copy.wait_recv()
    total = gain_box[0]
    for k in range(1, GROUP):
        total = total + gain_box[k]
    gain_all[place.dp] = total
    ends = [send(gain_all.at[place.dp], gain_all.at[place.dp], peer) for peer in place.copies]
    for copy in ends:
        copy.wait_recv()
    total = gain_all[0]
    for k in range(1, DP):
        total = total + gain_all[k]
    gain_grad[...] = total
    send.drain()


def call(kernel, outs, scratch, sems, collective, args, flops, anywhere=False):
    space = pl.ANY if anywhere else pltpu.VMEM
    return pl.pallas_call(
        kernel,
        out_shape=[jax.ShapeDtypeStruct(shape, dtype) for shape, dtype in outs],
        in_specs=[pl.BlockSpec(memory_space=space)] * len(args),
        out_specs=[pl.BlockSpec(memory_space=space)] * len(outs),
        scratch_shapes=list(scratch)
        + [pltpu.SemaphoreType.DMA((sems,)), pltpu.SemaphoreType.DMA((sems,))]
        + ([pltpu.SemaphoreType.DMA((3,))] if anywhere else []),
        compiler_params=pltpu.CompilerParams(
            collective_id=collective, has_side_effects=True, vmem_limit_bytes=VMEM_BYTES
        ),
        cost_estimate=pl.CostEstimate(
            flops=flops,
            bytes_accessed=sum(a.size * a.dtype.itemsize for a in args),
            transcendentals=0,
        ),
        name=kernel.__name__,
    )(*args)


def on_device(
    tokens,
    seq_len,
    norm_gain,
    main_weight,
    side_weight,
    side_terms,
    channel_terms,
    head_terms,
    output_weight,
    cotangent,
):
    place = lax.axis_index("mp")
    count = BLOCKS * L
    seq = tokens[0].astype(f32)
    scale = lax.rsqrt(jnp.mean(seq * seq, axis=-1, keepdims=True) + epsilon)
    normed = (seq * scale * norm_gain).astype(bf16)
    grad_out = cotangent[0].astype(f32)
    positions = (
        jnp.arange(BLOCKS)[:, None] * L + place * PIECE + jnp.arange(PIECE)[None, :]
    )
    valid = (positions < seq_len[0]).astype(f32)[:, :, None]
    grad_branch = (valid * grad_out).astype(bf16)
    own_steps = lax.dynamic_slice_in_dim(side_weight, 2 * N + place * HD, HD, 1)
    own_weights = jnp.concatenate(
        [
            main_weight.reshape(-1, 2 * IN),
            side_weight[:, : 2 * N],
            own_steps,
            jnp.zeros((own_steps.shape[0], N - HD), bf16),
            output_weight.T,
        ],
        1,
    )
    taps = jnp.concatenate([channel_terms[: CONV + 1], side_terms], 1)
    taps = jnp.concatenate([taps, jnp.zeros((3, MIX), f32)], 0)
    gain = channel_terms[CONV + 1 :]
    heads = jnp.zeros((8, N), f32)
    heads = heads.at[0, :HD].set(head_terms[0]).at[1, :HD].set(-jnp.exp(head_terms[1]))
    skip = jnp.repeat(head_terms[2], PW)[None]

    whole, weights, back = call(
        gather_kernel,
        [
            ((BLOCKS, GROUP, PIECE, D), bf16),
            ((DP, D // DP, COLS + IN), bf16),
            ((BLOCKS, GROUP, PIECE, D), bf16),
        ],
        [], 80, 0, [normed, own_weights, grad_branch], 0, True,
    )
    whole, back = whole.reshape(count, D), back.reshape(count, D)
    weights = weights.reshape(D, COLS + IN)
    raw, gates, steps, scan, mixed, states, g_gated, sums = call(
        forward_kernel,
        [
            ((count + 8, MIX), f32),
            ((count, IN), f32),
            ((count, N), f32),
            ((count, IN), f32),
            ((count, IN), f32),
            ((BLOCKS + 1, N, IN), f32),
            ((count, IN), f32),
            ((L, 128), f32),
        ],
        [pltpu.VMEM((L, 128), f32), pltpu.VMEM((N, IN), f32), pltpu.VMEM((GROUP, 16, L), f32)],
        7, 1, [whole, weights, back, taps, heads, skip, gain], 12 * 10**9,
    )
    g_all, gated, branch, totals = call(
        backward_kernel,
        [
            ((count, COLS), bf16),
            ((count, IN), bf16),
            ((BLOCKS, PIECE, D), f32),
            ((16, MIX), f32),
        ],
        [pltpu.VMEM((BLOCKS, GROUP, PIECE, D), bf16)]
        + SCATTER_SCRATCH
        + [pltpu.VMEM((N, IN), f32), pltpu.VMEM((8, MIX), f32)],
        32, 2,
        [raw, gates, steps, scan, mixed, states, g_gated, sums, weights, taps, heads, skip, gain],
        8 * 10**9,
    )
    result = (seq + valid * branch).astype(bf16)
    token_grad, gain_grad, mine_grad, side_grad, shared_sums, copy_sums = call(
        last_kernel,
        [
            ((BLOCKS, PIECE, D), f32),
            ((8, D), f32),
            ((D // DP, COLS + IN), f32),
            ((D // DP, 3 * N), f32),
            ((8, 2 * N), f32),
            ((16, MIX), f32),
        ],
        [pltpu.VMEM((BLOCKS, GROUP, PIECE, D), bf16)]
        + SCATTER_SCRATCH
        + [
            pltpu.VMEM((BLOCKS, PIECE, D), f32),
            pltpu.VMEM((8, 2, D // DP, COLS + IN), bf16),
            pltpu.VMEM((8, D // DP, COLS + IN), bf16),
            pltpu.VMEM((3, 2, D // DP, COLS + IN), bf16),
            pltpu.VMEM((D // DP, COLS + IN), bf16),
            pltpu.VMEM((D // DP, COLS + IN), bf16),
            pltpu.VMEM((GROUP, 8, 2 * N), f32),
            pltpu.VMEM((GROUP, D // DP, 3 * N), bf16),
            pltpu.VMEM((DP, 16, MIX), f32),
            pltpu.VMEM((GROUP, 8, D), f32),
            pltpu.VMEM((DP, 8, D), f32),
        ],
        96, 3,
        [whole, back, gated, g_all, weights, tokens[0], scale, cotangent[0], norm_gain[None], totals],
        15 * 10**9,
    )
    main_grad = mine_grad[:, : 2 * IN].reshape(-1, 2, IN)
    out_grad = mine_grad[:, COLS:].T
    conv_total = shared_sums[: CONV + 1]
    channel_total = copy_sums[: CONV + 2, :IN]
    decay = heads[1, :HD] * copy_sums[CONV + 3, :HD]
    skip_total = copy_sums[CONV + 2, :IN].reshape(HD, PW).sum(1)
    head_total = jnp.stack([copy_sums[CONV + 3, N : N + HD], decay, skip_total])
    return (
        result[None],
        token_grad[None],
        gain_grad[0],
        main_grad,
        side_grad[:, : 2 * N + 48],
        conv_total,
        channel_total,
        head_total,
        out_grad,
    )


def solution(mesh):
    placed = (
        P("dp", None, "mp", None),
        P("dp"),
        P(),
        P("dp", None, "mp"),
        P("dp", None),
        P(),
        P(None, "mp"),
        P(None, "mp"),
        P("mp", "dp"),
        P("dp", None, "mp", None),
    )
    return jax.shard_map(
        on_device,
        mesh=mesh,
        in_specs=placed,
        out_specs=(
            P("dp", None, "mp", None),
            P("dp", None, "mp", None),
            P(),
            P("dp", None, "mp"),
            P("dp", None),
            P(),
            P(None, "mp"),
            P(None, "mp"),
            P("mp", "dp"),
        ),
        check_vma=False,
    )
```

```python
import functools

import jax
import jax.numpy as jnp
from jax import lax
from jax.experimental import pallas as pl
from jax.experimental.pallas import tpu as pltpu
from jax.sharding import PartitionSpec as P

f32, bf16 = jnp.float32, jnp.bfloat16
CONV, D, INNER = 4, 1536, 3072
L, N, PW, IN, HD = 256, 128, 64, 384, 6
BLOCKS, GROUP, PIECE, DP = 8, 8, 32, 16
COLS = 2 * IN + 3 * N
MIX = IN + 2 * N
MESH = pl.DeviceIdType.MESH
VMEM_BYTES = 62 * 2**20
epsilon = 1e-05
NEG = -1e30

def mm(a, b):
    return lax.dot_general(a, b, (((1,), (0,)), ((), ())), preferred_element_type=f32)
def mm_nt(a, b):
    return lax.dot_general(a, b, (((1,), (1,)), ((), ())), preferred_element_type=f32)
def mm_tn(a, b):
    return lax.dot_general(a, b, (((0,), (0,)), ((), ())), preferred_element_type=f32)

def thirds(x):
    hi = x.astype(bf16)
    rest = x - hi.astype(f32)
    mid = rest.astype(bf16)
    return hi, mid, (rest - mid.astype(f32)).astype(bf16)

def exact_left(mask, x):
    a, b, c = thirds(x)
    return mm(mask, a) + mm(mask, b) + mm(mask, c)

def exact_right(x, mask):
    a, b, c = thirds(x)
    return mm(a, mask) + mm(b, mask) + mm(c, mask)

def sigmoid(x):
    return 1.0 / (1.0 + jnp.exp(-x))

def softplus(x):
    return jnp.maximum(x, 0.0) + jnp.log1p(jnp.exp(-jnp.abs(x)))

def tri(lower):
    r = lax.broadcasted_iota(jnp.int32, (L, L), 0)
    c = lax.broadcasted_iota(jnp.int32, (L, L), 1)
    return jnp.where((r >= c) if lower else (r <= c), 1.0, 0.0).astype(bf16)

def spread(cols, low):
    out = []
    for j in range(3):
        a = jnp.broadcast_to(cols[:, 2 * j : 2 * j + 1], (cols.shape[0], 128))
        b = jnp.broadcast_to(cols[:, 2 * j + 1 : 2 * j + 2], (cols.shape[0], 128))
        out.append(jnp.where(low, a, b))
    return jnp.concatenate(out, 1)

def conv_pre(window, taps):
    total = taps[4:5]
    for k in range(4):
        total = total + taps[k : k + 1] * window[5 + k : 5 + k + L]
    return total

def low_lanes(rows):
    return lax.broadcasted_iota(jnp.int32, (rows, 128), 1) < 64

def head_quantities(dt_raw, heads):
    pre = dt_raw + heads[0:1]
    dt = softplus(pre)
    logs = exact_left(tri(True), dt * heads[1:2])
    return pre, dt, logs

def half_mask(t):
    rows = 128
    r = lax.broadcasted_iota(jnp.int32, (rows, 128 * (t + 1)), 0) + 128 * t
    c = lax.broadcasted_iota(jnp.int32, (rows, 128 * (t + 1)), 1)
    return r >= c

def weights_of(logs, logs_t, h, t):
    w = 128 * (t + 1)
    col = jnp.broadcast_to(logs[128 * t : 128 * (t + 1), h : h + 1], (128, 128))
    if t:
        col = jnp.concatenate([col, col], 1)
    gap = col - logs_t[h : h + 1, :w]
    return jnp.exp(jnp.where(half_mask(t), gap, NEG))

def fwd_block(window, gates, dt_raw, taps, heads, skip, state):
    low = low_lanes(L)
    total = conv_pre(window, taps)
    act = total * sigmoid(total)
    x, b, c = act[:, :IN], act[:, IN : IN + N].astype(bf16), act[:, IN + N :].astype(bf16)
    pre, dt, logs = head_quantities(dt_raw, heads)
    logs_t = logs.T
    dt_l, logs_l = spread(dt, low), spread(logs, low)
    xd = (dt_l * x).astype(bf16)
    g = mm_nt(c, b)
    half_low = low_lanes(128)
    rows = [[], []]
    zero = jnp.zeros((), bf16)
    for j in range(3):
        pair = xd[:, 128 * j : 128 * (j + 1)]
        own = (jnp.where(low, pair, zero), jnp.where(low, zero, pair))
        for t in range(2):
            w = 128 * (t + 1)
            total_y = 0.0
            for e in range(2):
                m = weights_of(logs, logs_t, 2 * j + e, t) * g[128 * t : 128 * (t + 1), :w]
                total_y = total_y + mm(m.astype(bf16), own[e][:w])
            rows[t].append(total_y)
    intra = jnp.concatenate([jnp.concatenate(r, 1) for r in rows], 0)
    scan = intra + jnp.exp(logs_l) * mm(c, state.astype(bf16))
    last = logs_l[L - 1 : L]
    tails = jnp.exp(last - logs_l)
    state = jnp.exp(last) * state + mm_tn(b, (tails * xd.astype(f32)).astype(bf16))
    mixed = (scan + skip * x) * (gates * sigmoid(gates))
    return scan, mixed, state

def bwd_block(window, gates, dt_raw, taps, heads, skip, gain, state, scan, rnorm, products, g_gated, d_state, after):
    low = low_lanes(L)
    total = conv_pre(window, taps)
    sig = sigmoid(total)
    act = total * sig
    d_act = sig + act * (1.0 - sig)
    x, b, c = act[:, :IN], act[:, IN : IN + N].astype(bf16), act[:, IN + N :].astype(bf16)
    pre, dt, logs = head_quantities(dt_raw, heads)
    logs_t = logs.T
    dt_l, logs_l = spread(dt, low), spread(logs, low)
    xd = (dt_l * x).astype(bf16)
    xdf = xd.astype(f32)
    gsig = sigmoid(gates)
    gate = gates * gsig
    y = scan + skip * x
    mixed = y * gate
    g_mixed = rnorm * (g_gated * gain) - mixed * (rnorm * rnorm * rnorm * products * (1.0 / 3072.0))
    gain_sum = jnp.sum(g_gated * mixed * rnorm, axis=0, keepdims=True)
    dy = g_mixed * gate
    d_gates = g_mixed * y * (gsig + gate * (1.0 - gsig))
    skip_sum = jnp.sum(dy * x, axis=0, keepdims=True)
    dyb = dy.astype(bf16)
    g = mm_nt(c, b)
    zero = jnp.zeros((), bf16)
    dg = [0.0, 0.0]
    parts = []
    for j in range(3):
        pair_x = xd[:, 128 * j : 128 * (j + 1)]
        pair_y = dyb[:, 128 * j : 128 * (j + 1)]
        own = (jnp.where(low, pair_y, zero), jnp.where(low, zero, pair_y))
        upper, lower = 0.0, 0.0
        for e in range(2):
            for t in range(2):
                w = 128 * (t + 1)
                wt = weights_of(logs, logs_t, 2 * j + e, t)
                mine = own[e][128 * t : 128 * (t + 1)]
                dm = mm_nt(mine, pair_x[:w])
                dg[t] = dg[t] + dm * wt
                m = (wt * g[128 * t : 128 * (t + 1), :w]).astype(bf16)
                back = mm_tn(m, mine)
                upper = upper + back[:128]
                if t:
                    lower = lower + back[128:]
        parts.append(jnp.concatenate([upper, lower], 0))
    d_intra = jnp.concatenate(parts, 1)
    e_l = jnp.exp(logs_l)
    last = logs_l[L - 1 : L]
    tails = jnp.exp(last - logs_l)
    sb = state.astype(bf16)
    dsb = d_state.astype(bf16)
    edy = (e_l * dy).astype(bf16)
    txd = (tails * xdf).astype(bf16)
    v = mm(b, dsb)
    dxd = d_intra + tails * v
    dg0, dg1 = dg[0].astype(bf16), dg[1].astype(bf16)
    dc = mm_nt(edy, sb) + jnp.concatenate([mm(dg0, b[:128]), mm(dg1, b)], 0)
    first = mm_tn(dg0, c[:128])
    second = mm_tn(dg1, c[128:])
    db = mm_nt(txd, dsb) + jnp.concatenate([first + second[:128], second[128:]], 0)
    z = dyb.astype(f32) * scan - xdf * d_intra - txd.astype(f32) * v
    kept = jnp.sum(state * dsb.astype(f32), axis=0, keepdims=True)
    boundary = jnp.exp(last) * kept + jnp.sum(txd.astype(f32) * v, axis=0, keepdims=True)
    row = lax.broadcasted_iota(jnp.int32, (L, IN), 0)
    z = jnp.where(row == L - 1, z + boundary, z)
    r = lax.broadcasted_iota(jnp.int32, (IN, 128), 0)
    cc = lax.broadcasted_iota(jnp.int32, (IN, 128), 1)
    fold = jnp.where((r // PW) == cc, 1.0, 0.0).astype(bf16)
    dl = exact_right(z, fold)
    g_adt = exact_left(tri(False), dl)
    direct = exact_right(x * dxd, fold)
    d_pre = (direct + heads[1:2] * g_adt) * sigmoid(pre)
    decay_sum = jnp.sum(dt * g_adt, axis=0, keepdims=True)
    bias_sum = jnp.sum(d_pre, axis=0, keepdims=True)
    d_state = jnp.exp(last) * d_state + mm_tn(c, edy)
    dx = dt_l * dxd + skip * dy
    g_pre = jnp.concatenate([dx, db, dc], 1) * d_act
    longer = jnp.concatenate([g_pre, after], 0)
    d_raw = 0.0
    tap_sums = []
    for k in range(4):
        d_raw = d_raw + taps[k : k + 1] * longer[3 - k : 3 - k + L]
        tap_sums.append(jnp.sum(g_pre * window[5 + k : 5 + k + L], axis=0, keepdims=True))
    tap_sums.append(jnp.sum(g_pre, axis=0, keepdims=True))
    g_all = jnp.concatenate([d_gates.astype(bf16), d_raw.astype(bf16), d_pre.astype(bf16)], 1)
    return g_all, d_state, g_pre[:8], (jnp.concatenate(tap_sums, 0), gain_sum, skip_sum, decay_sum, bias_sum)


class Place:
    def __init__(self):
        dp, mp = lax.axis_index("dp"), lax.axis_index("mp")
        self.dp, self.mp = dp, mp
        self.hi, self.x = mp // 4, mp % 4
        self.lo = 1 - self.hi
        self.ylo, self.z, self.core = dp // 8, (dp // 2) % 4, dp % 2
        self.other_core = 1 - self.core
        self.mine, self.theirs = self.hi * 4, self.lo * 4
        self.xs = [(self.x + k) % 4 for k in range(4)]
        self.row = [self.mine + x for x in self.xs]
        self.far_row = [self.theirs + x for x in self.xs]
        self.right, self.left = (dp, self.row[1]), (dp, self.row[3])
        self.across = (dp, self.far_row[0])
        self.mate = (dp + 1 - 2 * self.core, mp)
        self.beside_dp = self.at(1 - self.ylo, self.z)
        self.beside = (self.beside_dp, mp)
        self.zs = [(self.z + k) % 4 for k in range(4)]
        self.near_dp = [self.at(self.ylo, z) for z in self.zs]
        self.far_dp = [self.at(1 - self.ylo, z) for z in self.zs]
        self.near_slot = [self.ylo * 4 + z for z in self.zs]
        self.far_slot = [(1 - self.ylo) * 4 + z for z in self.zs]
        self.along = [(self.near_dp[k], mp) for k in (1, 2, 3)]
        self.group = [(dp, (mp + k) % GROUP) for k in range(1, GROUP)]
        self.copies = [((dp + k) % DP, mp) for k in range(1, DP)]

    def at(self, ylo, z):
        return ylo * 8 + z * 2 + self.core


def meet(peers):
    barrier = pltpu.get_barrier_semaphore()
    for peer in peers:
        pl.semaphore_signal(barrier, inc=1, device_id=peer, device_id_type=MESH)
    pl.semaphore_wait(barrier, len(peers))


class View:
    def __init__(self, ref, *chain):
        self.ref, self.chain = ref, chain

    @property
    def at(self):
        return Indexer(self)

    def build(self):
        ref = self.ref
        for index in self.chain:
            ref = ref.at[index]
        return ref

    def __getitem__(self, index):
        return self.build()[index]

    def __setitem__(self, index, value):
        self.build()[index] = value


class Indexer:
    def __init__(self, view):
        self.view = view

    def __getitem__(self, index):
        return View(self.view.ref, *self.view.chain, index)


class Copy:
    def __init__(self, make):
        self.make = make
        make().start()

    def wait(self):
        self.make().wait()

    def wait_recv(self):
        self.make().wait_recv()

    def wait_send(self):
        self.make().wait_send()


class Sender:
    def __init__(self, send_sem, recv_sem, local_sem):
        self.send_sem, self.recv_sem, self.local_sem = send_sem, recv_sem, local_sem
        self.count, self.started, self.locals = 0, [], 0

    def __call__(self, source, target, peer):
        k = self.count
        self.count += 1
        copy = Copy(
            lambda: pltpu.make_async_remote_copy(
                src_ref=source.build(),
                dst_ref=target.build(),
                send_sem=self.send_sem.at[k],
                recv_sem=self.recv_sem.at[k],
                device_id=peer,
                device_id_type=MESH,
            )
        )
        self.started.append(copy)
        return copy

    def local(self, source, target):
        k = self.locals
        self.locals += 1
        return Copy(
            lambda: pltpu.make_async_copy(source.build(), target.build(), self.local_sem.at[k])
        )

    def drain(self):
        for copy in self.started:
            copy.wait_send()
        self.started = []


def step(plan, count=1):
    for _ in range(count):
        next(plan, None)


def finish(plan):
    for _ in plan:
        pass


def gather_unit(send, place, buf, first, second):
    me, lx, rx, ox = place.row[0], place.row[3], place.row[1], place.row[2]
    ym, lxy, rxy = place.far_row[0], place.far_row[3], place.far_row[1]
    right, left, across = place.right, place.left, place.across
    half = PIECE // 2

    def go(block, slot, h, to):
        part = buf.at[block, slot, pl.ds(half * h, half)]
        return send(part, part, to)

    c = [go(second, me, 0, across), go(second, me, 1, across)]
    a = [go(first, me, 0, right), go(first, me, 1, left)]
    a += [go(first, me, 1, right), go(first, me, 0, left)]
    b = [go(second, me, 0, right), go(second, me, 1, left)]
    b += [go(second, me, 1, right), go(second, me, 0, left)]
    y = [go(first, me, 0, across), go(first, me, 1, across)]
    yield
    a[0].wait_recv()
    f = [go(first, lx, 0, right)]
    y.append(go(first, lx, 0, across))
    a[1].wait_recv()
    f.append(go(first, rx, 1, left))
    y.append(go(first, rx, 1, across))
    yield
    a[2].wait_recv()
    y.append(go(first, lx, 1, across))
    a[3].wait_recv()
    y.append(go(first, rx, 0, across))
    yield
    b[0].wait_recv()
    k = [go(second, lx, 0, right)]
    b[1].wait_recv()
    k.append(go(second, rx, 1, left))
    c[0].wait_recv()
    c[1].wait_recv()
    d = [go(second, ym, 0, right), go(second, ym, 1, left)]
    d += [go(second, ym, 1, right), go(second, ym, 0, left)]
    yield
    f[0].wait_recv()
    y.append(go(first, ox, 0, across))
    f[1].wait_recv()
    y.append(go(first, ox, 1, across))
    yield
    d[0].wait_recv()
    e = [go(second, lxy, 0, right)]
    d[1].wait_recv()
    e.append(go(second, rxy, 1, left))
    yield
    for copy in [b[2], b[3], d[2], d[3]] + k + e + y:
        copy.wait_recv()
    yield


def row_gather_unit(send, place, buf, first):
    me, lx, rx = place.xs[0], place.xs[3], place.xs[1]

    def go(block, slot, to):
        part = buf.at[block, slot]
        return send(part, part, to)

    a = [go(first, me, place.right), go(first + 1, me, place.left)]
    a += [go(first + 1, me, place.right), go(first, me, place.left)]
    yield
    a[0].wait_recv()
    f = [go(first, lx, place.right)]
    a[1].wait_recv()
    f.append(go(first + 1, rx, place.left))
    yield
    for copy in a[2:] + f:
        copy.wait_recv()
    yield


def weight_steps(send, place, buf):
    def go(slot, peer):
        return send(buf.at[slot], buf.at[slot], peer)

    own, other = place.dp, place.beside_dp
    one = go(own, place.beside)
    near = [go(own, peer) for peer in place.along]
    mates = [go(own, place.mate)]
    yield
    one.wait_recv()
    far = [go(other, peer) for peer in place.along]
    mates.append(go(other, place.mate))
    yield
    for k in range(3):
        near[k].wait_recv()
        mates.append(go(place.near_dp[3 - k], place.mate))
    yield
    for k in range(3):
        far[k].wait_recv()
        mates.append(go(place.far_dp[3 - k], place.mate))
    yield
    for copy in mates:
        copy.wait_recv()
    yield


def add_into(target, other):
    target[...] = (target[...].astype(f32) + other[...].astype(f32)).astype(bf16)


def scatter_unit(send, place, buf, first, second, y_in, x_in, xx_in, t_out, t_in, total):
    right, left, across = place.right, place.left, place.across
    half = PIECE // 2
    mine, theirs = place.row, place.far_row
    order = (2, 1, 3, 0)

    def first_hop(k, block, side):
        slot = side[2]
        return [
            send(buf.at[block, slot, pl.ds(0, half)], x_in.at[k, 0], right),
            send(buf.at[block, slot, pl.ds(half, half)], x_in.at[k, 1], left),
        ]

    def second_hop(k, block, side, hops):
        hops[0].wait_recv()
        add_into(buf.at[block, side[1], pl.ds(0, half)], x_in.at[k, 0])
        one = send(buf.at[block, side[1]], xx_in.at[k, 0], right)
        hops[1].wait_recv()
        add_into(buf.at[block, side[3], pl.ds(half, half)], x_in.at[k, 1])
        return [one, send(buf.at[block, side[3]], xx_in.at[k, 1], left)]

    def three(k, block, side):
        return (
            buf[block, side[0]].astype(f32) + xx_in[k, 0].astype(f32) + xx_in[k, 1].astype(f32)
        )

    ahead = [send(buf.at[first, theirs[n]], y_in.at[k], across) for k, n in enumerate(order)]
    hop_t = first_hop(1, second, theirs)
    hop_m = first_hop(2, second, mine)
    yield
    two_t = second_hop(1, second, theirs, hop_t)
    yield
    ahead[0].wait_recv()
    add_into(buf.at[first, mine[2]], y_in.at[0])
    hop_a = first_hop(0, first, mine)
    two_m = second_hop(2, second, mine, hop_m)
    yield
    for copy in two_t:
        copy.wait_recv()
    t_out[...] = three(1, second, theirs).astype(bf16)
    last = send(t_out, t_in, across)
    yield
    for k in range(1, 4):
        ahead[k].wait_recv()
        add_into(buf.at[first, mine[order[k]]], y_in.at[k])
    two_a = second_hop(0, first, mine, hop_a)
    yield
    for copy in two_m + [last]:
        copy.wait_recv()
    total[second] = three(2, second, mine) + t_in[...].astype(f32)
    yield
    for copy in two_a:
        copy.wait_recv()
    total[first] = three(0, first, mine)
    yield


def row_scatter_unit(send, place, buf, first, x_in, xx_in, keep):
    xs = place.xs
    hops = [
        send(buf.at[first, xs[2]], x_in.at[0], place.right),
        send(buf.at[first + 1, xs[2]], x_in.at[1], place.left),
    ]
    yield
    hops[0].wait_recv()
    add_into(buf.at[first, xs[1]], x_in.at[0])
    two = [send(buf.at[pl.ds(first, 2), xs[1]], xx_in.at[0], place.right)]
    hops[1].wait_recv()
    add_into(buf.at[first + 1, xs[3]], x_in.at[1])
    two.append(send(buf.at[pl.ds(first, 2), xs[3]], xx_in.at[1], place.left))
    yield
    for copy in two:
        copy.wait_recv()
    for k in range(2):
        total = buf[first + k, xs[0]].astype(f32)
        keep(first + k, total + xx_in[0, k].astype(f32) + xx_in[1, k].astype(f32))
    yield


def reduce_steps(send, place, grads, swaps, core_in, z_in, y_out, w_in, keep):
    core = place.core
    for i, swap in enumerate(swaps):
        swap.wait_recv()
        for k in (2 * i, 2 * i + 1):
            add_into(grads.at[k, core], core_in.at[k])
    hops = []
    for k in range(3):
        for y, slots in enumerate((place.far_slot, place.near_slot)):
            slot = slots[k + 1]
            hops.append(send(grads.at[slot, core], z_in.at[k, y], place.along[k]))
    yield

    def joined(y, slots):
        total = grads[slots[0], core].astype(f32)
        for k in range(3):
            total = total + z_in[k, y].astype(f32)
        return total

    for hop in hops[::2]:
        hop.wait_recv()
    y_out[...] = joined(0, place.far_slot).astype(bf16)
    cross = send(y_out, w_in, place.beside)
    yield
    for hop in hops[1::2]:
        hop.wait_recv()
    cross.wait_recv()
    keep(joined(1, place.near_slot) + w_in[...].astype(f32))
    yield


def rows(block, count=L):
    return pl.ds(pl.multiple_of(block * count, count), count)


def pick(columns, block):
    lane = lax.broadcasted_iota(jnp.int32, columns.shape, 1)
    return jnp.sum(jnp.where(lane == block, columns, 0.0), axis=1, keepdims=True)


def run_blocks(body, hooks):
    def one(i, carry):
        body(i)
        for k, hook in hooks.items():
            pl.when(i == k)(hook)
        return carry

    lax.fori_loop(0, BLOCKS, one, 0)


def front_kernel(
    normed, own_weights, own_out, grad, taps, heads, skip, gain,
    whole_o, weights_o, out_o, back_o, raw_o, gates_o, steps_o, scan_o, states_o, g_gated_o, gated_o, sums,
    whole, weights, out, back, raw, gates, steps, scan, mixed, states, g_gated, gated, halves,
    squares, state, inbox, send_sem, recv_sem, local_sem,
):
    (
        normed, own_weights, own_out, grad, taps, heads, skip, gain, whole_o, weights_o, out_o,
        back_o, raw_o, gates_o, steps_o, scan_o, states_o, g_gated_o, gated_o, sums, whole,
        weights, out, back, raw, gates, steps, scan, mixed, states, g_gated, gated, halves,
        squares, state, inbox,
    ) = map(
        View,
        (
            normed, own_weights, own_out, grad, taps, heads, skip, gain, whole_o, weights_o, out_o,
            back_o, raw_o, gates_o, steps_o, scan_o, states_o, g_gated_o, gated_o, sums, whole,
            weights, out, back, raw, gates, steps, scan, mixed, states, g_gated, gated, halves,
            squares, state, inbox,
        ),
    )
    place = Place()
    whole[:, place.mp] = normed[...]
    weights[place.dp] = own_weights[...]
    out[place.dp, :, :IN] = own_out[...]
    back[:, place.xs[0]] = grad[...]
    meet(place.group + [place.mate, place.beside] + place.along)
    send = Sender(send_sem, recv_sem, local_sem)
    units = [gather_unit(send, place, whole, 2 * u, 2 * u + 1) for u in range(4)]
    columns = weight_steps(send, place, weights)
    outs = weight_steps(send, place, out)
    backs = [row_gather_unit(send, place, back, 2 * u) for u in range(4)]
    stored = []

    step(columns)
    pair = send(own_out, out.at[place.dp, :, pl.ds(IN, IN)], place.across)
    step(units[0])
    step(columns)
    step(units[1])
    step(units[0], 2)
    step(units[2])
    step(units[0], 2)
    step(columns)
    step(units[1], 2)
    step(units[3])
    step(units[0], 2)
    step(units[1], 2)
    step(columns)
    pair.wait_recv()
    step(outs)
    step(units[2], 2)
    step(units[1], 2)
    step(columns)

    raw[pl.ds(0, 8)] = jnp.zeros((8, MIX), f32)
    state[...] = jnp.zeros((N, IN), f32)
    squares[...] = jnp.zeros((L, 128), f32)
    lane = lax.broadcasted_iota(jnp.int32, (L, 128), 1)

    def body(i):
        at = rows(i)
        both = mm(whole[i].reshape(L, D), weights[...].reshape(D, COLS))
        gates[at] = both[:, :IN]
        steps[at] = both[:, IN + MIX :]
        raw[pl.ds(pl.multiple_of(i * L + 8, 8), L)] = both[:, IN : IN + MIX]
        states[i] = state[...]
        window = raw[pl.ds(pl.multiple_of(i * L, 8), L + 8)]
        inner, outer, after = fwd_block(
            window, gates[at], steps[at], taps[...], heads[...], skip[...], state[...]
        )
        scan[at] = inner
        mixed[at] = outer
        state[...] = after
        square = jnp.sum(outer * outer, axis=1, keepdims=True)
        squares[...] = jnp.where(lane == i, square, squares[...])

    def hook_0():
        step(units[2], 2)
        step(units[3], 2)
        step(outs)

    def hook_1():
        step(units[2], 3)
        step(units[3], 2)
        for unit in backs:
            step(unit)

    def hook_2():
        step(units[3], 1)
        step(outs)

    def hook_3():
        step(units[3], 2)
        step(backs[0])
        step(outs)

    def hook_4():
        step(backs[1])
        step(outs)

    def hook_5():
        step(backs[2])
        stored.append(send.local(whole, whole_o))
        stored.append(send.local(weights, weights_o))

    def hook_6():
        step(backs[3])
        stored.append(send.local(out, out_o))

    run_blocks(
        body,
        {0: hook_0, 1: hook_1, 2: hook_2, 3: hook_3, 4: hook_4, 5: hook_5, 6: hook_6},
    )
    states[BLOCKS] = state[...]
    stored.append(send.local(raw, raw_o))
    stored.append(send.local(gates, gates_o))
    stored.append(send.local(steps, steps_o))
    stored.append(send.local(scan, scan_o))
    stored.append(send.local(states, states_o))
    crossing = []
    for u in range(4):
        finish(backs[u])
        pairs = pl.ds(2 * u, 2)
        both = mm(back[pairs].reshape(L, D), out[...].reshape(D, 2 * IN)).astype(bf16)
        g_gated[pairs, place.hi] = both[:, :IN].reshape(2, L // 2, IN)
        halves[pairs] = both[:, IN:].reshape(2, L // 2, IN)
        crossing.append(send(halves.at[pairs], g_gated.at[pairs, place.hi], place.across))
    stored.append(send.local(back, back_o))

    for u in range(4):
        crossing[u].wait_recv()
        for i in (2 * u, 2 * u + 1):
            part = g_gated[i].reshape(L, IN).astype(f32) * gain[...] * mixed[pl.ds(i * L, L)]
            product = jnp.sum(part, axis=1, keepdims=True)
            squares[...] = jnp.where(lane == i + 8, product, squares[...])
    stored.append(send.local(g_gated, g_gated_o))
    inbox[place.mp] = squares[...].T[:16]
    copies = [send(inbox.at[place.mp], inbox.at[place.mp], peer) for peer in place.group]
    for copy in copies:
        copy.wait_recv()
    total = inbox[0]
    for k in range(1, GROUP):
        total = total + inbox[k]
    top = lax.rsqrt(total[:8] * (1.0 / INNER) + epsilon)
    found = jnp.concatenate([top, total[8:], jnp.zeros((112, L), f32)], 0).T
    sums[...] = found
    for i in range(BLOCKS):
        rounded = (mixed[pl.ds(i * L, L)] * found[:, i : i + 1] * gain[...]).astype(bf16)
        gated[i] = rounded.reshape(2, L // 2, IN)
    stored.append(send.local(gated, gated_o))
    for copy in stored:
        copy.wait()
    send.drain()


def back_kernel(
    whole_i, weights_i, out_i, back_i, raw_i, gates_i, steps_i, scan_i, states_i, g_gated_i, gated_i,
    sums, taps, heads, skip, gain, tokens, grad_out, valid, norm_gain,
    layer_out, token_grad, gain_grad, main_grad, side_grad, out_grad, shared_sums, copy_sums,
    weights, out, gated, gated_in, raw, gates, steps, scan, states, g_gated, g_all, left,
    row_parts, row_x, row_xx, parts, y_in, x_in, xx_in, t_out, t_in,
    grads, core_in, z_in, y_out, w_in, o_core, o_z, o_out, o_in, pair_out, pair_in,
    totals, d_state, after,
    inbox, side_box, sums_box, gain_box, gain_all, send_sem, recv_sem, local_sem,
):
    (
        whole_i, weights_i, out_i, back_i, raw_i, gates_i, steps_i, scan_i, states_i, g_gated_i,
        gated_i, sums, taps, heads, skip, gain, tokens, grad_out, valid, norm_gain, layer_out,
        token_grad, gain_grad, main_grad, side_grad, out_grad, shared_sums, copy_sums, weights,
        out, gated, gated_in, raw, gates, steps, scan, states, g_gated, g_all, left,
        row_parts, row_x, row_xx, parts, y_in, x_in, xx_in, t_out, t_in, grads, core_in,
        z_in, y_out, w_in, o_core, o_z, o_out, o_in, pair_out, pair_in, totals, d_state,
        after, inbox, side_box, sums_box, gain_box, gain_all,
    ) = map(
        View,
        (
            whole_i, weights_i, out_i, back_i, raw_i, gates_i, steps_i, scan_i, states_i, g_gated_i,
            gated_i, sums, taps, heads, skip, gain, tokens, grad_out, valid, norm_gain, layer_out,
            token_grad, gain_grad, main_grad, side_grad, out_grad, shared_sums, copy_sums, weights,
            out, gated, gated_in, raw, gates, steps, scan, states, g_gated, g_all, left,
            row_parts, row_x, row_xx, parts, y_in, x_in, xx_in, t_out, t_in, grads, core_in,
            z_in, y_out, w_in, o_core, o_z, o_out, o_in, pair_out, pair_in, totals, d_state,
            after, inbox, side_box, sums_box, gain_box, gain_all,
        ),
    )
    place = Place()
    send = Sender(send_sem, recv_sem, local_sem)

    def loads(i, slot):
        return [
            (raw_i.at[pl.ds(pl.multiple_of(i * L, 8), L + 8)], raw.at[slot]),
            (gates_i.at[rows(i)], gates.at[slot]),
            (steps_i.at[rows(i)], steps.at[slot]),
            (scan_i.at[rows(i)], scan.at[slot]),
            (states_i.at[i], states.at[slot]),
            (g_gated_i.at[i], g_gated.at[slot]),
        ]

    def load(i, slot, start):
        for k, (source, target) in enumerate(loads(i, slot)):
            copy = pltpu.make_async_copy(
                source.build(), target.build(), local_sem.at[10 + 6 * slot + k]
            )
            if start:
                copy.start()
            else:
                copy.wait()

    load(BLOCKS - 1, 1, True)
    first = [
        send.local(gated_i.at[:, place.hi], gated),
        send.local(out_i, out),
        send.local(weights_i, weights),
    ]
    load(BLOCKS - 2, 0, True)
    meet(place.group + place.copies)
    crossing = [
        send(gated_i.at[pl.ds(2 * u, 2), place.lo], gated_in.at[pl.ds(2 * u, 2)], place.across)
        for u in (3, 2, 1, 0)
    ][::-1]
    d_state[...] = jnp.zeros((N, IN), f32)
    after[...] = jnp.zeros((8, MIX), f32)
    totals[...] = jnp.zeros((8, MIX), f32)
    first[0].wait()
    first[1].wait()
    first[2].wait()

    def body(j):
        i = BLOCKS - 1 - j
        slot = lax.rem(i, 2)
        load(i, slot, False)
        g, ds, top, found = bwd_block(
            raw[slot], gates[slot], steps[slot], taps[...], heads[...], skip[...], gain[...],
            states[slot], scan[slot], pick(sums[...], i), pick(sums[...], i + 8),
            g_gated[slot].reshape(L, IN).astype(f32), d_state[...], after[...],
        )
        pl.when(i >= 2)(lambda: load(i - 2, slot, True))
        g_all[rows(i)] = g
        d_state[...] = ds
        after[...] = top
        tap_sums, gain_sum, skip_sum, decay_sum, bias_sum = found
        blank = jnp.zeros((1, MIX - IN), f32)
        fill = jnp.zeros((1, MIX - 2 * N), f32)
        totals[...] += jnp.concatenate(
            [
                tap_sums,
                jnp.concatenate([gain_sum, blank], 1),
                jnp.concatenate([skip_sum, blank], 1),
                jnp.concatenate([decay_sum, bias_sum, fill], 1),
            ],
            0,
        )
        part = mm_nt(g, weights[...].reshape(D, COLS))
        parts[i] = part.astype(bf16).reshape(GROUP, PIECE, D)

    def keep_layer(i, total):
        layer_out[i] = (tokens[i].astype(f32) + valid[i] * total).astype(bf16)

    row_units = [
        row_scatter_unit(
            send, place, row_parts, 2 * u, row_x.at[u], row_xx.at[u], keep_layer
        )
        for u in range(4)
    ]
    units = [
        scatter_unit(
            send, place, parts, 2 * u, 2 * u + 1,
            y_in.at[u], x_in.at[u], xx_in.at[u], t_out.at[u], t_in.at[u], token_grad,
        )
        for u in range(4)
    ]

    def row_product(u):
        crossing[u].wait_recv()
        pairs = pl.ds(2 * u, 2)
        own = gated[pairs].reshape(L, IN)
        other = gated_in[pairs].reshape(L, IN)
        flat = out[...].reshape(D, 2 * IN)
        part = mm_nt(own, flat[:, :IN]) + mm_nt(other, flat[:, IN:])
        row_parts[pairs] = part.astype(bf16).reshape(2, 4, PIECE, D)
        step(row_units[u])

    o_swaps, swaps = [], []
    o_grads = grads.at[:, :, :, pl.ds(0, 2 * IN)]
    back_loads = []

    def load_back(i):
        source = back_i.at[:, :, :, pl.ds(i * 384, 384)]
        back_loads.append(send.local(source, left.at[i % 2, :, pl.ds(0, 4)]))

    def out_products():
        for i in range(4):
            back_loads[i].wait()
            side = left[i % 2, :, pl.ds(0, 4)].reshape(BLOCKS * L // 2, 384)
            own = gated[...].reshape(BLOCKS * L // 2, IN)
            other = gated_in[...].reshape(BLOCKS * L // 2, IN)
            pairs = pl.ds(2 * i, 2)
            grads[pairs, :, :, :IN] = mm_tn(side, own).astype(bf16).reshape(2, 2, 96, IN)
            grads[pairs, :, :, IN : 2 * IN] = (
                mm_tn(side, other).astype(bf16).reshape(2, 2, 96, IN)
            )
            if i < 2:
                load_back(i + 2)
            o_swaps.append(
                send(o_grads.at[pairs, place.other_core], o_core.at[pairs], place.mate)
            )

    def keep_out(total):
        pair_out[...] = total[:, IN:]
        out_grad[...] = total[:, :IN]

    o_plan = reduce_steps(send, place, o_grads, o_swaps, o_core, o_z, o_out, o_in, keep_out)
    whole_loads = []

    def load_whole(i):
        source = whole_i.at[:, :, :, pl.ds(i * 384, 384)]
        whole_loads.append(send.local(source, left.at[i % 2]))

    def hook_0():
        row_product(3)

    def hook_1():
        step(units[3])
        row_product(2)
        step(row_units[3])

    def hook_2():
        step(units[3])
        row_product(1)
        step(row_units[3])
        step(row_units[2])

    def hook_3():
        step(units[2])
        step(units[3])
        row_product(0)
        step(row_units[1])
        step(row_units[2])
        load_back(0)
        load_back(1)

    def hook_4():
        step(units[3], 2)
        step(units[2])
        step(row_units[0])
        step(row_units[1])
        out_products()
        load_whole(0)
        load_whole(1)

    def hook_5():
        step(units[1])
        step(units[3], 2)
        step(units[2], 2)
        step(row_units[0])
        step(o_plan)

    def hook_6():
        step(units[1])
        step(units[2], 2)
        step(o_plan)

    crossed = []

    def hook_7():
        send.drain()
        step(units[0])
        step(units[1], 2)
        step(units[2])
        step(o_plan)
        crossed.append(send(pair_out, pair_in, place.across))

    run_blocks(
        body,
        {
            0: hook_0, 1: hook_1, 2: hook_2, 3: hook_3,
            4: hook_4, 5: hook_5, 6: hook_6, 7: hook_7,
        },
    )

    sums_box[place.dp] = totals[...]
    early = [send(sums_box.at[place.dp], sums_box.at[place.dp], peer) for peer in place.copies]

    for i in range(4):
        whole_loads[i].wait()
        side = left[i % 2].reshape(BLOCKS * L, 384)
        pairs = pl.ds(2 * i, 2)
        grads[pairs] = mm_tn(side, g_all[...]).astype(bf16).reshape(2, 2, 96, COLS)
        if i < 2:
            load_whole(i + 2)
        swaps.append(send(grads.at[pairs, place.other_core], core_in.at[pairs], place.mate))
        step(units[0])
        step(units[1])

    def keep_main(total):
        main_grad[...] = total[:, : 2 * IN]
        side_box[place.mp] = total[:, 2 * IN :].astype(bf16)

    plan = reduce_steps(send, place, grads, swaps, core_in, z_in, y_out, w_in, keep_main)
    step(plan)
    finish(units[2])
    finish(units[1])
    finish(units[0])
    crossed[0].wait_recv()
    out_grad[...] += pair_in[...]

    gain_row = norm_gain[...]
    gain_sum = jnp.zeros((1, D), f32)
    for i in range(BLOCKS):
        x = tokens[i].astype(f32)
        s = lax.rsqrt(jnp.mean(x * x, axis=1, keepdims=True) + epsilon)
        g = token_grad[i]
        dot = jnp.sum(g * gain_row * x, axis=1, keepdims=True)
        token_grad[i] = grad_out[i].astype(f32) + s * gain_row * g - x * (s * s * s * dot * (1.0 / D))
        gain_sum = gain_sum + jnp.sum(g * x * s, axis=0, keepdims=True)
    gain_box[place.mp] = jnp.concatenate([gain_sum, jnp.zeros((7, D), f32)], 0)
    gains = [send(gain_box.at[place.mp], gain_box.at[place.mp], peer) for peer in place.group]

    for copy in early:
        copy.wait_recv()
    copied = sums_box[0]
    for k in range(1, DP):
        copied = copied + sums_box[k]
    copy_sums[...] = copied
    inbox[place.mp] = copied[:, IN:]
    shares = [send(inbox.at[place.mp], inbox.at[place.mp], peer) for peer in place.group]
    step(plan)
    for copy in gains:
        copy.wait_recv()
    total = gain_box[0]
    for k in range(1, GROUP):
        total = total + gain_box[k]
    gain_all[place.dp] = total
    ends = [send(gain_all.at[place.dp], gain_all.at[place.dp], peer) for peer in place.copies]
    step(plan)
    sides = [send(side_box.at[place.mp], side_box.at[place.mp], peer) for peer in place.group]
    for copy in ends:
        copy.wait_recv()
    total = gain_all[0]
    for k in range(1, DP):
        total = total + gain_all[k]
    gain_grad[...] = total
    for copy in sides + shares:
        copy.wait_recv()
    both, steps_sum = 0.0, 0.0
    lane = lax.broadcasted_iota(jnp.int32, (N, N), 1)
    source = lax.broadcasted_iota(jnp.int32, (N, N), 0)
    shared = inbox[0]
    for k in range(GROUP):
        piece = side_box[k]
        both = both + piece[:, : 2 * N].astype(f32)
        spot = jnp.where((lane == source + HD * k) & (source < HD), 1.0, 0.0).astype(bf16)
        steps_sum = steps_sum + mm(piece[:, 2 * N :], spot)
        if k:
            shared = shared + inbox[k]
    side_grad[...] = jnp.concatenate([both, steps_sum], 1)
    shared_sums[...] = shared
    send.drain()


def call(kernel, outs, scratch, sems, collective, args, flops):
    vmem, anywhere = pltpu.VMEM, pl.ANY
    spec = {True: pl.BlockSpec(memory_space=anywhere), False: pl.BlockSpec(memory_space=vmem)}
    return pl.pallas_call(
        kernel,
        out_shape=[jax.ShapeDtypeStruct(shape, dtype) for shape, dtype, _ in outs],
        in_specs=[spec[far] for _, far in args],
        out_specs=[spec[far] for _, _, far in outs],
        scratch_shapes=[pltpu.VMEM(shape, dtype) for shape, dtype in scratch]
        + [pltpu.SemaphoreType.DMA((k,)) for k in sems],
        compiler_params=pltpu.CompilerParams(
            collective_id=collective, has_side_effects=True, vmem_limit_bytes=VMEM_BYTES
        ),
        cost_estimate=pl.CostEstimate(
            flops=flops,
            bytes_accessed=sum(a.size * a.dtype.itemsize for a, _ in args),
            transcendentals=0,
        ),
        name=kernel.__name__,
    )(*[a for a, _ in args])


def on_device(
    tokens,
    seq_len,
    norm_gain,
    main_weight,
    side_weight,
    side_terms,
    channel_terms,
    head_terms,
    output_weight,
    cotangent,
):
    place = lax.axis_index("mp")
    count, span = BLOCKS * L, D // DP
    seq = tokens[0].astype(f32)
    scale = lax.rsqrt(jnp.mean(seq * seq, axis=-1, keepdims=True) + epsilon)
    normed = (seq * scale * norm_gain).astype(bf16)
    positions = (
        jnp.arange(BLOCKS)[:, None] * L + place * PIECE + jnp.arange(PIECE)[None, :]
    )
    valid = (positions < seq_len[0]).astype(f32)[:, :, None]
    grad_branch = (valid * cotangent[0].astype(f32)).astype(bf16)
    own_steps = lax.dynamic_slice_in_dim(side_weight, 2 * N + place * HD, HD, 1)
    own_weights = jnp.concatenate(
        [
            main_weight.reshape(span, 2 * IN),
            side_weight[:, : 2 * N],
            own_steps,
            jnp.zeros((span, N - HD), bf16),
        ],
        1,
    )
    taps = jnp.concatenate([channel_terms[: CONV + 1], side_terms], 1)
    taps = jnp.concatenate([taps, jnp.zeros((3, MIX), f32)], 0)
    gain = channel_terms[CONV + 1 :]
    heads = jnp.zeros((8, N), f32)
    heads = heads.at[0, :HD].set(head_terms[0]).at[1, :HD].set(-jnp.exp(head_terms[1]))
    skip = jnp.repeat(head_terms[2], PW)[None]

    kept = [
        ((BLOCKS, GROUP, PIECE, D), bf16),
        ((DP, span, COLS), bf16),
        ((DP, span, 2 * IN), bf16),
        ((BLOCKS, 4, PIECE, D), bf16),
        ((count + 8, MIX), f32),
        ((count, IN), f32),
        ((count, N), f32),
        ((count, IN), f32),
        ((BLOCKS + 1, N, IN), f32),
        ((BLOCKS, 2, L // 2, IN), bf16),
        ((BLOCKS, 2, L // 2, IN), bf16),
    ]
    scratch = kept[:8] + [((count, IN), f32)] + kept[8:]
    scratch += [
        ((BLOCKS, L // 2, IN), bf16),
        ((L, 128), f32),
        ((N, IN), f32),
        ((GROUP, 16, L), f32),
    ]
    near = [(a, False) for a in (normed, own_weights, output_weight.T, grad_branch)]
    small = [(a, False) for a in (taps, heads, skip, gain)]
    *saved, sums = call(
        front_kernel,
        [(shape, dtype, True) for shape, dtype in kept] + [((L, 128), f32, False)],
        scratch,
        (192, 192, 16),
        0,
        near + small,
        12 * 10**9,
    )
    ends = (tokens[0], cotangent[0], valid, norm_gain[None])
    layer_out, token_grad, gain_grad, main_grad, side_grad, out_grad, shared_sums, copy_sums = call(
        back_kernel,
        [
            ((BLOCKS, PIECE, D), bf16, False),
            ((BLOCKS, PIECE, D), f32, False),
            ((8, D), f32, False),
            ((span, 2 * IN), f32, False),
            ((span, 3 * N), f32, False),
            ((span, IN), f32, False),
            ((8, 2 * N), f32, False),
            ((8, MIX), f32, False),
        ],
        [
            ((DP, span, COLS), bf16),
            ((DP, span, 2 * IN), bf16),
            ((BLOCKS, L // 2, IN), bf16),
            ((BLOCKS, L // 2, IN), bf16),
            ((2, L + 8, MIX), f32),
            ((2, L, IN), f32),
            ((2, L, N), f32),
            ((2, L, IN), f32),
            ((2, N, IN), f32),
            ((2, 2, L // 2, IN), bf16),
            ((count, COLS), bf16),
            ((2, BLOCKS, GROUP, PIECE, 384), bf16),
            ((BLOCKS, 4, PIECE, D), bf16),
            ((4, 2, PIECE, D), bf16),
            ((4, 2, 2, PIECE, D), bf16),
            ((BLOCKS, GROUP, PIECE, D), bf16),
            ((4, 4, PIECE, D), bf16),
            ((4, 3, 2, PIECE // 2, D), bf16),
            ((4, 3, 2, PIECE, D), bf16),
            ((4, PIECE, D), bf16),
            ((4, PIECE, D), bf16),
            ((8, 2, span, COLS), bf16),
            ((8, span, COLS), bf16),
            ((3, 2, span, COLS), bf16),
            ((span, COLS), bf16),
            ((span, COLS), bf16),
            ((8, span, 2 * IN), bf16),
            ((3, 2, span, 2 * IN), bf16),
            ((span, 2 * IN), bf16),
            ((span, 2 * IN), bf16),
            ((span, IN), f32),
            ((span, IN), f32),
            ((8, MIX), f32),
            ((N, IN), f32),
            ((8, MIX), f32),
            ((GROUP, 8, 2 * N), f32),
            ((GROUP, span, 3 * N), bf16),
            ((DP, 8, MIX), f32),
            ((GROUP, 8, D), f32),
            ((DP, 8, D), f32),
        ],
        (224, 224, 24),
        1,
        [(a, True) for a in saved]
        + [(sums, False)]
        + small
        + [(a, False) for a in ends],
        24 * 10**9,
    )
    main_grad = main_grad.reshape(span, 2, IN)
    conv_total = shared_sums[: CONV + 1]
    channel_total = copy_sums[: CONV + 2, :IN]
    decay = heads[1, :HD] * copy_sums[CONV + 3, :HD]
    skip_total = copy_sums[CONV + 2, :IN].reshape(HD, PW).sum(1)
    head_total = jnp.stack([copy_sums[CONV + 3, N : N + HD], decay, skip_total])
    return (
        layer_out[None],
        token_grad[None],
        gain_grad[0],
        main_grad,
        side_grad[:, : 2 * N + 48],
        conv_total,
        channel_total,
        head_total,
        out_grad.T,
    )


def solution(mesh):
    placed = (
        P("dp", None, "mp", None),
        P("dp"),
        P(),
        P("dp", None, "mp"),
        P("dp", None),
        P(),
        P(None, "mp"),
        P(None, "mp"),
        P("mp", "dp"),
        P("dp", None, "mp", None),
    )
    return jax.shard_map(
        on_device,
        mesh=mesh,
        in_specs=placed,
        out_specs=(
            P("dp", None, "mp", None),
            P("dp", None, "mp", None),
            P(),
            P("dp", None, "mp"),
            P("dp", None),
            P(),
            P(None, "mp"),
            P(None, "mp"),
            P("mp", "dp"),
        ),
        check_vma=False,
    )
```

```python
import functools

import jax
import jax.numpy as jnp
from jax import lax
from jax.experimental import pallas as pl
from jax.experimental.pallas import tpu as pltpu
from jax.sharding import PartitionSpec as P

f32, bf16 = jnp.float32, jnp.bfloat16
CONV, D, INNER = 4, 1536, 3072
L, N, PW, IN, HD = 256, 128, 64, 384, 6
BLOCKS, GROUP, PIECE, DP, HEADS = 8, 8, 32, 16, 48
COLS = 2 * IN + 3 * N
MIX = IN + 2 * N
MESH = pl.DeviceIdType.MESH
VMEM_BYTES = 63 * 2**20
epsilon = 1e-05
NEG = -1e30

def mm(a, b):
    return lax.dot_general(a, b, (((1,), (0,)), ((), ())), preferred_element_type=f32)
def mm_nt(a, b):
    return lax.dot_general(a, b, (((1,), (1,)), ((), ())), preferred_element_type=f32)
def mm_tn(a, b):
    return lax.dot_general(a, b, (((0,), (0,)), ((), ())), preferred_element_type=f32)

def thirds(x):
    hi = x.astype(bf16)
    rest = x - hi.astype(f32)
    mid = rest.astype(bf16)
    return hi, mid, (rest - mid.astype(f32)).astype(bf16)

def exact_left(mask, x):
    a, b, c = thirds(x)
    return mm(mask, a) + mm(mask, b) + mm(mask, c)

def exact_right(x, mask):
    a, b, c = thirds(x)
    return mm(a, mask) + mm(b, mask) + mm(c, mask)

def sigmoid(x):
    return 1.0 / (1.0 + jnp.exp(-x))

def softplus(x):
    return jnp.maximum(x, 0.0) + jnp.log1p(jnp.exp(-jnp.abs(x)))

def tri(lower):
    r = lax.broadcasted_iota(jnp.int32, (L, L), 0)
    c = lax.broadcasted_iota(jnp.int32, (L, L), 1)
    return jnp.where((r >= c) if lower else (r <= c), 1.0, 0.0).astype(bf16)

def spread(cols, low):
    out = []
    for j in range(3):
        a = jnp.broadcast_to(cols[:, 2 * j : 2 * j + 1], (cols.shape[0], 128))
        b = jnp.broadcast_to(cols[:, 2 * j + 1 : 2 * j + 2], (cols.shape[0], 128))
        out.append(jnp.where(low, a, b))
    return jnp.concatenate(out, 1)

def conv_pre(window, taps):
    total = taps[4:5]
    for k in range(4):
        total = total + taps[k : k + 1] * window[5 + k : 5 + k + L]
    return total

def low_lanes(rows):
    return lax.broadcasted_iota(jnp.int32, (rows, 128), 1) < 64

def head_quantities(dt_raw, heads):
    pre = dt_raw + heads[0:1]
    dt = softplus(pre)
    logs = exact_left(tri(True), dt * heads[1:2])
    return pre, dt, logs

def half_mask(t):
    rows = 128
    r = lax.broadcasted_iota(jnp.int32, (rows, 128 * (t + 1)), 0) + 128 * t
    c = lax.broadcasted_iota(jnp.int32, (rows, 128 * (t + 1)), 1)
    return r >= c

def weights_of(logs, logs_t, h, t):
    w = 128 * (t + 1)
    col = jnp.broadcast_to(logs[128 * t : 128 * (t + 1), h : h + 1], (128, 128))
    if t:
        col = jnp.concatenate([col, col], 1)
    gap = col - logs_t[h : h + 1, :w]
    return jnp.exp(jnp.where(half_mask(t), gap, NEG))

X, GATE, D_GATE, XD, TXD, GROW, TAIL, STEP = (IN * k for k in range(8))
KEYS = 8 * IN
D_ACT = KEYS + 2 * N
KEPT = D_ACT + MIX
SCAN, DT, D_STEP, KEPT_F = 0, IN, IN + N, IN + 2 * N


def fwd_block(window, gates, dt_raw, taps, heads, skip, state, tick, kept, kept_f, kept_h):
    low = low_lanes(L)
    total = conv_pre(window, taps)
    sig = sigmoid(total)
    act = total * sig
    kept[:, pl.ds(D_ACT, MIX)] = (sig + act * (1.0 - sig)).astype(bf16)
    x, keys = act[:, :IN], act[:, IN:].astype(bf16)
    kept[:, pl.ds(X, IN)] = x.astype(bf16)
    kept[:, pl.ds(KEYS, 2 * N)] = keys
    b, c = keys[:, :N], keys[:, N:]
    pre, dt, logs = head_quantities(dt_raw, heads)
    kept_f[:, pl.ds(DT, N)] = dt
    kept_f[:, pl.ds(D_STEP, N)] = sigmoid(pre)
    logs_t = logs.T
    dt_l, logs_l = spread(dt, low), spread(logs, low)
    xd = (dt_l * x).astype(bf16)
    kept[:, pl.ds(STEP, IN)] = dt_l.astype(bf16)
    kept[:, pl.ds(XD, IN)] = xd
    g = mm_nt(c, b)
    rows = [[], []]
    zero = jnp.zeros((), bf16)
    for j in range(3):
        tick(2 + j)
        pair = xd[:, 128 * j : 128 * (j + 1)]
        own = (jnp.where(low, pair, zero), jnp.where(low, zero, pair))
        for t in range(2):
            w = 128 * (t + 1)
            total_y = 0.0
            for e in range(2):
                h = 2 * j + e
                wt = weights_of(logs, logs_t, h, t)
                m = wt * g[128 * t : 128 * (t + 1), :w]
                total_y = total_y + mm(m.astype(bf16), own[e][:w])
                kept_h[h, pl.ds(128 * t, w)] = m.T.astype(bf16)
                for k in range(t + 1):
                    piece = wt[:, 128 * k : 128 * (k + 1)]
                    kept_h[HD + h, pl.ds(128 * (t + k), 128)] = piece.astype(bf16)
            rows[t].append(total_y)
    intra = jnp.concatenate([jnp.concatenate(r, 1) for r in rows], 0)
    grow = jnp.exp(logs_l)
    scan = intra + grow * mm(c, state.astype(bf16))
    last = logs_l[L - 1 : L]
    tails = jnp.exp(last - logs_l)
    txd = (tails * xd.astype(f32)).astype(bf16)
    state = jnp.exp(last) * state + mm_tn(b, txd)
    gsig = sigmoid(gates)
    gate = gates * gsig
    mixed = (scan + skip * x) * gate
    kept[:, pl.ds(GROW, IN)] = grow.astype(bf16)
    kept[:, pl.ds(TAIL, IN)] = tails.astype(bf16)
    kept[:, pl.ds(TXD, IN)] = txd
    kept[:, pl.ds(GATE, IN)] = gate.astype(bf16)
    kept[:, pl.ds(D_GATE, IN)] = (gsig + gate * (1.0 - gsig)).astype(bf16)
    kept_f[:, pl.ds(SCAN, IN)] = scan
    return mixed, state


def bwd_block(window, kept, kept_f, kept_h, taps, heads, skip, gain, state, rnorm, products, g_gated, d_state, after, tick):
    low = low_lanes(L)

    def wide(at, width=IN):
        return kept[:, pl.ds(at, width)]

    x, gate = wide(X).astype(f32), wide(GATE).astype(f32)
    scan = kept_f[:, pl.ds(SCAN, IN)]
    y = scan + skip * x
    mixed = y * gate
    g_mixed = rnorm * (g_gated * gain) - mixed * (rnorm * rnorm * rnorm * products * (1.0 / INNER))
    gain_sum = jnp.sum(g_gated * mixed * rnorm, axis=0, keepdims=True)
    dy = g_mixed * gate
    d_gates = (g_mixed * y * wide(D_GATE).astype(f32)).astype(bf16)
    skip_sum = jnp.sum(dy * x, axis=0, keepdims=True)
    dyb = dy.astype(bf16)
    zero = jnp.zeros((), bf16)
    dg = [0.0, 0.0]
    parts = []
    for j in range(3):
        if j == 1:
            tick(2)
        pair_x = kept[:, pl.ds(XD + 128 * j, 128)]
        pair_y = dyb[:, 128 * j : 128 * (j + 1)]
        own = (jnp.where(low, pair_y, zero), jnp.where(low, zero, pair_y))
        upper, lower = 0.0, 0.0
        for e in range(2):
            h = 2 * j + e
            for t in range(2):
                w = 128 * (t + 1)
                mine = own[e][128 * t : 128 * (t + 1)]
                dm = mm_nt(mine, pair_x[:w])
                pieces = [kept_h[HD + h, pl.ds(128 * (t + k), 128)] for k in range(t + 1)]
                wt = jnp.concatenate(pieces, 1) if t else pieces[0]
                dg[t] = dg[t] + dm * wt.astype(f32)
                back = mm(kept_h[h, pl.ds(128 * t, w)], mine)
                upper = upper + back[:128]
                if t:
                    lower = lower + back[128:]
        parts.append(jnp.concatenate([upper, lower], 0))
    tick(4)
    d_intra = jnp.concatenate(parts, 1)
    b, c = wide(KEYS, N), wide(KEYS + N, N)
    grow, txd = wide(GROW), wide(TXD)
    last = grow[L - 1 : L].astype(f32)
    sb = state.astype(bf16)
    dsb = d_state.astype(bf16)
    edy = (grow.astype(f32) * dy).astype(bf16)
    v = mm(b, dsb)
    dxd = d_intra + wide(TAIL).astype(f32) * v
    dg0, dg1 = dg[0].astype(bf16), dg[1].astype(bf16)
    dc = mm_nt(edy, sb) + jnp.concatenate([mm(dg0, b[:128]), mm(dg1, b)], 0)
    first = mm_tn(dg0, c[:128])
    second = mm_tn(dg1, c[128:])
    db = mm_nt(txd, dsb) + jnp.concatenate([first + second[:128], second[128:]], 0)
    tail_part = txd.astype(f32) * v
    z = dyb.astype(f32) * scan - wide(XD).astype(f32) * d_intra - tail_part
    kept_sum = jnp.sum(state * dsb.astype(f32), axis=0, keepdims=True)
    boundary = last * kept_sum + jnp.sum(tail_part, axis=0, keepdims=True)
    row = lax.broadcasted_iota(jnp.int32, (L, IN), 0)
    z = jnp.where(row == L - 1, z + boundary, z)
    r = lax.broadcasted_iota(jnp.int32, (IN, 128), 0)
    cc = lax.broadcasted_iota(jnp.int32, (IN, 128), 1)
    fold = jnp.where((r // PW) == cc, 1.0, 0.0).astype(bf16)
    g_adt = exact_left(tri(False), exact_right(z, fold))
    direct = exact_right(x * dxd, fold)
    dt = kept_f[:, pl.ds(DT, N)]
    d_pre = (direct + heads[1:2] * g_adt) * kept_f[:, pl.ds(D_STEP, N)]
    decay_sum = jnp.sum(dt * g_adt, axis=0, keepdims=True)
    bias_sum = jnp.sum(d_pre, axis=0, keepdims=True)
    d_state = last * d_state + mm_tn(c, edy)
    dx = wide(STEP).astype(f32) * dxd + skip * dy
    g_pre = jnp.concatenate([dx, db, dc], 1) * wide(D_ACT, MIX).astype(f32)
    longer = jnp.concatenate([g_pre, after], 0)
    d_raw = 0.0
    tap_sums = []
    for k in range(4):
        d_raw = d_raw + taps[k : k + 1] * longer[3 - k : 3 - k + L]
        tap_sums.append(jnp.sum(g_pre * window[5 + k : 5 + k + L], axis=0, keepdims=True))
    tap_sums.append(jnp.sum(g_pre, axis=0, keepdims=True))
    g_all = jnp.concatenate([d_gates, d_raw.astype(bf16), d_pre.astype(bf16)], 1)
    sums = (jnp.concatenate(tap_sums, 0), gain_sum, skip_sum, decay_sum, bias_sum)
    return g_all, d_state, g_pre[:8], sums


class Place:
    def __init__(self):
        dp, mp = lax.axis_index("dp"), lax.axis_index("mp")
        self.dp, self.mp = dp, mp
        self.hi, self.x = mp // 4, mp % 4
        self.lo = 1 - self.hi
        self.ylo, self.z, self.core = dp // 8, (dp // 2) % 4, dp % 2
        self.other_core, self.other_ylo = 1 - self.core, 1 - self.ylo
        self.mine, self.theirs = self.hi * 4, self.lo * 4
        self.xs = [(self.x + k) % 4 for k in range(4)]
        self.row = [self.mine + x for x in self.xs]
        self.far_row = [self.theirs + x for x in self.xs]
        self.right, self.left = (dp, self.row[1]), (dp, self.row[3])
        self.across = (dp, self.far_row[0])
        self.mate = (dp + 1 - 2 * self.core, mp)
        self.beside_dp = self.at(1 - self.ylo, self.z)
        self.beside = (self.beside_dp, mp)
        self.zs = [(self.z + k) % 4 for k in range(4)]
        self.near_dp = [self.at(self.ylo, z) for z in self.zs]
        self.far_dp = [self.at(1 - self.ylo, z) for z in self.zs]
        self.near_slot = [self.ylo * 4 + z for z in self.zs]
        self.far_slot = [(1 - self.ylo) * 4 + z for z in self.zs]
        self.along = [(self.near_dp[k], mp) for k in (1, 2, 3)]
        self.z_gap = [(z + 3 - self.z) % 4 for z in range(4)]
        self.z_dp = [self.at(self.ylo, z) for z in range(4)]
        self.group = [(dp, (mp + k) % GROUP) for k in range(1, GROUP)]
        self.copies = [((dp + k) % DP, mp) for k in range(1, DP)]

    def at(self, ylo, z):
        return ylo * 8 + z * 2 + self.core


def greet(peers):
    barrier = pltpu.get_barrier_semaphore()
    for peer in peers:
        pl.semaphore_signal(barrier, inc=1, device_id=peer, device_id_type=MESH)
    return lambda: pl.semaphore_wait(barrier, len(peers))


class View:
    def __init__(self, ref, *chain):
        self.ref, self.chain = ref, chain

    @property
    def at(self):
        return Indexer(self)

    def build(self):
        ref = self.ref
        for index in self.chain:
            ref = ref.at[index]
        return ref

    def __getitem__(self, index):
        return self.build()[index]

    def __setitem__(self, index, value):
        self.build()[index] = value


class Indexer:
    def __init__(self, view):
        self.view = view

    def __getitem__(self, index):
        return View(self.view.ref, *self.view.chain, index)


class Copy:
    def __init__(self, book, make):
        self.book, self.make = book, make
        book.do(lambda: make().start())

    def wait(self):
        self.book.do(lambda: self.make().wait())

    def wait_recv(self):
        self.book.do(lambda: self.make().wait_recv())

    def wait_send(self):
        self.book.do(lambda: self.make().wait_send())


class Sender:
    def __init__(self, send_sem, recv_sem, local_sem):
        self.send_sem, self.recv_sem, self.local_sem = send_sem, recv_sem, local_sem
        self.count, self.started, self.locals, self.kept = 0, [], 0, None

    def do(self, action):
        if self.kept is None:
            action()
        else:
            self.kept.append(action)

    def reserve(self, count):
        self.count += count
        return self.count - count

    def record(self, plan):
        steps = []
        while True:
            self.kept = []
            more = next(plan, self) is not self
            if self.kept:
                steps.append(self.kept)
            if not more:
                self.kept = None
                return steps

    def __call__(self, source, target, peer):
        k = self.count
        self.count += 1
        copy = Copy(
            self,
            lambda: pltpu.make_async_remote_copy(
                src_ref=source.build(),
                dst_ref=target.build(),
                send_sem=self.send_sem.at[k],
                recv_sem=self.recv_sem.at[k],
                device_id=peer,
                device_id_type=MESH,
            ),
        )
        self.started.append(copy)
        return copy

    def local(self, source, target):
        k = self.locals
        self.locals += 1
        return Copy(
            self,
            lambda: pltpu.make_async_copy(source.build(), target.build(), self.local_sem.at[k]),
        )

    def settle(self, copies):
        for copy in copies:
            copy.wait_send()
        self.started = [copy for copy in self.started if copy not in copies]

    def drain(self):
        self.settle(self.started)


def run(actions):
    for action in actions:
        action()


class Table:
    def __init__(self):
        self.rows = {}

    def add(self, block, tick, actions):
        self.rows.setdefault((block, tick), []).extend(actions)

    def ticker(self, block):
        def tick(t):
            for k in range(BLOCKS):
                if (k, t) in self.rows:
                    pl.when(block == k)(lambda k=k: run(self.rows[(k, t)]))

        return tick


def gather_unit(send, place, buf, first, second):
    me, lx, rx, ox = place.row[0], place.row[3], place.row[1], place.row[2]
    ym, lxy, rxy = place.far_row[0], place.far_row[3], place.far_row[1]
    right, left, across = place.right, place.left, place.across
    half = PIECE // 2

    def go(block, slot, h, to):
        part = buf.at[block, slot, pl.ds(half * h, half)]
        return send(part, part, to)

    c = [go(second, me, 0, across), go(second, me, 1, across)]
    a = [go(first, me, 0, right), go(first, me, 1, left)]
    a += [go(first, me, 1, right), go(first, me, 0, left)]
    b = [go(second, me, 0, right), go(second, me, 1, left)]
    b += [go(second, me, 1, right), go(second, me, 0, left)]
    y = [go(first, me, 0, across), go(first, me, 1, across)]
    yield
    a[0].wait_recv()
    f = [go(first, lx, 0, right)]
    y.append(go(first, lx, 0, across))
    a[1].wait_recv()
    f.append(go(first, rx, 1, left))
    y.append(go(first, rx, 1, across))
    yield
    a[2].wait_recv()
    y.append(go(first, lx, 1, across))
    a[3].wait_recv()
    y.append(go(first, rx, 0, across))
    yield
    b[0].wait_recv()
    k = [go(second, lx, 0, right)]
    b[1].wait_recv()
    k.append(go(second, rx, 1, left))
    c[0].wait_recv()
    c[1].wait_recv()
    d = [go(second, ym, 0, right), go(second, ym, 1, left)]
    d += [go(second, ym, 1, right), go(second, ym, 0, left)]
    yield
    f[0].wait_recv()
    y.append(go(first, ox, 0, across))
    f[1].wait_recv()
    y.append(go(first, ox, 1, across))
    for copy in b[2:] + y[:2]:
        copy.wait_recv()
    yield
    d[0].wait_recv()
    e = [go(second, lxy, 0, right)]
    d[1].wait_recv()
    e.append(go(second, rxy, 1, left))
    yield
    for copy in d[2:] + k + e + y[2:]:
        copy.wait_recv()
    yield


def row_gather_unit(send, place, buf, first):
    me, lx, rx = place.xs[0], place.xs[3], place.xs[1]

    def go(block, slot, to):
        part = buf.at[block, slot]
        return send(part, part, to)

    a = [go(first, me, place.right), go(first + 1, me, place.left)]
    a += [go(first + 1, me, place.right), go(first, me, place.left)]
    yield
    a[0].wait_recv()
    f = [go(first, lx, place.right)]
    a[1].wait_recv()
    f.append(go(first + 1, rx, place.left))
    yield
    for copy in a[2:] + f:
        copy.wait_recv()
    yield


def weight_steps(send, place, buf):
    def go(slot, peer):
        return send(buf.at[slot], buf.at[slot], peer)

    own, other = place.dp, place.beside_dp
    one = go(own, place.beside)
    near = [go(own, peer) for peer in place.along]
    mates = [go(own, place.mate)]
    yield
    one.wait_recv()
    far = [go(other, peer) for peer in place.along]
    mates.append(go(other, place.mate))
    yield
    for k in range(3):
        near[k].wait_recv()
        mates.append(go(place.near_dp[3 - k], place.mate))
    yield
    for k in range(3):
        far[k].wait_recv()
        mates.append(go(place.far_dp[3 - k], place.mate))
    yield
    for copy in mates:
        copy.wait_recv()
    yield


def add_into(send, target, other):
    def action():
        target[...] = target[...] + other[...]

    send.do(action)


def put(send, target, index, value):
    def action():
        target[index] = value()

    send.do(action)


def scatter_unit(send, place, buf, first, second, y_in, x_in, xx_in, t_out, t_in, total):
    right, left, across = place.right, place.left, place.across
    half = PIECE // 2
    mine, theirs = place.row, place.far_row
    order = (2, 1, 3, 0)

    def first_hop(k, block, side):
        slot = side[2]
        return [
            send(buf.at[block, slot, pl.ds(0, half)], x_in.at[k, 0], right),
            send(buf.at[block, slot, pl.ds(half, half)], x_in.at[k, 1], left),
        ]

    def second_hop(k, block, side, hops):
        hops[0].wait_recv()
        add_into(send, buf.at[block, side[1], pl.ds(0, half)], x_in.at[k, 0])
        one = send(buf.at[block, side[1]], xx_in.at[k, 0], right)
        hops[1].wait_recv()
        add_into(send, buf.at[block, side[3], pl.ds(half, half)], x_in.at[k, 1])
        return [one, send(buf.at[block, side[3]], xx_in.at[k, 1], left)]

    def three(k, block, side):
        return (
            buf[block, side[0]].astype(f32) + xx_in[k, 0].astype(f32) + xx_in[k, 1].astype(f32)
        )

    ahead = [send(buf.at[first, theirs[n]], y_in.at[k], across) for k, n in enumerate(order)]
    hop_t = first_hop(1, second, theirs)
    hop_m = first_hop(2, second, mine)
    yield
    two_t = second_hop(1, second, theirs, hop_t)
    yield
    ahead[0].wait_recv()
    add_into(send, buf.at[first, mine[2]], y_in.at[0])
    hop_a = first_hop(0, first, mine)
    two_m = second_hop(2, second, mine, hop_m)
    yield
    for copy in two_t:
        copy.wait_recv()
    put(send, t_out, ..., lambda: three(1, second, theirs).astype(bf16))
    last = send(t_out, t_in, across)
    yield
    for k in range(1, 4):
        ahead[k].wait_recv()
        add_into(send, buf.at[first, mine[order[k]]], y_in.at[k])
    two_a = second_hop(0, first, mine, hop_a)
    yield
    for copy in two_m + [last]:
        copy.wait_recv()
    put(send, total, second, lambda: three(2, second, mine) + t_in[...].astype(f32))
    yield
    for copy in two_a:
        copy.wait_recv()
    put(send, total, first, lambda: three(0, first, mine))
    yield


def row_scatter_unit(send, place, buf, first, x_in, xx_in, keep):
    xs = place.xs
    hops = [
        send(buf.at[first, xs[2]], x_in.at[0], place.right),
        send(buf.at[first + 1, xs[2]], x_in.at[1], place.left),
    ]
    yield
    hops[0].wait_recv()
    add_into(send, buf.at[first, xs[1]], x_in.at[0])
    two = [send(buf.at[pl.ds(first, 2), xs[1]], xx_in.at[0], place.right)]
    hops[1].wait_recv()
    add_into(send, buf.at[first + 1, xs[3]], x_in.at[1])
    two.append(send(buf.at[pl.ds(first, 2), xs[3]], xx_in.at[1], place.left))
    yield
    for copy in two:
        copy.wait_recv()

    def last(k):
        total = buf[first + k, xs[0]].astype(f32)
        keep(first + k, total + xx_in[0, k].astype(f32) + xx_in[1, k].astype(f32))

    for k in range(2):
        send.do(lambda k=k: last(k))
    yield


class Reduction:
    def __init__(self, send, place, grads, core_in, z_in, y_out, w_in, keep):
        self.send, self.place, self.grads, self.core_in = send, place, grads, core_in
        self.z_in, self.y_out, self.w_in, self.keep = z_in, y_out, w_in, keep
        self.swaps, self.base = [], send.reserve(8)

    def swap(self, i):
        pairs = pl.ds(2 * i, 2)
        part = self.grads.at[pairs, self.place.other_core]
        self.swaps.append(self.send(part, self.core_in.at[pairs], self.place.mate))

    def hop(self, k, y, slot, peer):
        at = self.base + 2 * k + y
        return pltpu.make_async_remote_copy(
            src_ref=self.grads.at[slot, self.place.core].build(),
            dst_ref=self.z_in.at[k, y].build(),
            send_sem=self.send.send_sem.at[at],
            recv_sem=self.send.recv_sem.at[at],
            device_id=peer,
            device_id_type=MESH,
        )

    def fold(self, i):
        place = self.place
        self.swaps[i].wait_recv()
        for slot in (2 * i, 2 * i + 1):
            add_into(self.send, self.grads.at[slot, place.core], self.core_in.at[slot])
            y, z = slot // 4, slot % 4

            def action(slot=slot, y=y, z=z):
                k, peer = place.z_gap[z], (place.z_dp[z], place.mp)
                pl.when(place.z != z)(lambda: self.hop(k, y, slot, peer).start())

            self.send.do(action)

    def arrive(self, y):
        for k in range(3):
            self.send.do(lambda k=k: self.hop(k, y, 0, self.place.along[k]).wait_recv())

    def joined(self, y, slot):
        total = self.grads[slot, self.place.core].astype(f32)
        for k in range(3):
            total = total + self.z_in[k, y].astype(f32)
        return total

    def cross(self):
        y, slot = self.place.other_ylo, self.place.far_slot[0]
        self.arrive(y)
        put(self.send, self.y_out, ..., lambda: self.joined(y, slot).astype(bf16))
        self.crossed = self.send(self.y_out, self.w_in, self.place.beside)

    def end(self):
        y, slot = self.place.ylo, self.place.near_slot[0]
        self.arrive(y)
        self.crossed.wait_recv()
        self.send.do(lambda: self.keep(self.joined(y, slot) + self.w_in[...].astype(f32)))

    def settle(self):
        for k in range(3):
            for y in range(2):
                self.hop(k, y, 0, self.place.along[k]).wait_send()


def rows(block, count=L):
    return pl.ds(pl.multiple_of(block * count, count), count)


def pick(columns, block):
    lane = lax.broadcasted_iota(jnp.int32, columns.shape, 1)
    return jnp.sum(jnp.where(lane == block, columns, 0.0), axis=1, keepdims=True)


def parameters(channel_terms, side_terms, head_terms, taps, heads, skip, gain):
    taps[pl.ds(0, CONV + 1), pl.ds(0, IN)] = channel_terms[pl.ds(0, CONV + 1)]
    taps[pl.ds(0, CONV + 1), pl.ds(IN, 2 * N)] = side_terms[...]
    taps[pl.ds(CONV + 1, 3)] = jnp.zeros((3, MIX), f32)
    gain[...] = channel_terms[pl.ds(CONV + 1, 1)]
    wide = jnp.concatenate([head_terms[...], jnp.zeros((3, N - HD), f32)], 1)
    lane = lax.broadcasted_iota(jnp.int32, (1, N), 1)
    decay = jnp.where(lane < HD, -jnp.exp(wide[1:2]), 0.0)
    heads[...] = jnp.concatenate([wide[0:1], decay, jnp.zeros((6, N), f32)], 0)
    skip[...] = spread(jnp.broadcast_to(wide[2:3], (8, N)), low_lanes(8))[0:1]


def valid_rows(seq_len, place, block):
    row = lax.broadcasted_iota(jnp.int32, (PIECE, 1), 0)
    position = row + (place.mp * PIECE + block * L)
    return jnp.where(position < seq_len[...], 1.0, 0.0)


def front_kernel(
    tokens, grad_out, seq_len, norm_gain, main_weight, side_weight, output_weight,
    channel_terms, side_terms, head_terms,
    whole_o, weights_o, out_o, back_o, raw_o, kept_o, kept_f_o, kept_h_o, states_o, g_gated_o, gated_o, sums,
    whole, weights, out, back, raw, states, g_gated, gated, gates, steps, kept, kept_f, kept_h, mixed, halves,
    taps, heads, skip, gain, squares, state, inbox, send_sem, recv_sem, local_sem,
):
    (
        tokens, grad_out, seq_len, norm_gain, main_weight, side_weight, output_weight,
        channel_terms, side_terms, head_terms, whole_o, weights_o, out_o, back_o, raw_o,
        kept_o, kept_f_o, kept_h_o, states_o, g_gated_o, gated_o, sums, whole, weights, out,
        back, raw, states, g_gated, gated, gates, steps, kept, kept_f, kept_h, mixed,
        halves, taps, heads, skip, gain, squares, state, inbox,
    ) = map(
        View,
        (
            tokens, grad_out, seq_len, norm_gain, main_weight, side_weight, output_weight,
            channel_terms, side_terms, head_terms, whole_o, weights_o, out_o, back_o, raw_o,
            kept_o, kept_f_o, kept_h_o, states_o, g_gated_o, gated_o, sums, whole, weights, out,
            back, raw, states, g_gated, gated, gates, steps, kept, kept_f, kept_h, mixed,
            halves, taps, heads, skip, gain, squares, state, inbox,
        ),
    )
    place = Place()
    meet = greet(place.group + [place.mate, place.beside] + place.along)
    scale_row = norm_gain[...].reshape(1, D)
    for i in range(BLOCKS):
        x = tokens[i].astype(f32)
        scale = lax.rsqrt(jnp.mean(x * x, axis=1, keepdims=True) + epsilon)
        whole[i, place.mp] = (x * scale * scale_row).astype(bf16)
    columns = weights.at[place.dp]
    for k in range(2):
        columns[:, pl.ds(k * IN, IN)] = main_weight[:, k].astype(bf16)
    columns[:, pl.ds(2 * IN, 2 * N)] = side_weight[:, pl.ds(0, 2 * N)]
    source = lax.broadcasted_iota(jnp.int32, (HEADS, N), 0)
    lane = lax.broadcasted_iota(jnp.int32, (HEADS, N), 1)
    spot = jnp.where((source == lane + HD * place.mp) & (lane < HD), 1.0, 0.0).astype(bf16)
    own_steps = mm(side_weight[:, pl.ds(2 * N, HEADS)], spot)
    columns[:, pl.ds(2 * IN + 2 * N, N)] = own_steps.astype(bf16)
    out[place.dp, :, pl.ds(0, IN)] = output_weight[...]
    meet()
    send = Sender(send_sem, recv_sem, local_sem)
    units = [send.record(gather_unit(send, place, whole, 2 * u, 2 * u + 1)) for u in range(4)]
    cols = send.record(weight_steps(send, place, weights))
    outs = send.record(weight_steps(send, place, out))
    backs = [send.record(row_gather_unit(send, place, back, 2 * u)) for u in range(4)]

    run(cols[0])
    own_out = out.at[place.dp, :, pl.ds(0, IN)]
    pair = send(own_out, out.at[place.dp, :, pl.ds(IN, IN)], place.across)
    for unit in units:
        run(unit[0])
    for i in range(BLOCKS):
        rounded = valid_rows(seq_len, place, i) * grad_out[i].astype(f32)
        back[i, place.xs[0]] = rounded.astype(bf16)
    parameters(channel_terms, side_terms, head_terms, taps, heads, skip, gain)
    raw[pl.ds(0, 8)] = jnp.zeros((8, MIX), f32)
    state[...] = jnp.zeros((N, IN), f32)
    squares[...] = jnp.zeros((L, 128), f32)

    def project_rows(device, first=0, count=BLOCKS):
        block = whole[pl.ds(first, count), device].reshape(count * PIECE, D)
        both = mm(block, weights[...].reshape(D, COLS))
        for i in range(count):
            part = both[i * PIECE : (i + 1) * PIECE]
            start = (first + i) * L + device * PIECE
            at = pl.ds(pl.multiple_of(start, PIECE), PIECE)
            gates[at] = part[:, :IN]
            steps[at] = part[:, IN + MIX :]
            raw[pl.ds(pl.multiple_of(start + 8, 8), PIECE)] = part[:, IN : IN + MIX]

    far = (place.row[2], place.far_row[3], place.far_row[1], place.far_row[2])

    def early(k):
        run(units[0][k] + units[1][k])

    def late(k):
        run(units[2][k] + units[3][k])

    early(1)
    run(cols[1])
    early(2)
    late(1)
    pair.wait_recv()
    run(outs[0] + cols[2])
    early(3)
    late(2)
    for back_unit in backs:
        run(back_unit[0])
    run(cols[3])
    early(4)
    late(3)
    run(cols[4])
    project_rows(place.row[0])
    early(5)
    late(4)
    project_rows(place.row[3])
    run(outs[1])
    project_rows(place.row[1])
    early(6)
    late(5)
    project_rows(place.far_row[0])
    run(backs[0][1] + backs[1][1])
    for device in far:
        project_rows(device, 0, 4)
    stored = []

    def second_half():
        for device in far:
            project_rows(device, 4, 4)

    def store_early():
        stored.append(send.local(whole, whole_o))
        stored.append(send.local(weights, weights_o))
        yield

    lane = lax.broadcasted_iota(jnp.int32, (L, 128), 1)
    crossing = [None] * 4

    def project(u):
        pairs = pl.ds(2 * u, 2)

        def action():
            both = mm(back[pairs].reshape(L, D), out[...].reshape(D, 2 * IN)).astype(bf16)
            g_gated[pairs, place.hi] = both[:, :IN].reshape(2, L // 2, IN)
            halves[pairs] = both[:, IN:].reshape(2, L // 2, IN)

        send.do(action)
        crossing[u] = send(halves.at[pairs], g_gated.at[pairs, place.hi], place.across)
        yield

    projections = [send.record(project(u))[0] for u in range(4)]
    def store_out():
        stored.append(send.local(out, out_o))
        yield

    table = Table()
    for block, tick, actions in (
        (0, 2, backs[2][1] + backs[3][1] + outs[2]),
        (0, 5, units[2][6]),
        (1, 3, units[3][6] + outs[3]),
        (2, 3, outs[4]),
        (2, 5, backs[0][2] + projections[0]),
        (3, 5, [second_half] + send.record(store_early())[0]),
        (4, 2, backs[1][2] + projections[1]),
        (5, 2, send.record(store_out())[0]),
        (6, 2, backs[2][2] + projections[2]),
    ):
        table.add(block, tick, actions)

    def block_copies(i):
        slot = lax.rem(i, 2)
        below = pl.ds(pl.multiple_of(i * L + 8, 8), L)
        pairs = [
            (raw.at[below], raw_o.at[below]),
            (kept.at[slot], kept_o.at[i]),
            (kept_f.at[slot], kept_f_o.at[i]),
            (kept_h.at[slot], kept_h_o.at[i]),
            (states.at[i], states_o.at[i]),
        ]
        return [
            pltpu.make_async_copy(source.build(), target.build(), local_sem.at[16 + 5 * slot + k])
            for k, (source, target) in enumerate(pairs)
        ]

    def block_wait(i):
        for copy in block_copies(i):
            copy.wait()

    def body(i, carry):
        tick = table.ticker(i)
        at = rows(i)
        slot = lax.rem(i, 2)
        pl.when(i >= 2)(lambda: block_wait(i - 2))
        states[i] = state[...]
        window = raw[pl.ds(pl.multiple_of(i * L, 8), L + 8)]
        outer, following = fwd_block(
            window, gates[at], steps[at], taps[...], heads[...], skip[...], state[...], tick,
            kept.at[slot], kept_f.at[slot], kept_h.at[slot],
        )
        mixed[at] = outer
        state[...] = following
        square = jnp.sum(outer * outer, axis=1, keepdims=True)
        squares[...] = jnp.where(lane == i, square, squares[...])
        for copy in block_copies(i):
            copy.start()
        tick(5)
        return carry

    lax.fori_loop(0, BLOCKS, body, 0)
    inbox[place.mp] = squares[...].T[:8]
    copies = [send(inbox.at[place.mp], inbox.at[place.mp], peer) for peer in place.group]
    stored.append(send.local(raw.at[pl.ds(0, 8)], raw_o.at[pl.ds(0, 8)]))
    run(backs[3][2] + projections[3])
    stored.append(send.local(back, back_o))
    for copy in copies:
        copy.wait_recv()
    total = inbox[0]
    for k in range(1, GROUP):
        total = total + inbox[k]
    top = lax.rsqrt(total * (1.0 / INNER) + epsilon)
    scales = jnp.concatenate([top, jnp.zeros((120, L), f32)], 0).T
    for i in range(BLOCKS):
        rounded = (mixed[pl.ds(i * L, L)] * scales[:, i : i + 1] * gain[...]).astype(bf16)
        gated[i] = rounded.reshape(2, L // 2, IN)
    stored.append(send.local(gated, gated_o))
    for u in range(4):
        crossing[u].wait_recv()
        for i in (2 * u, 2 * u + 1):
            part = g_gated[i].reshape(L, IN).astype(f32) * gain[...] * mixed[pl.ds(i * L, L)]
            product = jnp.sum(part, axis=1, keepdims=True)
            scales = jnp.where(lane == i + 8, product, scales)
    sums[...] = scales
    stored.append(send.local(g_gated, g_gated_o))
    for copy in stored:
        copy.wait()

    block_wait(jnp.int32(BLOCKS - 2))
    block_wait(jnp.int32(BLOCKS - 1))
    send.drain()


def back_kernel(
    whole_i, weights_i, out_i, back_i, raw_i, kept_i, kept_f_i, kept_h_i, states_i, g_gated_i, gated_i,
    sums, tokens, grad_out, seq_len, norm_gain, channel_terms, side_terms, head_terms,
    layer_out, token_grad, gain_grad, main_grad, side_grad, out_grad, conv_grad, channel_grad, head_grad,
    weights, out, gated, raw, kept, kept_f, kept_h, states, g_gated, g_all, left,
    row_parts, row_x, row_xx, parts, y_in, x_in, xx_in, t_out, t_in,
    grads, core_in, z_in, y_out, w_in, s_core, s_z, s_out, s_in, o_core, o_z, o_out, o_in, pair_out, pair_in,
    taps, heads, skip, gain, columns, totals, d_state, after, gain_part,
    products_box, share_box, side_box, sums_box, gain_box, gain_all, send_sem, recv_sem, local_sem,
):
    (
        whole_i, weights_i, out_i, back_i, raw_i, kept_i, kept_f_i, kept_h_i, states_i,
        g_gated_i, gated_i, sums, tokens, grad_out, seq_len, norm_gain, channel_terms,
        side_terms, head_terms, layer_out, token_grad, gain_grad, main_grad, side_grad,
        out_grad, conv_grad, channel_grad, head_grad, weights, out, gated, raw, kept,
        kept_f, kept_h, states, g_gated, g_all, left, row_parts, row_x, row_xx, parts, y_in,
        x_in, xx_in, t_out, t_in, grads, core_in, z_in, y_out, w_in, s_core, s_z, s_out,
        s_in, o_core, o_z, o_out, o_in, pair_out, pair_in, taps, heads, skip, gain, columns,
        totals, d_state, after, gain_part, products_box, share_box, side_box, sums_box,
        gain_box, gain_all,
    ) = map(
        View,
        (
            whole_i, weights_i, out_i, back_i, raw_i, kept_i, kept_f_i, kept_h_i, states_i,
            g_gated_i, gated_i, sums, tokens, grad_out, seq_len, norm_gain, channel_terms,
            side_terms, head_terms, layer_out, token_grad, gain_grad, main_grad, side_grad,
            out_grad, conv_grad, channel_grad, head_grad, weights, out, gated, raw, kept,
            kept_f, kept_h, states, g_gated, g_all, left, row_parts, row_x, row_xx, parts, y_in,
            x_in, xx_in, t_out, t_in, grads, core_in, z_in, y_out, w_in, s_core, s_z, s_out,
            s_in, o_core, o_z, o_out, o_in, pair_out, pair_in, taps, heads, skip, gain, columns,
            totals, d_state, after, gain_part, products_box, share_box, side_box, sums_box,
            gain_box, gain_all,
        ),
    )
    place = Place()
    meet = greet(place.group + place.copies)
    send = Sender(send_sem, recv_sem, local_sem)

    def loads(i, slot):
        return [
            (raw_i.at[pl.ds(pl.multiple_of(i * L, 8), L + 8)], raw.at[slot]),
            (kept_i.at[i], kept.at[slot]),
            (kept_f_i.at[i], kept_f.at[slot]),
            (kept_h_i.at[i], kept_h.at[slot]),
            (states_i.at[i], states.at[slot]),
            (g_gated_i.at[i], g_gated.at[slot]),
        ]

    def load(i, slot, start):
        for k, (source, target) in enumerate(loads(i, slot)):
            copy = pltpu.make_async_copy(
                source.build(), target.build(), local_sem.at[16 + 6 * slot + k]
            )
            if start:
                copy.start()
            else:
                copy.wait()

    load(BLOCKS - 1, 1, True)
    first = [
        send.local(gated_i.at[:, place.hi], gated.at[:, :, pl.ds(0, IN)]),
        send.local(out_i, out),
        send.local(weights_i, weights),
    ]
    load(BLOCKS - 2, 0, True)
    products_box[place.mp] = sums[...].T[8:16]
    meet()
    shares = [
        send(products_box.at[place.mp], products_box.at[place.mp], peer) for peer in place.group
    ]
    crossing = [
        send(
            gated_i.at[pl.ds(2 * u, 2), place.lo],
            gated.at[pl.ds(2 * u, 2), :, pl.ds(IN, IN)],
            place.across,
        )
        for u in (3, 2, 1, 0)
    ][::-1]
    parameters(channel_terms, side_terms, head_terms, taps, heads, skip, gain)
    d_state[...] = jnp.zeros((N, IN), f32)
    after[...] = jnp.zeros((8, MIX), f32)
    totals[...] = jnp.zeros((8, MIX), f32)
    gain_part[...] = jnp.zeros((1, D), f32)
    for copy in shares:
        copy.wait_recv()
    total = products_box[0]
    for k in range(1, GROUP):
        total = total + products_box[k]
    summed = jnp.concatenate([jnp.zeros((8, L), f32), total, jnp.zeros((112, L), f32)], 0).T
    lane = lax.broadcasted_iota(jnp.int32, (L, 128), 1)
    columns[...] = jnp.where(lane < 8, sums[...], summed)
    for copy in first:
        copy.wait()

    def keep_layer(i, total):
        layer_out[i] = (
            tokens[i].astype(f32) + valid_rows(seq_len, place, i) * total
        ).astype(bf16)

    def row_plan(u):
        def action():
            pairs = pl.ds(2 * u, 2)
            part = mm_nt(gated[pairs].reshape(L, 2 * IN), out[...].reshape(D, 2 * IN))
            row_parts[pairs] = part.astype(bf16).reshape(2, 4, PIECE, D)

        crossing[u].wait_recv()
        yield
        send.do(action)
        yield from row_scatter_unit(
            send, place, row_parts, 2 * u, row_x.at[u], row_xx.at[u], keep_layer
        )

    def keep_out(total):
        pair_out[...] = total[:, IN:]
        out_grad[...] = total[:, :IN]

    def keep_main(total):
        main_grad[:, 0] = total[:, :IN]
        main_grad[:, 1] = total[:, IN:]

    def keep_side(total):
        turned = total[:, 2 * N :].T[:16]
        blank = jnp.zeros((16, 2 * N - D // DP), f32)
        side_box[place.mp, pl.ds(0, D // DP)] = total[:, : 2 * N].astype(bf16)
        side_box[place.mp, pl.ds(D // DP, 16)] = jnp.concatenate([turned, blank], 1).astype(bf16)

    main_part = grads.at[:, :, :, pl.ds(0, 2 * IN)]
    side_part = grads.at[:, :, :, pl.ds(2 * IN, 3 * N)]
    out_sum = Reduction(send, place, main_part, o_core, o_z, o_out, o_in, keep_out)
    main_sum = Reduction(send, place, main_part, core_in, z_in, y_out, w_in, keep_main)
    side_sum = Reduction(send, place, side_part, s_core, s_z, s_out, s_in, keep_side)

    def out_plan():
        chunks = [
            send.local(
                back_i.at[:, :, :, pl.ds(i * 384, 384)], left.at[i, :, pl.ds(0, 4)]
            )
            for i in range(2)
        ]
        yield
        for i in range(4):
            chunks[i].wait()

            def action(i=i):
                side = left[i % 2, :, pl.ds(0, 4)].reshape(BLOCKS * L // 2, 384)
                pairs = pl.ds(2 * i, 2)
                part = mm_tn(side, gated[...].reshape(BLOCKS * L // 2, 2 * IN))
                grads[pairs, :, :, : 2 * IN] = part.astype(bf16).reshape(2, 2, 96, 2 * IN)

            send.do(action)
            if i < 2:
                chunks.append(
                    send.local(
                        back_i.at[:, :, :, pl.ds((i + 2) * 384, 384)],
                        left.at[i, :, pl.ds(0, 4)],
                    )
                )
            out_sum.swap(i)
            if i == 3:
                whole_loads.append(load_whole(0))
                whole_loads.append(load_whole(1))
            yield
        for i in range(4):
            out_sum.fold(i)
        yield
        out_sum.cross()
        yield
        out_sum.end()
        pair = send(pair_out, pair_in, place.across)
        yield
        pair.wait_recv()

        def finish():
            out_grad[...] += pair_in[...]

        send.do(finish)
        yield

    whole_loads = []

    def load_whole(i):
        return send.local(whole_i.at[:, :, :, pl.ds(i * 384, 384)], left.at[i % 2])

    row_units = [send.record(row_plan(u)) for u in range(4)]
    outs = send.record(out_plan())

    def final_rows(i):
        gain_row = norm_gain[...].reshape(1, D)
        x = tokens[i].astype(f32)
        s = lax.rsqrt(jnp.mean(x * x, axis=1, keepdims=True) + epsilon)
        g = token_grad[i]
        dot = jnp.sum(g * gain_row * x, axis=1, keepdims=True)
        token_grad[i] = grad_out[i].astype(f32) + s * gain_row * g - x * (s * s * s * dot * (1.0 / D))
        gain_part[...] += jnp.sum(g * x * s, axis=0, keepdims=True)

    units = [
        send.record(
            scatter_unit(
                send, place, parts, 2 * u, 2 * u + 1,
                y_in.at[u], x_in.at[u], xx_in.at[u], t_out.at[u], t_in.at[u], token_grad,
            )
        )
        for u in range(4)
    ]
    for u in range(4):
        units[u][6] += [lambda i=2 * u + k: final_rows(i) for k in range(2)]

    table = Table()
    for block, tick, actions in (
        (0, 0, row_units[3][0]),
        (0, 0, row_units[3][1]),
        (0, 6, row_units[2][0]),
        (0, 6, row_units[2][1]),
        (1, 4, row_units[3][2]),
        (1, 6, units[3][0]),
        (1, 6, outs[0]),
        (2, 2, row_units[1][0]),
        (2, 2, row_units[0][0]),
        (2, 4, outs[1]),
        (2, 4, row_units[2][2]),
        (2, 6, outs[2]),
        (3, 2, outs[3]),
        (3, 4, units[3][1]),
        (3, 4, row_units[3][3]),
        (3, 5, units[3][2]),
        (3, 5, outs[4]),
        (3, 6, units[2][0]),
        (4, 0, row_units[2][3]),
        (4, 2, units[3][3]),
        (4, 2, outs[5]),
        (4, 6, units[3][4]),
        (4, 6, row_units[1][1]),
        (5, 4, units[2][1]),
        (5, 5, units[2][2]),
        (5, 6, units[3][5]),
        (5, 6, units[1][0]),
        (6, 0, units[2][3]),
        (6, 0, row_units[1][2]),
        (6, 5, units[3][6]),
        (6, 5, row_units[0][1]),
        (6, 6, units[2][4]),
        (6, 6, outs[6]),
        (7, 4, units[1][1]),
        (7, 5, units[1][2]),
        (7, 5, outs[7]),
        (7, 6, units[2][5]),
        (7, 6, units[0][0]),
    ):
        table.add(block, tick, actions)

    def body(j, carry):
        tick = table.ticker(j)
        i = BLOCKS - 1 - j
        slot = lax.rem(i, 2)
        tick(0)
        load(i, slot, False)
        g, ds, top, found = bwd_block(
            raw[slot], kept.at[slot], kept_f.at[slot], kept_h.at[slot],
            taps[...], heads[...], skip[...], gain[...],
            states[slot], pick(columns[...], i), pick(columns[...], i + 8),
            g_gated[slot].reshape(L, IN).astype(f32), d_state[...], after[...], tick,
        )
        pl.when(i >= 2)(lambda: load(i - 2, slot, True))
        g_all[rows(i)] = g
        d_state[...] = ds
        after[...] = top
        tap_sums, gain_sum, skip_sum, decay_sum, bias_sum = found
        blank = jnp.zeros((1, MIX - IN), f32)
        fill = jnp.zeros((1, MIX - 2 * N), f32)
        totals[...] += jnp.concatenate(
            [
                tap_sums,
                jnp.concatenate([gain_sum, blank], 1),
                jnp.concatenate([skip_sum, blank], 1),
                jnp.concatenate([decay_sum, bias_sum, fill], 1),
            ],
            0,
        )
        tick(5)
        part = mm_nt(g, weights[...].reshape(D, COLS))
        parts[i] = part.astype(bf16).reshape(GROUP, PIECE, D)
        tick(6)
        return carry

    lax.fori_loop(0, BLOCKS, body, 0)

    sums_box[place.dp] = totals[...]
    early = [send(sums_box.at[place.dp], sums_box.at[place.dp], peer) for peer in place.copies]
    send.settle(out_sum.swaps)
    out_sum.settle()
    late = [
        units[1][3] + row_units[0][2] + units[2][6],
        units[0][1] + units[0][2] + row_units[1][3],
        units[1][4] + units[0][3],
        units[1][5],
        units[0][4] + units[1][6],
        units[0][5] + units[0][6],
        row_units[0][3],
    ]
    for i in range(4):
        whole_loads[i].wait()
        side = left[i % 2].reshape(BLOCKS * L, 384)
        pairs = pl.ds(2 * i, 2)
        grads[pairs] = mm_tn(side, g_all[...]).astype(bf16).reshape(2, 2, 96, COLS)
        if i < 2:
            whole_loads.append(load_whole(i + 2))
        side_sum.swap(i)
        main_sum.swap(i)
        if i:
            side_sum.fold(i - 1)
            main_sum.fold(i - 1)
        run(late[i])
    side_sum.fold(3)
    main_sum.fold(3)
    run(outs[8])
    run(late[4])
    for copy in early:
        copy.wait_recv()
    copied = sums_box[0]
    for k in range(1, DP):
        copied = copied + sums_box[k]
    share_box[place.mp] = copied[:, IN:]
    shares = [send(share_box.at[place.mp], share_box.at[place.mp], peer) for peer in place.group]
    channel_grad[...] = copied[: CONV + 2, :IN]
    r = lax.broadcasted_iota(jnp.int32, (IN, N), 0)
    c = lax.broadcasted_iota(jnp.int32, (IN, N), 1)
    fold = jnp.where((r // PW) == c, 1.0, 0.0).astype(bf16)
    skips = exact_right(jnp.broadcast_to(copied[CONV + 2 : CONV + 3, :IN], (8, IN)), fold)
    decays = heads[pl.ds(1, 1)] * copied[CONV + 3 :, :N]
    biases = copied[CONV + 3 :, N : 2 * N]
    head_grad[...] = jnp.concatenate([biases, decays, skips[0:1]], 0)[:, :HD]
    side_sum.cross()
    run(late[5])

    gain_sum = gain_part[...]
    pieces = [gain_sum[:, k * 128 : (k + 1) * 128] for k in range(D // 128)]
    gain_box[place.mp] = jnp.concatenate(pieces + [jnp.zeros((4, 128), f32)], 0)
    gains = [send(gain_box.at[place.mp], gain_box.at[place.mp], peer) for peer in place.group]
    for copy in shares:
        copy.wait_recv()
    shared = share_box[0]
    for k in range(1, GROUP):
        shared = shared + share_box[k]
    conv_grad[...] = shared[: CONV + 1]
    for copy in gains:
        copy.wait_recv()
    total = gain_box[0]
    for k in range(1, GROUP):
        total = total + gain_box[k]
    gain_all[place.dp] = total
    ends = [send(gain_all.at[place.dp], gain_all.at[place.dp], peer) for peer in place.copies]
    side_sum.end()
    sides = [send(side_box.at[place.mp], side_box.at[place.mp], peer) for peer in place.group]
    main_sum.cross()
    run(late[6])
    main_sum.end()
    for copy in sides:
        copy.wait_recv()
    both, steps_sum = 0.0, 0.0
    lane = lax.broadcasted_iota(jnp.int32, (16, N), 1)
    source = lax.broadcasted_iota(jnp.int32, (16, N), 0)
    for k in range(GROUP):
        both = both + side_box[k, pl.ds(0, D // DP)].astype(f32)
        spot = jnp.where((lane == source + HD * k) & (source < HD), 1.0, 0.0).astype(bf16)
        turned = side_box[k, pl.ds(D // DP, 16), pl.ds(0, N)]
        steps_sum = steps_sum + mm_tn(turned, spot)[: D // DP]
    side_grad[...] = jnp.concatenate([both, steps_sum], 1)[:, : 2 * N + HEADS]
    for copy in ends:
        copy.wait_recv()
    total = gain_all[0]
    for k in range(1, DP):
        total = total + gain_all[k]
    for k in range(D // 128):
        gain_grad[pl.ds(k * 128, 128)] = total[k]
    send.drain()
    main_sum.settle()
    side_sum.settle()


def call(kernel, outs, scratch, sems, collective, args, flops):
    vmem, anywhere = pltpu.VMEM, pl.ANY
    spec = {True: pl.BlockSpec(memory_space=anywhere), False: pl.BlockSpec(memory_space=vmem)}
    return pl.pallas_call(
        kernel,
        out_shape=[jax.ShapeDtypeStruct(shape, dtype) for shape, dtype, _ in outs],
        in_specs=[spec[far] for _, far in args],
        out_specs=[spec[far] for _, _, far in outs],
        scratch_shapes=[pltpu.VMEM(shape, dtype) for shape, dtype in scratch]
        + [pltpu.SemaphoreType.DMA((k,)) for k in sems],
        compiler_params=pltpu.CompilerParams(
            collective_id=collective, has_side_effects=True, vmem_limit_bytes=VMEM_BYTES
        ),
        cost_estimate=pl.CostEstimate(
            flops=flops,
            bytes_accessed=sum(a.size * a.dtype.itemsize for a, _ in args),
            transcendentals=0,
        ),
        name=kernel.__name__,
    )(*[a for a, _ in args])


def deliver_kernel(*refs):
    count = (len(refs) - 2) // 3
    ins, outs, held = refs[:count], refs[count : 2 * count], refs[2 * count : 3 * count]
    sems = refs[-2:]
    copies = [
        [
            pltpu.make_async_copy(source, middle, sems[0].at[k]),
            pltpu.make_async_copy(middle, target, sems[1].at[k]),
        ]
        for k, (source, middle, target) in enumerate(zip(ins, held, outs))
    ]
    for copy, _ in copies:
        copy.start()
    for first, second in copies:
        first.wait()
        second.start()
    for _, copy in copies:
        copy.wait()


def deliver(arrays):
    anywhere = pl.BlockSpec(memory_space=pl.ANY)
    return pl.pallas_call(
        deliver_kernel,
        out_shape=[jax.ShapeDtypeStruct(a.shape, a.dtype) for a in arrays],
        in_specs=[anywhere] * len(arrays),
        out_specs=[anywhere] * len(arrays),
        scratch_shapes=[pltpu.VMEM(a.shape, a.dtype) for a in arrays]
        + [pltpu.SemaphoreType.DMA((len(arrays),))] * 2,
        compiler_params=pltpu.CompilerParams(vmem_limit_bytes=VMEM_BYTES),
        name="deliver_kernel",
    )(*arrays)


def on_device(
    tokens,
    seq_len,
    norm_gain,
    main_weight,
    side_weight,
    side_terms,
    channel_terms,
    head_terms,
    output_weight,
    cotangent,
):
    count, span = BLOCKS * L, D // DP
    saved = [
        ((BLOCKS, GROUP, PIECE, D), bf16),
        ((DP, span, COLS), bf16),
        ((DP, span, 2 * IN), bf16),
        ((BLOCKS, 4, PIECE, D), bf16),
        ((count + 8, MIX), f32),
        ((BLOCKS, L, KEPT), bf16),
        ((BLOCKS, L, KEPT_F), f32),
        ((BLOCKS, 2 * HD, IN, N), bf16),
        ((BLOCKS, N, IN), f32),
        ((BLOCKS, 2, L // 2, IN), bf16),
        ((BLOCKS, 2, L // 2, IN), bf16),
    ]
    terms = [((8, MIX), f32), ((8, N), f32), ((1, IN), f32), ((1, IN), f32)]
    blocks = [((2, L, KEPT), bf16), ((2, L, KEPT_F), f32), ((2, 2 * HD, IN, N), bf16)]
    scratch = saved[:5] + saved[8:] + [((count, IN), f32), ((count, N), f32)] + blocks
    scratch += [((count, IN), f32), ((BLOCKS, L // 2, IN), bf16)] + terms
    scratch += [((L, 128), f32), ((N, IN), f32), ((GROUP, 8, L), f32)]
    own = [tokens[0], cotangent[0], seq_len.reshape(1, 1), norm_gain]
    weights = [main_weight, side_weight, output_weight.T]
    small = [channel_terms, side_terms, head_terms]
    *passed, sums = call(
        front_kernel,
        [(shape, dtype, True) for shape, dtype in saved] + [((L, 128), f32, False)],
        scratch,
        (192, 192, 28),
        0,
        [(a, False) for a in own + weights + small],
        12 * 10**9,
    )
    outs = call(
        back_kernel,
        [
            ((BLOCKS, PIECE, D), bf16, False),
            ((BLOCKS, PIECE, D), f32, False),
            ((D,), f32, False),
            ((span, 2, IN), f32, False),
            ((span, 2 * N + HEADS), f32, False),
            ((span, IN), f32, False),
            ((CONV + 1, 2 * N), f32, False),
            ((CONV + 2, IN), f32, False),
            ((3, HD), f32, False),
        ],
        [
            ((DP, span, COLS), bf16),
            ((DP, span, 2 * IN), bf16),
            ((BLOCKS, L // 2, 2 * IN), bf16),
            ((2, L + 8, MIX), f32),
            *blocks,
            ((2, N, IN), f32),
            ((2, 2, L // 2, IN), bf16),
            ((count, COLS), bf16),
            ((2, BLOCKS, GROUP, PIECE, 384), bf16),
            ((BLOCKS, 4, PIECE, D), bf16),
            ((4, 2, PIECE, D), bf16),
            ((4, 2, 2, PIECE, D), bf16),
            ((BLOCKS, GROUP, PIECE, D), bf16),
            ((4, 4, PIECE, D), bf16),
            ((4, 3, 2, PIECE // 2, D), bf16),
            ((4, 3, 2, PIECE, D), bf16),
            ((4, PIECE, D), bf16),
            ((4, PIECE, D), bf16),
            ((8, 2, span, COLS), bf16),
        ]
        + [
            shape
            for width in (2 * IN, 3 * N, 2 * IN)
            for shape in (
                ((8, span, width), bf16),
                ((3, 2, span, width), bf16),
                ((span, width), bf16),
                ((span, width), bf16),
            )
        ]
        + [((span, IN), f32), ((span, IN), f32)]
        + terms
        + [
            ((L, 128), f32),
            ((8, MIX), f32),
            ((N, IN), f32),
            ((8, MIX), f32),
            ((1, D), f32),
            ((GROUP, 8, L), f32),
            ((GROUP, 8, 2 * N), f32),
            ((GROUP, span + 16, 2 * N), bf16),
            ((DP, 8, MIX), f32),
            ((GROUP, 16, 128), f32),
            ((DP, 16, 128), f32),
        ],
        (256, 256, 28),
        1,
        [(a, True) for a in passed] + [(a, False) for a in [sums] + own + small],
        24 * 10**9,
    )
    layer_out, token_grad, gain_grad, main_grad, side_grad, out_grad, *rest = deliver(outs)
    return (
        layer_out[None],
        token_grad[None],
        gain_grad,
        main_grad,
        side_grad,
        *rest,
        out_grad.T,
    )


def solution(mesh):
    placed = (
        P("dp", None, "mp", None),
        P("dp"),
        P(),
        P("dp", None, "mp"),
        P("dp", None),
        P(),
        P(None, "mp"),
        P(None, "mp"),
        P("mp", "dp"),
        P("dp", None, "mp", None),
    )
    return jax.shard_map(
        on_device,
        mesh=mesh,
        in_specs=placed,
        out_specs=(
            P("dp", None, "mp", None),
            P("dp", None, "mp", None),
            P(),
            P("dp", None, "mp"),
            P("dp", None),
            P(),
            P(None, "mp"),
            P(None, "mp"),
            P("mp", "dp"),
        ),
        check_vma=False,
    )
```

```python
import functools

import jax
import jax.numpy as jnp
from jax import lax
from jax.experimental import pallas as pl
from jax.experimental.pallas import tpu as pltpu
from jax.sharding import PartitionSpec as P

f32, bf16 = jnp.float32, jnp.bfloat16
CONV, D, INNER = 4, 1536, 3072
L, N, PW, IN, HD = 256, 128, 64, 384, 6
BLOCKS, GROUP, PIECE, DP, HEADS = 8, 8, 32, 16, 48
COLS = 2 * IN + 3 * N
MIX = IN + 2 * N
MESH = pl.DeviceIdType.MESH
VMEM_BYTES = 63 * 2**20
epsilon = 1e-05
NEG = -1e30

def mm(a, b):
    return lax.dot_general(a, b, (((1,), (0,)), ((), ())), preferred_element_type=f32)
def mm_nt(a, b):
    return lax.dot_general(a, b, (((1,), (1,)), ((), ())), preferred_element_type=f32)
def mm_tn(a, b):
    return lax.dot_general(a, b, (((0,), (0,)), ((), ())), preferred_element_type=f32)

def thirds(x):
    hi = x.astype(bf16)
    rest = x - hi.astype(f32)
    mid = rest.astype(bf16)
    return hi, mid, (rest - mid.astype(f32)).astype(bf16)

def exact_left(mask, x):
    a, b, c = thirds(x)
    return mm(mask, a) + mm(mask, b) + mm(mask, c)

def exact_right(x, mask):
    a, b, c = thirds(x)
    return mm(a, mask) + mm(b, mask) + mm(c, mask)

def sigmoid(x):
    return 1.0 / (1.0 + jnp.exp(-x))

def softplus(x):
    return jnp.maximum(x, 0.0) + jnp.log1p(jnp.exp(-jnp.abs(x)))

def tri(lower):
    r = lax.broadcasted_iota(jnp.int32, (L, L), 0)
    c = lax.broadcasted_iota(jnp.int32, (L, L), 1)
    return jnp.where((r >= c) if lower else (r <= c), 1.0, 0.0).astype(bf16)

def spread(cols, low):
    out = []
    for j in range(3):
        a = jnp.broadcast_to(cols[:, 2 * j : 2 * j + 1], (cols.shape[0], 128))
        b = jnp.broadcast_to(cols[:, 2 * j + 1 : 2 * j + 2], (cols.shape[0], 128))
        out.append(jnp.where(low, a, b))
    return jnp.concatenate(out, 1)

def conv_pre(window, taps):
    total = taps[4:5]
    for k in range(4):
        total = total + taps[k : k + 1] * window[5 + k : 5 + k + L]
    return total

def low_lanes(rows):
    return lax.broadcasted_iota(jnp.int32, (rows, 128), 1) < 64

def head_quantities(dt_raw, heads):
    pre = dt_raw + heads[0:1]
    dt = softplus(pre)
    logs = exact_left(tri(True), dt * heads[1:2])
    return pre, dt, logs

def half_mask(t):
    rows = 128
    r = lax.broadcasted_iota(jnp.int32, (rows, 128 * (t + 1)), 0) + 128 * t
    c = lax.broadcasted_iota(jnp.int32, (rows, 128 * (t + 1)), 1)
    return r >= c

def weights_of(logs, logs_t, h, t):
    w = 128 * (t + 1)
    col = jnp.broadcast_to(logs[128 * t : 128 * (t + 1), h : h + 1], (128, 128))
    if t:
        col = jnp.concatenate([col, col], 1)
    gap = col - logs_t[h : h + 1, :w]
    return jnp.exp(jnp.where(half_mask(t), gap, NEG))

X, GATE, D_GATE, XD, TXD, GROW, TAIL, STEP = (IN * k for k in range(8))
KEYS = 8 * IN
D_ACT = KEYS + 2 * N
KEPT = D_ACT + MIX
SCAN, DT, D_STEP, KEPT_F = 0, IN, IN + N, IN + 2 * N


def fwd_block(window, gates, dt_raw, taps, heads, skip, state, tick, kept, kept_f, kept_h):
    low = low_lanes(L)
    total = conv_pre(window, taps)
    sig = sigmoid(total)
    act = total * sig
    kept[:, pl.ds(D_ACT, MIX)] = (sig + act * (1.0 - sig)).astype(bf16)
    x, keys = act[:, :IN], act[:, IN:].astype(bf16)
    kept[:, pl.ds(X, IN)] = x.astype(bf16)
    kept[:, pl.ds(KEYS, 2 * N)] = keys
    b, c = keys[:, :N], keys[:, N:]
    pre, dt, logs = head_quantities(dt_raw, heads)
    kept_f[:, pl.ds(DT, N)] = dt
    kept_f[:, pl.ds(D_STEP, N)] = sigmoid(pre)
    logs_t = logs.T
    dt_l, logs_l = spread(dt, low), spread(logs, low)
    xd = (dt_l * x).astype(bf16)
    kept[:, pl.ds(STEP, IN)] = dt_l.astype(bf16)
    kept[:, pl.ds(XD, IN)] = xd
    g = mm_nt(c, b)
    rows = [[], []]
    zero = jnp.zeros((), bf16)
    for j in range(3):
        tick(2 + j)
        pair = xd[:, 128 * j : 128 * (j + 1)]
        own = (jnp.where(low, pair, zero), jnp.where(low, zero, pair))
        for t in range(2):
            w = 128 * (t + 1)
            total_y = 0.0
            for e in range(2):
                h = 2 * j + e
                wt = weights_of(logs, logs_t, h, t)
                m = wt * g[128 * t : 128 * (t + 1), :w]
                total_y = total_y + mm(m.astype(bf16), own[e][:w])
                kept_h[h, pl.ds(128 * t, w)] = m.T.astype(bf16)
                for k in range(t + 1):
                    piece = wt[:, 128 * k : 128 * (k + 1)]
                    kept_h[HD + h, pl.ds(128 * (t + k), 128)] = piece.astype(bf16)
            rows[t].append(total_y)
    intra = jnp.concatenate([jnp.concatenate(r, 1) for r in rows], 0)
    grow = jnp.exp(logs_l)
    scan = intra + grow * mm(c, state.astype(bf16))
    last = logs_l[L - 1 : L]
    tails = jnp.exp(last - logs_l)
    txd = (tails * xd.astype(f32)).astype(bf16)
    state = jnp.exp(last) * state + mm_tn(b, txd)
    gsig = sigmoid(gates)
    gate = gates * gsig
    mixed = (scan + skip * x) * gate
    kept[:, pl.ds(GROW, IN)] = grow.astype(bf16)
    kept[:, pl.ds(TAIL, IN)] = tails.astype(bf16)
    kept[:, pl.ds(TXD, IN)] = txd
    kept[:, pl.ds(GATE, IN)] = gate.astype(bf16)
    kept[:, pl.ds(D_GATE, IN)] = (gsig + gate * (1.0 - gsig)).astype(bf16)
    kept_f[:, pl.ds(SCAN, IN)] = scan
    return mixed, state


def bwd_block(window, kept, kept_f, kept_h, taps, heads, skip, gain, state, rnorm, products, g_gated, d_state, after, tick):
    low = low_lanes(L)

    def wide(at, width=IN):
        return kept[:, pl.ds(at, width)]

    x, gate = wide(X).astype(f32), wide(GATE).astype(f32)
    scan = kept_f[:, pl.ds(SCAN, IN)]
    y = scan + skip * x
    mixed = y * gate
    g_mixed = rnorm * (g_gated * gain) - mixed * (rnorm * rnorm * rnorm * products * (1.0 / INNER))
    gain_sum = jnp.sum(g_gated * mixed * rnorm, axis=0, keepdims=True)
    dy = g_mixed * gate
    d_gates = (g_mixed * y * wide(D_GATE).astype(f32)).astype(bf16)
    skip_sum = jnp.sum(dy * x, axis=0, keepdims=True)
    dyb = dy.astype(bf16)
    zero = jnp.zeros((), bf16)
    dg = [0.0, 0.0]
    parts = []
    for j in range(3):
        if j == 1:
            tick(2)
        pair_x = kept[:, pl.ds(XD + 128 * j, 128)]
        pair_y = dyb[:, 128 * j : 128 * (j + 1)]
        own = (jnp.where(low, pair_y, zero), jnp.where(low, zero, pair_y))
        upper, lower = 0.0, 0.0
        for e in range(2):
            h = 2 * j + e
            for t in range(2):
                w = 128 * (t + 1)
                mine = own[e][128 * t : 128 * (t + 1)]
                dm = mm_nt(mine, pair_x[:w])
                pieces = [kept_h[HD + h, pl.ds(128 * (t + k), 128)] for k in range(t + 1)]
                wt = jnp.concatenate(pieces, 1) if t else pieces[0]
                dg[t] = dg[t] + dm * wt.astype(f32)
                back = mm(kept_h[h, pl.ds(128 * t, w)], mine)
                upper = upper + back[:128]
                if t:
                    lower = lower + back[128:]
        parts.append(jnp.concatenate([upper, lower], 0))
    tick(4)
    d_intra = jnp.concatenate(parts, 1)
    b, c = wide(KEYS, N), wide(KEYS + N, N)
    grow, txd = wide(GROW), wide(TXD)
    last = grow[L - 1 : L].astype(f32)
    sb = state.astype(bf16)
    dsb = d_state.astype(bf16)
    edy = (grow.astype(f32) * dy).astype(bf16)
    v = mm(b, dsb)
    dxd = d_intra + wide(TAIL).astype(f32) * v
    dg0, dg1 = dg[0].astype(bf16), dg[1].astype(bf16)
    dc = mm_nt(edy, sb) + jnp.concatenate([mm(dg0, b[:128]), mm(dg1, b)], 0)
    first = mm_tn(dg0, c[:128])
    second = mm_tn(dg1, c[128:])
    db = mm_nt(txd, dsb) + jnp.concatenate([first + second[:128], second[128:]], 0)
    tail_part = txd.astype(f32) * v
    z = dyb.astype(f32) * scan - wide(XD).astype(f32) * d_intra - tail_part
    kept_sum = jnp.sum(state * dsb.astype(f32), axis=0, keepdims=True)
    boundary = last * kept_sum + jnp.sum(tail_part, axis=0, keepdims=True)
    row = lax.broadcasted_iota(jnp.int32, (L, IN), 0)
    z = jnp.where(row == L - 1, z + boundary, z)
    r = lax.broadcasted_iota(jnp.int32, (IN, 128), 0)
    cc = lax.broadcasted_iota(jnp.int32, (IN, 128), 1)
    fold = jnp.where((r // PW) == cc, 1.0, 0.0).astype(bf16)
    g_adt = exact_left(tri(False), exact_right(z, fold))
    direct = exact_right(x * dxd, fold)
    dt = kept_f[:, pl.ds(DT, N)]
    d_pre = (direct + heads[1:2] * g_adt) * kept_f[:, pl.ds(D_STEP, N)]
    decay_sum = jnp.sum(dt * g_adt, axis=0, keepdims=True)
    bias_sum = jnp.sum(d_pre, axis=0, keepdims=True)
    d_state = last * d_state + mm_tn(c, edy)
    dx = wide(STEP).astype(f32) * dxd + skip * dy
    g_pre = jnp.concatenate([dx, db, dc], 1) * wide(D_ACT, MIX).astype(f32)
    longer = jnp.concatenate([g_pre, after], 0)
    d_raw = 0.0
    tap_sums = []
    for k in range(4):
        d_raw = d_raw + taps[k : k + 1] * longer[3 - k : 3 - k + L]
        tap_sums.append(jnp.sum(g_pre * window[5 + k : 5 + k + L], axis=0, keepdims=True))
    tap_sums.append(jnp.sum(g_pre, axis=0, keepdims=True))
    g_all = jnp.concatenate([d_gates, d_raw.astype(bf16), d_pre.astype(bf16)], 1)
    sums = (jnp.concatenate(tap_sums, 0), gain_sum, skip_sum, decay_sum, bias_sum)
    return g_all, d_state, g_pre[:8], sums


class Place:
    def __init__(self):
        dp, mp = lax.axis_index("dp"), lax.axis_index("mp")
        self.dp, self.mp = dp, mp
        self.hi, self.x = mp // 4, mp % 4
        self.lo = 1 - self.hi
        self.ylo, self.z, self.core = dp // 8, (dp // 2) % 4, dp % 2
        self.other_core, self.other_ylo = 1 - self.core, 1 - self.ylo
        self.mine, self.theirs = self.hi * 4, self.lo * 4
        self.xs = [(self.x + k) % 4 for k in range(4)]
        self.row = [self.mine + x for x in self.xs]
        self.far_row = [self.theirs + x for x in self.xs]
        self.right, self.left = (dp, self.row[1]), (dp, self.row[3])
        self.across = (dp, self.far_row[0])
        self.line = [(dp, self.row[k]) for k in (1, 3, 2)]
        self.mate = (dp + 1 - 2 * self.core, mp)
        self.beside_dp = self.at(1 - self.ylo, self.z)
        self.beside = (self.beside_dp, mp)
        self.zs = [(self.z + k) % 4 for k in range(4)]
        self.near_dp = [self.at(self.ylo, z) for z in self.zs]
        self.far_dp = [self.at(1 - self.ylo, z) for z in self.zs]
        self.near_slot = [self.ylo * 4 + z for z in self.zs]
        self.far_slot = [(1 - self.ylo) * 4 + z for z in self.zs]
        self.along = [(self.near_dp[k], mp) for k in (1, 2, 3)]
        self.z_gap = [(z + 3 - self.z) % 4 for z in range(4)]
        self.z_dp = [self.at(self.ylo, z) for z in range(4)]
        self.group = [(dp, (mp + k) % GROUP) for k in range(1, GROUP)]
        self.copies = [((dp + k) % DP, mp) for k in range(1, DP)]

    def at(self, ylo, z):
        return ylo * 8 + z * 2 + self.core


def greet(peers):
    barrier = pltpu.get_barrier_semaphore()
    for peer in peers:
        pl.semaphore_signal(barrier, inc=1, device_id=peer, device_id_type=MESH)
    return lambda: pl.semaphore_wait(barrier, len(peers))


class View:
    def __init__(self, ref, *chain):
        self.ref, self.chain = ref, chain

    @property
    def at(self):
        return Indexer(self)

    def build(self):
        ref = self.ref
        for index in self.chain:
            ref = ref.at[index]
        return ref

    def __getitem__(self, index):
        return self.build()[index]

    def __setitem__(self, index, value):
        self.build()[index] = value


class Indexer:
    def __init__(self, view):
        self.view = view

    def __getitem__(self, index):
        return View(self.view.ref, *self.view.chain, index)


class Copy:
    def __init__(self, book, make):
        self.book, self.make = book, make
        book.do(lambda: make().start())

    def wait(self):
        self.book.do(lambda: self.make().wait())

    def wait_recv(self):
        self.book.do(lambda: self.make().wait_recv())

    def wait_send(self):
        self.book.do(lambda: self.make().wait_send())


class Sender:
    def __init__(self, send_sem, recv_sem, local_sem):
        self.send_sem, self.recv_sem, self.local_sem = send_sem, recv_sem, local_sem
        self.count, self.started, self.locals, self.kept = 0, [], 0, None

    def do(self, action):
        if self.kept is None:
            action()
        else:
            self.kept.append(action)

    def reserve(self, count):
        self.count += count
        return self.count - count

    def record(self, plan):
        steps = []
        while True:
            self.kept = []
            more = next(plan, self) is not self
            if self.kept:
                steps.append(self.kept)
            if not more:
                self.kept = None
                return steps

    def __call__(self, source, target, peer):
        k = self.count
        self.count += 1
        copy = Copy(
            self,
            lambda: pltpu.make_async_remote_copy(
                src_ref=source.build(),
                dst_ref=target.build(),
                send_sem=self.send_sem.at[k],
                recv_sem=self.recv_sem.at[k],
                device_id=peer,
                device_id_type=MESH,
            ),
        )
        self.started.append(copy)
        return copy

    def local(self, source, target):
        k = self.locals
        self.locals += 1
        return Copy(
            self,
            lambda: pltpu.make_async_copy(source.build(), target.build(), self.local_sem.at[k]),
        )

    def settle(self, copies):
        for copy in copies:
            copy.wait_send()
        self.started = [copy for copy in self.started if copy not in copies]

    def drain(self):
        self.settle(self.started)


def run(actions):
    for action in actions:
        action()


class Table:
    def __init__(self):
        self.rows = {}

    def add(self, block, tick, actions):
        self.rows.setdefault((block, tick), []).extend(actions)

    def ticker(self, block):
        def tick(t):
            if isinstance(block, int):
                run(self.rows.get((block, t), []))
                return
            for k in range(BLOCKS):
                if (k, t) in self.rows:
                    pl.when(block == k)(lambda k=k: run(self.rows[(k, t)]))

        return tick


def gather_unit(send, place, buf, first, second):
    me, lx, rx, ox = place.row[0], place.row[3], place.row[1], place.row[2]
    ym, lxy, rxy = place.far_row[0], place.far_row[3], place.far_row[1]
    right, left, across = place.right, place.left, place.across
    half = PIECE // 2

    def go(block, slot, h, to):
        part = buf.at[block, slot, pl.ds(half * h, half)]
        return send(part, part, to)

    c = [go(second, me, 0, across), go(second, me, 1, across)]
    a = [go(first, me, 0, right), go(first, me, 1, left)]
    a += [go(first, me, 1, right), go(first, me, 0, left)]
    b = [go(second, me, 0, right), go(second, me, 1, left)]
    b += [go(second, me, 1, right), go(second, me, 0, left)]
    y = [go(first, me, 0, across), go(first, me, 1, across)]
    yield
    a[0].wait_recv()
    f = [go(first, lx, 0, right)]
    y.append(go(first, lx, 0, across))
    a[1].wait_recv()
    f.append(go(first, rx, 1, left))
    y.append(go(first, rx, 1, across))
    yield
    a[2].wait_recv()
    y.append(go(first, lx, 1, across))
    a[3].wait_recv()
    y.append(go(first, rx, 0, across))
    yield
    b[0].wait_recv()
    k = [go(second, lx, 0, right)]
    b[1].wait_recv()
    k.append(go(second, rx, 1, left))
    c[0].wait_recv()
    c[1].wait_recv()
    d = [go(second, ym, 0, right), go(second, ym, 1, left)]
    d += [go(second, ym, 1, right), go(second, ym, 0, left)]
    yield
    f[0].wait_recv()
    y.append(go(first, ox, 0, across))
    f[1].wait_recv()
    y.append(go(first, ox, 1, across))
    for copy in b[2:] + y[:2]:
        copy.wait_recv()
    yield
    d[0].wait_recv()
    e = [go(second, lxy, 0, right)]
    d[1].wait_recv()
    e.append(go(second, rxy, 1, left))
    yield
    for copy in d[2:] + k + e + y[2:]:
        copy.wait_recv()
    yield


def row_gather_unit(send, place, buf, first):
    me, lx, rx = place.xs[0], place.xs[3], place.xs[1]

    def go(block, slot, to):
        part = buf.at[block, slot]
        return send(part, part, to)

    a = [go(first, me, place.right), go(first + 1, me, place.left)]
    a += [go(first + 1, me, place.right), go(first, me, place.left)]
    yield
    a[0].wait_recv()
    f = [go(first, lx, place.right)]
    a[1].wait_recv()
    f.append(go(first + 1, rx, place.left))
    yield
    for copy in a[2:] + f:
        copy.wait_recv()
    yield


def weight_steps(send, place, buf):
    def go(slot, peer):
        return send(buf.at[slot], buf.at[slot], peer)

    own, other = place.dp, place.beside_dp
    one = go(own, place.beside)
    near = [go(own, peer) for peer in place.along]
    mates = [go(own, place.mate)]
    yield
    one.wait_recv()
    far = [go(other, peer) for peer in place.along]
    mates.append(go(other, place.mate))
    yield
    for k in range(3):
        near[k].wait_recv()
        mates.append(go(place.near_dp[3 - k], place.mate))
    yield
    for k in range(3):
        far[k].wait_recv()
        mates.append(go(place.far_dp[3 - k], place.mate))
    yield
    for copy in mates:
        copy.wait_recv()
    yield


def add_into(send, target, other):
    def action():
        target[...] = target[...] + other[...]

    send.do(action)


def put(send, target, index, value):
    def action():
        target[index] = value()

    send.do(action)


def scatter_unit(send, place, buf, first, second, y_in, x_in, xx_in, t_out, t_in, total):
    right, left, across = place.right, place.left, place.across
    half = PIECE // 2
    mine, theirs = place.row, place.far_row
    order = (2, 1, 3, 0)

    def first_hop(k, block, side):
        slot = side[2]
        return [
            send(buf.at[block, slot, pl.ds(0, half)], x_in.at[k, 0], right),
            send(buf.at[block, slot, pl.ds(half, half)], x_in.at[k, 1], left),
        ]

    def second_hop(k, block, side, hops):
        hops[0].wait_recv()
        add_into(send, buf.at[block, side[1], pl.ds(0, half)], x_in.at[k, 0])
        one = send(buf.at[block, side[1]], xx_in.at[k, 0], right)
        hops[1].wait_recv()
        add_into(send, buf.at[block, side[3], pl.ds(half, half)], x_in.at[k, 1])
        return [one, send(buf.at[block, side[3]], xx_in.at[k, 1], left)]

    def three(k, block, side):
        return (
            buf[block, side[0]].astype(f32) + xx_in[k, 0].astype(f32) + xx_in[k, 1].astype(f32)
        )

    ahead = [send(buf.at[first, theirs[n]], y_in.at[k], across) for k, n in enumerate(order)]
    hop_t = first_hop(1, second, theirs)
    hop_m = first_hop(2, second, mine)
    yield
    two_t = second_hop(1, second, theirs, hop_t)
    yield
    ahead[0].wait_recv()
    add_into(send, buf.at[first, mine[2]], y_in.at[0])
    hop_a = first_hop(0, first, mine)
    two_m = second_hop(2, second, mine, hop_m)
    yield
    for copy in two_t:
        copy.wait_recv()
    put(send, t_out, ..., lambda: three(1, second, theirs).astype(bf16))
    last = send(t_out, t_in, across)
    yield
    for k in range(1, 4):
        ahead[k].wait_recv()
        add_into(send, buf.at[first, mine[order[k]]], y_in.at[k])
    two_a = second_hop(0, first, mine, hop_a)
    yield
    for copy in two_m + [last]:
        copy.wait_recv()
    put(send, total, second, lambda: three(2, second, mine) + t_in[...].astype(f32))
    yield
    for copy in two_a:
        copy.wait_recv()
    put(send, total, first, lambda: three(0, first, mine))
    yield


def row_scatter_unit(send, place, buf, first, x_in, xx_in, keep):
    xs = place.xs
    hops = [
        send(buf.at[first, xs[2]], x_in.at[0], place.right),
        send(buf.at[first + 1, xs[2]], x_in.at[1], place.left),
    ]
    yield
    hops[0].wait_recv()
    add_into(send, buf.at[first, xs[1]], x_in.at[0])
    two = [send(buf.at[pl.ds(first, 2), xs[1]], xx_in.at[0], place.right)]
    hops[1].wait_recv()
    add_into(send, buf.at[first + 1, xs[3]], x_in.at[1])
    two.append(send(buf.at[pl.ds(first, 2), xs[3]], xx_in.at[1], place.left))
    yield
    for copy in two:
        copy.wait_recv()

    def last(k):
        total = buf[first + k, xs[0]].astype(f32)
        keep(first + k, total + xx_in[0, k].astype(f32) + xx_in[1, k].astype(f32))

    for k in range(2):
        send.do(lambda k=k: last(k))
    yield


class Reduction:
    def __init__(self, send, place, grads, core_in, z_in, y_out, w_in, keep):
        self.send, self.place, self.grads, self.core_in = send, place, grads, core_in
        self.z_in, self.y_out, self.w_in, self.keep = z_in, y_out, w_in, keep
        self.swaps, self.base = {}, send.reserve(8)

    def swap(self, i):
        pairs = pl.ds(2 * i, 2)
        part = self.grads.at[pairs, self.place.other_core]
        self.swaps[i] = self.send(part, self.core_in.at[pairs], self.place.mate)

    def hop(self, k, y, slot, peer):
        at = self.base + 2 * k + y
        return pltpu.make_async_remote_copy(
            src_ref=self.grads.at[slot, self.place.core].build(),
            dst_ref=self.z_in.at[k, y].build(),
            send_sem=self.send.send_sem.at[at],
            recv_sem=self.send.recv_sem.at[at],
            device_id=peer,
            device_id_type=MESH,
        )

    def fold(self, i):
        place = self.place
        self.swaps[i].wait_recv()
        for slot in (2 * i, 2 * i + 1):
            add_into(self.send, self.grads.at[slot, place.core], self.core_in.at[slot])
            y, z = slot // 4, slot % 4

            def action(slot=slot, y=y, z=z):
                k, peer = place.z_gap[z], (place.z_dp[z], place.mp)
                pl.when(place.z != z)(lambda: self.hop(k, y, slot, peer).start())

            self.send.do(action)

    def arrive(self, y):
        for k in range(3):
            self.send.do(lambda k=k: self.hop(k, y, 0, self.place.along[k]).wait_recv())

    def joined(self, y, slot):
        total = self.grads[slot, self.place.core].astype(f32)
        for k in range(3):
            total = total + self.z_in[k, y].astype(f32)
        return total

    def cross(self):
        y, slot = self.place.other_ylo, self.place.far_slot[0]
        self.arrive(y)
        put(self.send, self.y_out, ..., lambda: self.joined(y, slot).astype(bf16))
        self.crossed = self.send(self.y_out, self.w_in, self.place.beside)

    def end(self):
        y, slot = self.place.ylo, self.place.near_slot[0]
        self.arrive(y)
        self.crossed.wait_recv()
        self.send.do(lambda: self.keep(self.joined(y, slot) + self.w_in[...].astype(f32)))

    def settle(self):
        for k in range(3):
            for y in range(2):
                self.hop(k, y, 0, self.place.along[k]).wait_send()


def rows(block, count=L):
    return pl.ds(pl.multiple_of(block * count, count), count)


def pick(columns, block):
    lane = lax.broadcasted_iota(jnp.int32, columns.shape, 1)
    return jnp.sum(jnp.where(lane == block, columns, 0.0), axis=1, keepdims=True)


def parameters(channel_terms, side_terms, head_terms, taps, heads, skip, gain):
    taps[pl.ds(0, CONV + 1), pl.ds(0, IN)] = channel_terms[pl.ds(0, CONV + 1)]
    taps[pl.ds(0, CONV + 1), pl.ds(IN, 2 * N)] = side_terms[...]
    taps[pl.ds(CONV + 1, 3)] = jnp.zeros((3, MIX), f32)
    gain[...] = channel_terms[pl.ds(CONV + 1, 1)]
    wide = jnp.concatenate([head_terms[...], jnp.zeros((3, N - HD), f32)], 1)
    lane = lax.broadcasted_iota(jnp.int32, (1, N), 1)
    decay = jnp.where(lane < HD, -jnp.exp(wide[1:2]), 0.0)
    heads[...] = jnp.concatenate([wide[0:1], decay, jnp.zeros((6, N), f32)], 0)
    skip[...] = spread(jnp.broadcast_to(wide[2:3], (8, N)), low_lanes(8))[0:1]


def valid_rows(seq_len, place, block):
    row = lax.broadcasted_iota(jnp.int32, (PIECE, 1), 0)
    position = row + (place.mp * PIECE + block * L)
    return jnp.where(position < seq_len[...], 1.0, 0.0)


def front_kernel(
    tokens, grad_out, seq_len, norm_gain, main_weight, side_weight, output_weight,
    channel_terms, side_terms, head_terms,
    whole_o, weights_o, out_o, back_o, raw_o, kept_o, kept_f_o, kept_h_o, states_o, g_gated_o, gated_o, sums,
    whole, weights, out, back, raw, states, g_gated, gated, gates, steps, kept, kept_f, kept_h, mixed, halves,
    taps, heads, skip, gain, squares, state, inbox, send_sem, recv_sem, local_sem,
):
    (
        tokens, grad_out, seq_len, norm_gain, main_weight, side_weight, output_weight,
        channel_terms, side_terms, head_terms, whole_o, weights_o, out_o, back_o, raw_o,
        kept_o, kept_f_o, kept_h_o, states_o, g_gated_o, gated_o, sums, whole, weights, out,
        back, raw, states, g_gated, gated, gates, steps, kept, kept_f, kept_h, mixed,
        halves, taps, heads, skip, gain, squares, state, inbox,
    ) = map(
        View,
        (
            tokens, grad_out, seq_len, norm_gain, main_weight, side_weight, output_weight,
            channel_terms, side_terms, head_terms, whole_o, weights_o, out_o, back_o, raw_o,
            kept_o, kept_f_o, kept_h_o, states_o, g_gated_o, gated_o, sums, whole, weights, out,
            back, raw, states, g_gated, gated, gates, steps, kept, kept_f, kept_h, mixed,
            halves, taps, heads, skip, gain, squares, state, inbox,
        ),
    )
    place = Place()
    meet = greet(place.group + [place.mate, place.beside] + place.along)
    scale_row = norm_gain[...].reshape(1, D)
    for i in range(BLOCKS):
        x = tokens[i].astype(f32)
        scale = lax.rsqrt(jnp.mean(x * x, axis=1, keepdims=True) + epsilon)
        whole[i, place.mp] = (x * scale * scale_row).astype(bf16)
    columns = weights.at[place.dp]
    for k in range(2):
        columns[:, pl.ds(k * IN, IN)] = main_weight[:, k].astype(bf16)
    columns[:, pl.ds(2 * IN, 2 * N)] = side_weight[:, pl.ds(0, 2 * N)]
    source = lax.broadcasted_iota(jnp.int32, (HEADS, N), 0)
    lane = lax.broadcasted_iota(jnp.int32, (HEADS, N), 1)
    spot = jnp.where((source == lane + HD * place.mp) & (lane < HD), 1.0, 0.0).astype(bf16)
    own_steps = mm(side_weight[:, pl.ds(2 * N, HEADS)], spot)
    columns[:, pl.ds(2 * IN + 2 * N, N)] = own_steps.astype(bf16)
    out[place.dp, :, pl.ds(0, IN)] = output_weight[...]
    meet()
    send = Sender(send_sem, recv_sem, local_sem)
    units = [send.record(gather_unit(send, place, whole, 2 * u, 2 * u + 1)) for u in range(4)]
    cols = send.record(weight_steps(send, place, weights))
    outs = send.record(weight_steps(send, place, out))
    backs = [send.record(row_gather_unit(send, place, back, 2 * u)) for u in range(4)]

    run(cols[0])
    own_out = out.at[place.dp, :, pl.ds(0, IN)]
    pair = send(own_out, out.at[place.dp, :, pl.ds(IN, IN)], place.across)
    for unit in units:
        run(unit[0])
    for i in range(BLOCKS):
        rounded = valid_rows(seq_len, place, i) * grad_out[i].astype(f32)
        back[i, place.xs[0]] = rounded.astype(bf16)
    parameters(channel_terms, side_terms, head_terms, taps, heads, skip, gain)
    raw[pl.ds(0, 8)] = jnp.zeros((8, MIX), f32)
    state[...] = jnp.zeros((N, IN), f32)
    squares[...] = jnp.zeros((L, 128), f32)

    def project_rows(device, first=0, count=BLOCKS):
        block = whole[pl.ds(first, count), device].reshape(count * PIECE, D)
        both = mm(block, weights[...].reshape(D, COLS))
        for i in range(count):
            part = both[i * PIECE : (i + 1) * PIECE]
            start = (first + i) * L + device * PIECE
            at = pl.ds(pl.multiple_of(start, PIECE), PIECE)
            gates[at] = part[:, :IN]
            steps[at] = part[:, IN + MIX :]
            raw[pl.ds(pl.multiple_of(start + 8, 8), PIECE)] = part[:, IN : IN + MIX]

    far = (place.row[2], place.far_row[3], place.far_row[1], place.far_row[2])

    def early(k):
        run(units[0][k] + units[1][k])

    def late(k):
        run(units[2][k] + units[3][k])

    early(1)
    run(cols[1])
    early(2)
    late(1)
    pair.wait_recv()
    run(outs[0] + cols[2])
    early(3)
    late(2)
    for back_unit in backs:
        run(back_unit[0])
    run(cols[3])
    early(4)
    late(3)
    run(cols[4])
    project_rows(place.row[0])
    early(5)
    late(4)
    project_rows(place.row[3])
    run(outs[1])
    project_rows(place.row[1])
    early(6)
    late(5)
    project_rows(place.far_row[0])
    run(backs[0][1] + backs[1][1])
    for device in far:
        project_rows(device, 0, 4)
    stored = []

    def second_half():
        for device in far:
            project_rows(device, 4, 4)

    def store_early():
        stored.append(send.local(whole, whole_o))
        stored.append(send.local(weights, weights_o))
        yield

    lane = lax.broadcasted_iota(jnp.int32, (L, 128), 1)
    crossing = [None] * 4

    def project(u):
        pairs = pl.ds(2 * u, 2)

        def action():
            both = mm(back[pairs].reshape(L, D), out[...].reshape(D, 2 * IN)).astype(bf16)
            g_gated[pairs, place.hi] = both[:, :IN].reshape(2, L // 2, IN)
            halves[pairs] = both[:, IN:].reshape(2, L // 2, IN)

        send.do(action)
        crossing[u] = send(halves.at[pairs], g_gated.at[pairs, place.hi], place.across)
        yield

    projections = [send.record(project(u))[0] for u in range(4)]
    def store_out():
        stored.append(send.local(out, out_o))
        yield

    table = Table()
    for block, tick, actions in (
        (0, 2, backs[2][1] + backs[3][1] + outs[2]),
        (0, 5, units[2][6]),
        (1, 3, units[3][6] + outs[3]),
        (2, 3, outs[4]),
        (2, 5, backs[3][2] + projections[3]),
        (3, 5, [second_half] + send.record(store_early())[0]),
        (4, 2, backs[2][2] + projections[2]),
        (5, 2, send.record(store_out())[0]),
        (6, 2, backs[1][2] + projections[1]),
    ):
        table.add(block, tick, actions)

    def block_copies(i):
        slot = lax.rem(i, 2)
        below = pl.ds(pl.multiple_of(i * L + 8, 8), L)
        pairs = [
            (raw.at[below], raw_o.at[below]),
            (kept.at[slot], kept_o.at[i]),
            (kept_f.at[slot], kept_f_o.at[i]),
            (kept_h.at[slot], kept_h_o.at[i]),
            (states.at[i], states_o.at[i]),
        ]
        return [
            pltpu.make_async_copy(source.build(), target.build(), local_sem.at[16 + 5 * slot + k])
            for k, (source, target) in enumerate(pairs)
        ]

    def block_wait(i):
        for copy in block_copies(i):
            copy.wait()

    def body(i, carry):
        tick = table.ticker(i)
        at = rows(i)
        slot = lax.rem(i, 2)
        pl.when(i >= 2)(lambda: block_wait(i - 2))
        states[i] = state[...]
        window = raw[pl.ds(pl.multiple_of(i * L, 8), L + 8)]
        outer, following = fwd_block(
            window, gates[at], steps[at], taps[...], heads[...], skip[...], state[...], tick,
            kept.at[slot], kept_f.at[slot], kept_h.at[slot],
        )
        mixed[at] = outer
        state[...] = following
        square = jnp.sum(outer * outer, axis=1, keepdims=True)
        squares[...] = jnp.where(lane == i, square, squares[...])
        for copy in block_copies(i):
            copy.start()
        tick(5)
        return carry

    lax.fori_loop(0, BLOCKS, body, 0)
    inbox[place.mp] = squares[...].T[:8]
    copies = [send(inbox.at[place.mp], inbox.at[place.mp], peer) for peer in place.group]
    stored.append(send.local(raw.at[pl.ds(0, 8)], raw_o.at[pl.ds(0, 8)]))
    run(backs[0][2] + projections[0])
    stored.append(send.local(back, back_o))
    for copy in copies:
        copy.wait_recv()
    total = inbox[0]
    for k in range(1, GROUP):
        total = total + inbox[k]
    top = lax.rsqrt(total * (1.0 / INNER) + epsilon)
    scales = jnp.concatenate([top, jnp.zeros((120, L), f32)], 0).T
    for i in range(BLOCKS):
        rounded = (mixed[pl.ds(i * L, L)] * scales[:, i : i + 1] * gain[...]).astype(bf16)
        gated[i] = rounded.reshape(2, L // 2, IN)
    stored.append(send.local(gated, gated_o))

    def products(u, scales):
        crossing[u].wait_recv()
        for i in (2 * u, 2 * u + 1):
            part = g_gated[i].reshape(L, IN).astype(f32) * gain[...] * mixed[pl.ds(i * L, L)]
            product = jnp.sum(part, axis=1, keepdims=True)
            scales = jnp.where(lane == i + 8, product, scales)
        return scales

    for u in (3, 2, 1, 0):
        scales = products(u, scales)
    sums[...] = scales
    stored.append(send.local(g_gated, g_gated_o))
    for copy in stored:
        copy.wait()

    block_wait(jnp.int32(BLOCKS - 2))
    block_wait(jnp.int32(BLOCKS - 1))
    send.drain()


def back_kernel(
    whole_i, weights_i, out_i, back_i, raw_i, kept_i, kept_f_i, kept_h_i, states_i, g_gated_i, gated_i,
    sums, tokens, grad_out, seq_len, norm_gain, channel_terms, side_terms, head_terms,
    layer_out, token_grad, gain_grad, main_grad, side_grad, out_grad, conv_grad, channel_grad, head_grad,
    weights, out, gated, raw, kept, kept_f, kept_h, states, g_gated, whole, g_all, left,
    row_parts, row_x, row_xx, parts, y_in, x_in, xx_in, t_out, t_in,
    grads, core_in, z_in, y_out, w_in, s_core, s_z, s_out, s_in, o_core, o_z, o_out, o_in, pair_out, pair_in,
    taps, heads, skip, gain, columns, totals, d_state, after, gain_part,
    products_box, share_box, side_own, side_in, side_box, sums_box, send_sem, recv_sem, local_sem,
):
    (
        whole_i, weights_i, out_i, back_i, raw_i, kept_i, kept_f_i, kept_h_i, states_i,
        g_gated_i, gated_i, sums, tokens, grad_out, seq_len, norm_gain, channel_terms,
        side_terms, head_terms, layer_out, token_grad, gain_grad, main_grad, side_grad,
        out_grad, conv_grad, channel_grad, head_grad, weights, out, gated, raw, kept,
        kept_f, kept_h, states, g_gated, whole, g_all, left, row_parts, row_x, row_xx,
        parts, y_in, x_in, xx_in, t_out, t_in, grads, core_in, z_in, y_out, w_in, s_core,
        s_z, s_out, s_in, o_core, o_z, o_out, o_in, pair_out, pair_in, taps, heads, skip,
        gain, columns, totals, d_state, after, gain_part, products_box, share_box, side_own,
        side_in, side_box, sums_box,
    ) = map(
        View,
        (
            whole_i, weights_i, out_i, back_i, raw_i, kept_i, kept_f_i, kept_h_i, states_i,
            g_gated_i, gated_i, sums, tokens, grad_out, seq_len, norm_gain, channel_terms,
            side_terms, head_terms, layer_out, token_grad, gain_grad, main_grad, side_grad,
            out_grad, conv_grad, channel_grad, head_grad, weights, out, gated, raw, kept,
            kept_f, kept_h, states, g_gated, whole, g_all, left, row_parts, row_x, row_xx,
            parts, y_in, x_in, xx_in, t_out, t_in, grads, core_in, z_in, y_out, w_in, s_core,
            s_z, s_out, s_in, o_core, o_z, o_out, o_in, pair_out, pair_in, taps, heads, skip,
            gain, columns, totals, d_state, after, gain_part, products_box, share_box, side_own,
            side_in, side_box, sums_box,
        ),
    )
    place = Place()
    meet = greet(place.group + place.copies)
    send = Sender(send_sem, recv_sem, local_sem)

    def loads(i, slot):
        return [
            (raw_i.at[pl.ds(pl.multiple_of(i * L, 8), L + 8)], raw.at[slot]),
            (kept_i.at[i], kept.at[slot]),
            (kept_f_i.at[i], kept_f.at[slot]),
            (kept_h_i.at[i], kept_h.at[slot]),
            (states_i.at[i], states.at[slot]),
            (g_gated_i.at[i], g_gated.at[slot]),
        ]

    def load(i, slot, start):
        for k, (source, target) in enumerate(loads(i, slot)):
            copy = pltpu.make_async_copy(
                source.build(), target.build(), local_sem.at[16 + 6 * slot + k]
            )
            if start:
                copy.start()
            else:
                copy.wait()

    def known_rows(i):
        return pltpu.make_async_copy(whole_i.at[i].build(), whole.build(), local_sem.at[28])

    load(BLOCKS - 1, 1, True)
    known_rows(BLOCKS - 1).start()
    first = [
        send.local(gated_i.at[:, place.hi], gated.at[:, :, pl.ds(0, IN)]),
        send.local(out_i, out),
        send.local(weights_i, weights),
    ]
    load(BLOCKS - 2, 0, True)
    products_box[place.mp] = sums[...].T[8:16]
    meet()
    product_copies = [
        send(products_box.at[place.mp], products_box.at[place.mp], peer) for peer in place.group
    ]
    crossing = [
        send(
            gated_i.at[pl.ds(2 * u, 2), place.lo],
            gated.at[pl.ds(2 * u, 2), :, pl.ds(IN, IN)],
            place.across,
        )
        for u in (3, 2, 1, 0)
    ][::-1]
    parameters(channel_terms, side_terms, head_terms, taps, heads, skip, gain)
    d_state[...] = jnp.zeros((N, IN), f32)
    after[...] = jnp.zeros((8, MIX), f32)
    totals[...] = jnp.zeros((8, 2 * IN), f32)
    gain_part[...] = jnp.zeros((1, D), f32)
    columns[...] = sums[...]

    def late_products():
        for copy in product_copies:
            copy.wait_recv()
        total = products_box[0]
        for k in range(1, GROUP):
            total = total + products_box[k]
        summed = jnp.concatenate([jnp.zeros((8, L), f32), total, jnp.zeros((112, L), f32)], 0).T
        lane = lax.broadcasted_iota(jnp.int32, (L, 128), 1)
        columns[...] = jnp.where(lane >= 8, summed, columns[...])

    late_products()

    for copy in first:
        copy.wait()

    def keep_layer(i, total):
        layer_out[i] = (
            tokens[i].astype(f32) + valid_rows(seq_len, place, i) * total
        ).astype(bf16)

    def row_plan(u):
        def action():
            pairs = pl.ds(2 * u, 2)
            part = mm_nt(gated[pairs].reshape(L, 2 * IN), out[...].reshape(D, 2 * IN))
            row_parts[pairs] = part.astype(bf16).reshape(2, 4, PIECE, D)

        crossing[u].wait_recv()
        yield
        send.do(action)
        yield from row_scatter_unit(
            send, place, row_parts, 2 * u, row_x.at[u], row_xx.at[u], keep_layer
        )

    def keep_out(total):
        pair_out[...] = total[:, IN:]
        out_grad[...] = total[:, :IN]

    def keep_main(total):
        main_grad[:, 0] = total[:, :IN]
        main_grad[:, 1] = total[:, IN:]

    def keep_side(total):
        turned = total[:, 2 * N :].T[:16]
        blank = jnp.zeros((16, 2 * N - D // DP), f32)
        side_own[pl.ds(0, D // DP)] = total[:, : 2 * N].astype(bf16)
        side_own[pl.ds(D // DP, 16)] = jnp.concatenate([turned, blank], 1).astype(bf16)

    main_part = grads.at[:, :, :, pl.ds(0, 2 * IN)]
    side_part = grads.at[:, :, :, pl.ds(2 * IN, 3 * N)]
    out_sum = Reduction(send, place, main_part, o_core, o_z, o_out, o_in, keep_out)
    main_sum = Reduction(send, place, main_part, core_in, z_in, y_out, w_in, keep_main)
    side_sum = Reduction(send, place, side_part, s_core, s_z, s_out, s_in, keep_side)

    def out_plan():
        chunks = [
            send.local(
                back_i.at[:, :, :, pl.ds(i * 384, 384)], left.at[i, :, pl.ds(0, 4)]
            )
            for i in range(2)
        ]
        yield
        for i in range(4):
            chunks[i].wait()

            def action(i=i):
                side = left[i % 2, :, pl.ds(0, 4)].reshape(BLOCKS * L // 2, 384)
                pairs = pl.ds(2 * i, 2)
                part = mm_tn(side, gated[...].reshape(BLOCKS * L // 2, 2 * IN))
                grads[pairs, :, :, : 2 * IN] = part.astype(bf16).reshape(2, 2, 96, 2 * IN)

            send.do(action)
            if i < 2:
                chunks.append(
                    send.local(
                        back_i.at[:, :, :, pl.ds((i + 2) * 384, 384)],
                        left.at[i, :, pl.ds(0, 4)],
                    )
                )
            out_sum.swap(i)
            if i == 3:
                whole_loads.append(load_whole(0))
                whole_loads.append(load_whole(1))
            yield
        for i in range(4):
            out_sum.fold(i)
        yield
        out_sum.cross()
        yield
        out_sum.end()
        pair = send(pair_out, pair_in, place.across)
        yield
        pair.wait_recv()

        def finish():
            out_grad[...] += pair_in[...]

        send.do(finish)
        yield

    whole_loads = []

    def load_whole(i):
        return send.local(whole_i.at[:, :, :, pl.ds(i * 384, 384)], left.at[i % 2])

    row_units = [send.record(row_plan(u)) for u in range(4)]
    outs = send.record(out_plan())

    def final_rows(i):
        gain_row = norm_gain[...].reshape(1, D)
        x = tokens[i].astype(f32)
        s = lax.rsqrt(jnp.mean(x * x, axis=1, keepdims=True) + epsilon)
        g = token_grad[i]
        dot = jnp.sum(g * gain_row * x, axis=1, keepdims=True)
        token_grad[i] = grad_out[i].astype(f32) + s * gain_row * g - x * (s * s * s * dot * (1.0 / D))

    units = [
        send.record(
            scatter_unit(
                send, place, parts, 2 * u, 2 * u + 1,
                y_in.at[u], x_in.at[u], xx_in.at[u], t_out.at[u], t_in.at[u], token_grad,
            )
        )
        for u in range(4)
    ]
    for u in range(4):
        units[u][6] += [lambda i=2 * u + k: final_rows(i) for k in range(2)]

    table = Table()
    for block, tick, actions in (
        (0, 0, row_units[3][0]),
        (0, 0, row_units[3][1]),
        (0, 6, row_units[2][0]),
        (0, 6, row_units[2][1]),
        (1, 4, row_units[3][2]),
        (1, 6, units[3][0]),
        (1, 6, outs[0]),
        (2, 2, row_units[1][0]),
        (2, 2, row_units[0][0]),
        (2, 4, outs[1]),
        (2, 4, row_units[2][2]),
        (2, 6, outs[2]),
        (3, 2, outs[3]),
        (3, 4, units[3][1]),
        (3, 4, row_units[3][3]),
        (3, 5, units[3][2]),
        (3, 5, outs[4]),
        (3, 6, units[2][0]),
        (4, 0, row_units[2][3]),
        (4, 2, units[3][3]),
        (4, 2, outs[5]),
        (4, 6, units[3][4]),
        (4, 6, row_units[1][1]),
        (5, 4, units[2][1]),
        (5, 5, units[2][2]),
        (5, 6, units[3][5]),
        (5, 6, units[1][0]),
        (6, 0, units[2][3]),
        (6, 0, row_units[1][2]),
        (6, 5, units[3][6]),
        (6, 5, row_units[0][1]),
        (6, 6, units[2][4]),
        (6, 6, outs[6]),
        (7, 4, units[1][1]),
        (7, 5, units[1][2]),
        (7, 5, outs[7]),
        (7, 6, units[2][5]),
        (7, 6, units[0][0]),
    ):
        table.add(block, tick, actions)

    def body(j):
        tick = table.ticker(j)
        i = BLOCKS - 1 - j
        slot = i % 2
        tick(0)
        load(i, slot, False)
        g, ds, top, found = bwd_block(
            raw[slot], kept.at[slot], kept_f.at[slot], kept_h.at[slot],
            taps[...], heads[...], skip[...], gain[...],
            states[slot], pick(columns[...], i), pick(columns[...], i + 8),
            g_gated[slot].reshape(L, IN).astype(f32), d_state[...], after[...], tick,
        )
        g_all[rows(i)] = g
        d_state[...] = ds
        after[...] = top
        tap_sums, gain_sum, skip_sum, decay_sum, bias_sum = found
        blank = jnp.zeros((1, IN), f32)
        fill = jnp.zeros((1, IN - 2 * N), f32)
        totals[...] += jnp.concatenate(
            [
                jnp.concatenate([tap_sums, jnp.zeros((CONV + 1, 2 * IN - MIX), f32)], 1),
                jnp.concatenate([gain_sum, blank], 1),
                jnp.concatenate([skip_sum, blank], 1),
                jnp.concatenate([decay_sum, bias_sum, fill, blank], 1),
            ],
            0,
        )
        tick(5)
        part = mm_nt(g, weights[...].reshape(D, COLS)).astype(bf16)
        parts[i] = part.reshape(GROUP, PIECE, D)
        known_rows(i).wait()
        product = part * whole[...].reshape(L, D)
        gain_part[...] += mm(jnp.ones((8, L), bf16), product)[0:1]
        if i >= 1:
            known_rows(i - 1).start()
        if i >= 2:
            load(i - 2, slot, True)
        tick(6)

    for block in range(BLOCKS):
        body(block)

    gain_sum = gain_part[...] / norm_gain[...].reshape(1, D)
    narrow = [gain_sum[:, k * N : (k + 1) * N] for k in range(CONV + 1)]
    start = (CONV + 1) * N
    broad = [gain_sum[:, start : start + IN], gain_sum[:, start + IN : start + 2 * IN]]
    rest = gain_sum[:, start + 2 * IN :]
    broad.append(jnp.concatenate([rest, jnp.zeros((1, 3 * IN - D + start), f32)], 1))
    found = totals[...]
    upper = jnp.concatenate([found[: CONV + 1, :MIX], jnp.concatenate(narrow, 0)], 1)
    lower = jnp.concatenate([found[CONV + 1 :, :IN], jnp.concatenate(broad, 0)], 1)
    sums_box[0] = jnp.concatenate([upper, lower], 0)
    stage = [send(sums_box.at[0], sums_box.at[1], place.mate)]
    send.settle(list(out_sum.swaps.values()))
    out_sum.settle()
    late = [
        units[1][3] + row_units[0][2] + units[2][6],
        units[0][1] + units[0][2] + row_units[1][3],
        units[1][4] + units[0][3],
        units[1][5],
        units[0][4] + units[1][6],
        units[0][5] + units[0][6],
        row_units[0][3],
    ]

    def whole_chunk(load, slot):
        whole_loads[load].wait()
        return left[slot].reshape(BLOCKS * L, 384)

    def side_chunk(i):
        pairs = pl.ds(2 * i, 2)
        part = mm_tn(whole_chunk(i, i % 2), g_all[:, pl.ds(2 * IN, 3 * N)]).astype(bf16)
        grads[pairs, :, :, 2 * IN :] = part.reshape(2, 2, 96, 3 * N)
        side_sum.swap(i)

    def main_chunk(i, load=None):
        pairs = pl.ds(2 * i, 2)
        if load is not None:
            whole_loads[load].wait()
        side = left[i % 2].reshape(BLOCKS * L, 384)
        part = mm_tn(side, g_all[:, pl.ds(0, 2 * IN)]).astype(bf16)
        grads[pairs, :, :, : 2 * IN] = part.reshape(2, 2, 96, 2 * IN)
        main_sum.swap(i)

    side_chunk(0)
    whole_loads.append(load_whole(2))
    side_chunk(1)
    whole_loads.append(load_whole(3))
    run(late[0])
    side_chunk(2)
    stage[0].wait_recv()
    sums_box[2] = sums_box[0] + sums_box[1]
    stage = [send(sums_box.at[2], sums_box.at[3 + k], peer) for k, peer in enumerate(place.along)]
    side_chunk(3)
    run(late[1])
    main_chunk(2)
    whole_loads.append(load_whole(0))
    for i in range(4):
        side_sum.fold(i)
    main_chunk(3)
    whole_loads.append(load_whole(1))
    run(late[2])
    for copy in stage:
        copy.wait_recv()
    sums_box[6] = sums_box[2] + sums_box[3] + sums_box[4] + sums_box[5]
    stage = [send(sums_box.at[6], sums_box.at[7], place.beside)]
    main_chunk(0, 4)
    main_sum.fold(2)
    main_sum.fold(3)
    run(late[3])
    main_chunk(1, 5)
    main_sum.fold(0)
    side_sum.cross()
    main_sum.fold(1)
    run(late[4])
    side_sum.end()
    pair = send(side_own, side_in, place.across)
    main_sum.cross()
    pair.wait_recv()
    total = side_own[pl.ds(0, D // DP)].astype(f32) + side_in[pl.ds(0, D // DP)].astype(f32)
    side_box[place.x, pl.ds(0, D // DP)] = total.astype(bf16)
    side_box[place.x, pl.ds(D // DP, 16)] = side_own[pl.ds(D // DP, 16)]
    side_box[place.x, pl.ds(D // DP + 16, 16)] = side_in[pl.ds(D // DP, 16)]
    sides = [send(side_box.at[place.x], side_box.at[place.x], peer) for peer in place.line]
    stage[0].wait_recv()
    copied = sums_box[6] + sums_box[7]
    share_box[place.mp] = copied[:, IN:]
    shares = [send(share_box.at[place.mp], share_box.at[place.mp], peer) for peer in place.group]
    channel_grad[...] = copied[: CONV + 2, :IN]
    r = lax.broadcasted_iota(jnp.int32, (IN, N), 0)
    c = lax.broadcasted_iota(jnp.int32, (IN, N), 1)
    fold = jnp.where((r // PW) == c, 1.0, 0.0).astype(bf16)
    skips = exact_right(jnp.broadcast_to(copied[CONV + 2 : CONV + 3, :IN], (8, IN)), fold)
    decays = heads[pl.ds(1, 1)] * copied[CONV + 3 :, :N]
    biases = copied[CONV + 3 :, N : 2 * N]
    head_grad[...] = jnp.concatenate([biases, decays, skips[0:1]], 0)[:, :HD]
    run(late[5])

    for copy in shares:
        copy.wait_recv()
    shared = share_box[0]
    for k in range(1, GROUP):
        shared = shared + share_box[k]
    conv_grad[...] = shared[: CONV + 1, : 2 * N]
    for k in range(CONV + 1):
        gain_grad[pl.ds(k * N, N)] = shared[k, 2 * N :]
    for k in range(3):
        width = min(IN, D - start - k * IN)
        gain_grad[pl.ds(start + k * IN, width)] = shared[CONV + 1 + k, :width]
    run(late[6])
    run(outs[8])
    main_sum.end()
    for copy in sides:
        copy.wait_recv()
    both, steps_sum = 0.0, 0.0
    lane = lax.broadcasted_iota(jnp.int32, (16, N), 1)
    source = lax.broadcasted_iota(jnp.int32, (16, N), 0)
    for k in range(4):
        both = both + side_box[k, pl.ds(0, D // DP)].astype(f32)
        for at, first in ((D // DP, place.mine), (D // DP + 16, place.theirs)):
            spot = (lane == source + HD * (first + k)) & (source < HD)
            turned = side_box[k, pl.ds(at, 16), pl.ds(0, N)]
            picked = mm_tn(turned, jnp.where(spot, 1.0, 0.0).astype(bf16))
            steps_sum = steps_sum + picked[: D // DP]
    side_grad[...] = jnp.concatenate([both, steps_sum], 1)[:, : 2 * N + HEADS]
    send.drain()
    main_sum.settle()
    side_sum.settle()


def call(kernel, outs, scratch, sems, collective, args, flops):
    vmem, anywhere = pltpu.VMEM, pl.ANY
    spec = {True: pl.BlockSpec(memory_space=anywhere), False: pl.BlockSpec(memory_space=vmem)}
    return pl.pallas_call(
        kernel,
        out_shape=[jax.ShapeDtypeStruct(shape, dtype) for shape, dtype, _ in outs],
        in_specs=[spec[far] for _, far in args],
        out_specs=[spec[far] for _, _, far in outs],
        scratch_shapes=[pltpu.VMEM(shape, dtype) for shape, dtype in scratch]
        + [pltpu.SemaphoreType.DMA((k,)) for k in sems],
        compiler_params=pltpu.CompilerParams(
            collective_id=collective, has_side_effects=True, vmem_limit_bytes=VMEM_BYTES
        ),
        cost_estimate=pl.CostEstimate(
            flops=flops,
            bytes_accessed=sum(a.size * a.dtype.itemsize for a, _ in args),
            transcendentals=0,
        ),
        name=kernel.__name__,
    )(*[a for a, _ in args])


def deliver_kernel(*refs):
    count = (len(refs) - 2) // 3
    ins, outs, held = refs[:count], refs[count : 2 * count], refs[2 * count : 3 * count]
    sems = refs[-2:]
    copies = [
        [
            pltpu.make_async_copy(source, middle, sems[0].at[k]),
            pltpu.make_async_copy(middle, target, sems[1].at[k]),
        ]
        for k, (source, middle, target) in enumerate(zip(ins, held, outs))
    ]
    for copy, _ in copies:
        copy.start()
    for first, second in copies:
        first.wait()
        second.start()
    for _, copy in copies:
        copy.wait()


def deliver(arrays):
    anywhere = pl.BlockSpec(memory_space=pl.ANY)
    return pl.pallas_call(
        deliver_kernel,
        out_shape=[jax.ShapeDtypeStruct(a.shape, a.dtype) for a in arrays],
        in_specs=[anywhere] * len(arrays),
        out_specs=[anywhere] * len(arrays),
        scratch_shapes=[pltpu.VMEM(a.shape, a.dtype) for a in arrays]
        + [pltpu.SemaphoreType.DMA((len(arrays),))] * 2,
        compiler_params=pltpu.CompilerParams(vmem_limit_bytes=VMEM_BYTES),
        name="deliver_kernel",
    )(*arrays)


def on_device(
    tokens,
    seq_len,
    norm_gain,
    main_weight,
    side_weight,
    side_terms,
    channel_terms,
    head_terms,
    output_weight,
    cotangent,
):
    count, span = BLOCKS * L, D // DP
    saved = [
        ((BLOCKS, GROUP, PIECE, D), bf16),
        ((DP, span, COLS), bf16),
        ((DP, span, 2 * IN), bf16),
        ((BLOCKS, 4, PIECE, D), bf16),
        ((count + 8, MIX), f32),
        ((BLOCKS, L, KEPT), bf16),
        ((BLOCKS, L, KEPT_F), f32),
        ((BLOCKS, 2 * HD, IN, N), bf16),
        ((BLOCKS, N, IN), f32),
        ((BLOCKS, 2, L // 2, IN), bf16),
        ((BLOCKS, 2, L // 2, IN), bf16),
    ]
    terms = [((8, MIX), f32), ((8, N), f32), ((1, IN), f32), ((1, IN), f32)]
    blocks = [((2, L, KEPT), bf16), ((2, L, KEPT_F), f32), ((2, 2 * HD, IN, N), bf16)]
    scratch = saved[:5] + saved[8:] + [((count, IN), f32), ((count, N), f32)] + blocks
    scratch += [((count, IN), f32), ((BLOCKS, L // 2, IN), bf16)] + terms
    scratch += [((L, 128), f32), ((N, IN), f32), ((GROUP, 8, L), f32)]
    own = [tokens[0], cotangent[0], seq_len.reshape(1, 1), norm_gain]
    weights = [main_weight, side_weight, output_weight.T]
    small = [channel_terms, side_terms, head_terms]
    *passed, sums = call(
        front_kernel,
        [(shape, dtype, True) for shape, dtype in saved] + [((L, 128), f32, False)],
        scratch,
        (192, 192, 28),
        0,
        [(a, False) for a in own + weights + small],
        12 * 10**9,
    )
    outs = call(
        back_kernel,
        [
            ((BLOCKS, PIECE, D), bf16, False),
            ((BLOCKS, PIECE, D), f32, False),
            ((D,), f32, False),
            ((span, 2, IN), f32, False),
            ((span, 2 * N + HEADS), f32, False),
            ((span, IN), f32, False),
            ((CONV + 1, 2 * N), f32, False),
            ((CONV + 2, IN), f32, False),
            ((3, HD), f32, False),
        ],
        [
            ((DP, span, COLS), bf16),
            ((DP, span, 2 * IN), bf16),
            ((BLOCKS, L // 2, 2 * IN), bf16),
            ((2, L + 8, MIX), f32),
            *blocks,
            ((2, N, IN), f32),
            ((2, 2, L // 2, IN), bf16),
            ((GROUP, PIECE, D), bf16),
            ((count, COLS), bf16),
            ((2, BLOCKS, GROUP, PIECE, 384), bf16),
            ((BLOCKS, 4, PIECE, D), bf16),
            ((4, 2, PIECE, D), bf16),
            ((4, 2, 2, PIECE, D), bf16),
            ((BLOCKS, GROUP, PIECE, D), bf16),
            ((4, 4, PIECE, D), bf16),
            ((4, 3, 2, PIECE // 2, D), bf16),
            ((4, 3, 2, PIECE, D), bf16),
            ((4, PIECE, D), bf16),
            ((4, PIECE, D), bf16),
            ((8, 2, span, COLS), bf16),
        ]
        + [
            shape
            for width in (2 * IN, 3 * N, 2 * IN)
            for shape in (
                ((8, span, width), bf16),
                ((3, 2, span, width), bf16),
                ((span, width), bf16),
                ((span, width), bf16),
            )
        ]
        + [((span, IN), f32), ((span, IN), f32)]
        + terms
        + [
            ((L, 128), f32),
            ((8, 2 * IN), f32),
            ((N, IN), f32),
            ((8, MIX), f32),
            ((1, D), f32),
            ((GROUP, 8, L), f32),
            ((GROUP, 8, IN), f32),
            ((span + 16, 2 * N), bf16),
            ((span + 16, 2 * N), bf16),
            ((4, span + 32, 2 * N), bf16),
            ((8, 8, 2 * IN), f32),
        ],
        (256, 256, 30),
        1,
        [(a, True) for a in passed] + [(a, False) for a in [sums] + own + small],
        24 * 10**9,
    )
    layer_out, token_grad, gain_grad, main_grad, side_grad, out_grad, *rest = deliver(outs)
    return (
        layer_out[None],
        token_grad[None],
        gain_grad,
        main_grad,
        side_grad,
        *rest,
        out_grad.T,
    )


def solution(mesh):
    placed = (
        P("dp", None, "mp", None),
        P("dp"),
        P(),
        P("dp", None, "mp"),
        P("dp", None),
        P(),
        P(None, "mp"),
        P(None, "mp"),
        P("mp", "dp"),
        P("dp", None, "mp", None),
    )
    return jax.shard_map(
        on_device,
        mesh=mesh,
        in_specs=placed,
        out_specs=(
            P("dp", None, "mp", None),
            P("dp", None, "mp", None),
            P(),
            P("dp", None, "mp"),
            P("dp", None),
            P(),
            P(None, "mp"),
            P(None, "mp"),
            P("mp", "dp"),
        ),
        check_vma=False,
    )
```

```python
import functools

import jax
import jax.numpy as jnp
from jax import lax
from jax.experimental import pallas as pl
from jax.experimental.pallas import tpu as pltpu
from jax.sharding import PartitionSpec as P

f32, bf16 = jnp.float32, jnp.bfloat16
CONV, D, INNER = 4, 1536, 3072
L, N, PW, IN, HD = 256, 128, 64, 384, 6
BLOCKS, GROUP, PIECE, DP, HEADS = 8, 8, 32, 16, 48
COLS = 2 * IN + 3 * N
MIX = IN + 2 * N
MESH = pl.DeviceIdType.MESH
VMEM_BYTES = 63 * 2**20
epsilon = 1e-05
NEG = -1e30

def mm(a, b):
    return lax.dot_general(a, b, (((1,), (0,)), ((), ())), preferred_element_type=f32)
def mm_nt(a, b):
    return lax.dot_general(a, b, (((1,), (1,)), ((), ())), preferred_element_type=f32)
def mm_tn(a, b):
    return lax.dot_general(a, b, (((0,), (0,)), ((), ())), preferred_element_type=f32)

def thirds(x):
    hi = x.astype(bf16)
    rest = x - hi.astype(f32)
    mid = rest.astype(bf16)
    return hi, mid, (rest - mid.astype(f32)).astype(bf16)

def exact_left(mask, x):
    a, b, c = thirds(x)
    return mm(mask, a) + mm(mask, b) + mm(mask, c)

def exact_right(x, mask):
    a, b, c = thirds(x)
    return mm(a, mask) + mm(b, mask) + mm(c, mask)

def sigmoid(x):
    return 1.0 / (1.0 + jnp.exp(-x))

def softplus(x):
    return jnp.maximum(x, 0.0) + jnp.log1p(jnp.exp(-jnp.abs(x)))

def tri(lower):
    r = lax.broadcasted_iota(jnp.int32, (L, L), 0)
    c = lax.broadcasted_iota(jnp.int32, (L, L), 1)
    return jnp.where((r >= c) if lower else (r <= c), 1.0, 0.0).astype(bf16)

def spread(cols, low):
    out = []
    for j in range(3):
        a = jnp.broadcast_to(cols[:, 2 * j : 2 * j + 1], (cols.shape[0], 128))
        b = jnp.broadcast_to(cols[:, 2 * j + 1 : 2 * j + 2], (cols.shape[0], 128))
        out.append(jnp.where(low, a, b))
    return jnp.concatenate(out, 1)

def conv_pre(window, taps):
    total = taps[4:5]
    for k in range(4):
        total = total + taps[k : k + 1] * window[5 + k : 5 + k + L]
    return total

def low_lanes(rows):
    return lax.broadcasted_iota(jnp.int32, (rows, 128), 1) < 64

def head_quantities(dt_raw, heads):
    pre = dt_raw + heads[0:1]
    dt = softplus(pre)
    logs = exact_left(tri(True), dt * heads[1:2])
    return pre, dt, logs

def half_mask(t):
    rows = 128
    r = lax.broadcasted_iota(jnp.int32, (rows, 128 * (t + 1)), 0) + 128 * t
    c = lax.broadcasted_iota(jnp.int32, (rows, 128 * (t + 1)), 1)
    return r >= c

def weights_of(logs, logs_t, h, t):
    w = 128 * (t + 1)
    col = jnp.broadcast_to(logs[128 * t : 128 * (t + 1), h : h + 1], (128, 128))
    if t:
        col = jnp.concatenate([col, col], 1)
    gap = col - logs_t[h : h + 1, :w]
    return jnp.exp(jnp.where(half_mask(t), gap, NEG))

X, GATE, D_GATE, XD, TXD, GROW, TAIL, STEP = (IN * k for k in range(8))
KEYS = 8 * IN
D_ACT = KEYS + 2 * N
KEPT = D_ACT + MIX
SCAN, DT, D_STEP, KEPT_F = 0, IN, IN + N, IN + 2 * N


def fwd_block(window, gates, dt_raw, taps, heads, skip, state, tick, kept, kept_f, kept_h):
    low = low_lanes(L)
    total = conv_pre(window, taps)
    sig = sigmoid(total)
    act = total * sig
    kept[:, pl.ds(D_ACT, MIX)] = (sig + act * (1.0 - sig)).astype(bf16)
    x, keys = act[:, :IN], act[:, IN:].astype(bf16)
    kept[:, pl.ds(X, IN)] = x.astype(bf16)
    kept[:, pl.ds(KEYS, 2 * N)] = keys
    b, c = keys[:, :N], keys[:, N:]
    pre, dt, logs = head_quantities(dt_raw, heads)
    kept_f[:, pl.ds(DT, N)] = dt
    kept_f[:, pl.ds(D_STEP, N)] = sigmoid(pre)
    logs_t = logs.T
    dt_l, logs_l = spread(dt, low), spread(logs, low)
    xd = (dt_l * x).astype(bf16)
    kept[:, pl.ds(STEP, IN)] = dt_l.astype(bf16)
    kept[:, pl.ds(XD, IN)] = xd
    g = mm_nt(c, b)
    rows = [[], []]
    zero = jnp.zeros((), bf16)
    for j in range(3):
        tick(2 + j)
        pair = xd[:, 128 * j : 128 * (j + 1)]
        own = (jnp.where(low, pair, zero), jnp.where(low, zero, pair))
        for t in range(2):
            w = 128 * (t + 1)
            total_y = 0.0
            for e in range(2):
                h = 2 * j + e
                wt = weights_of(logs, logs_t, h, t)
                m = wt * g[128 * t : 128 * (t + 1), :w]
                total_y = total_y + mm(m.astype(bf16), own[e][:w])
                kept_h[h, pl.ds(128 * t, w)] = m.T.astype(bf16)
                for k in range(t + 1):
                    piece = wt[:, 128 * k : 128 * (k + 1)]
                    kept_h[HD + h, pl.ds(128 * (t + k), 128)] = piece.astype(bf16)
            rows[t].append(total_y)
    intra = jnp.concatenate([jnp.concatenate(r, 1) for r in rows], 0)
    grow = jnp.exp(logs_l)
    scan = intra + grow * mm(c, state.astype(bf16))
    last = logs_l[L - 1 : L]
    tails = jnp.exp(last - logs_l)
    txd = (tails * xd.astype(f32)).astype(bf16)
    state = jnp.exp(last) * state + mm_tn(b, txd)
    gsig = sigmoid(gates)
    gate = gates * gsig
    mixed = (scan + skip * x) * gate
    kept[:, pl.ds(GROW, IN)] = grow.astype(bf16)
    kept[:, pl.ds(TAIL, IN)] = tails.astype(bf16)
    kept[:, pl.ds(TXD, IN)] = txd
    kept[:, pl.ds(GATE, IN)] = gate.astype(bf16)
    kept[:, pl.ds(D_GATE, IN)] = (gsig + gate * (1.0 - gsig)).astype(bf16)
    kept_f[:, pl.ds(SCAN, IN)] = scan
    return mixed, state


def bwd_block(window, kept, kept_f, kept_h, taps, heads, skip, gain, state, rnorm, products, g_gated, d_state, after, tick):
    low = low_lanes(L)

    def wide(at, width=IN):
        return kept[:, pl.ds(at, width)]

    x, gate = wide(X).astype(f32), wide(GATE).astype(f32)
    scan = kept_f[:, pl.ds(SCAN, IN)]
    y = scan + skip * x
    mixed = y * gate
    g_mixed = rnorm * (g_gated * gain) - mixed * (rnorm * rnorm * rnorm * products * (1.0 / INNER))
    gain_sum = jnp.sum(g_gated * mixed * rnorm, axis=0, keepdims=True)
    dy = g_mixed * gate
    d_gates = (g_mixed * y * wide(D_GATE).astype(f32)).astype(bf16)
    skip_sum = jnp.sum(dy * x, axis=0, keepdims=True)
    dyb = dy.astype(bf16)
    zero = jnp.zeros((), bf16)
    dg = [0.0, 0.0]
    parts = []
    for j in range(3):
        if j == 1:
            tick(2)
        pair_x = kept[:, pl.ds(XD + 128 * j, 128)]
        pair_y = dyb[:, 128 * j : 128 * (j + 1)]
        own = (jnp.where(low, pair_y, zero), jnp.where(low, zero, pair_y))
        upper, lower = 0.0, 0.0
        for e in range(2):
            h = 2 * j + e
            for t in range(2):
                w = 128 * (t + 1)
                mine = own[e][128 * t : 128 * (t + 1)]
                dm = mm_nt(mine, pair_x[:w])
                pieces = [kept_h[HD + h, pl.ds(128 * (t + k), 128)] for k in range(t + 1)]
                wt = jnp.concatenate(pieces, 1) if t else pieces[0]
                dg[t] = dg[t] + dm * wt.astype(f32)
                back = mm(kept_h[h, pl.ds(128 * t, w)], mine)
                upper = upper + back[:128]
                if t:
                    lower = lower + back[128:]
        parts.append(jnp.concatenate([upper, lower], 0))
    tick(4)
    d_intra = jnp.concatenate(parts, 1)
    b, c = wide(KEYS, N), wide(KEYS + N, N)
    grow, txd = wide(GROW), wide(TXD)
    last = grow[L - 1 : L].astype(f32)
    sb = state.astype(bf16)
    dsb = d_state.astype(bf16)
    edy = (grow.astype(f32) * dy).astype(bf16)
    v = mm(b, dsb)
    dxd = d_intra + wide(TAIL).astype(f32) * v
    dg0, dg1 = dg[0].astype(bf16), dg[1].astype(bf16)
    dc = mm_nt(edy, sb) + jnp.concatenate([mm(dg0, b[:128]), mm(dg1, b)], 0)
    first = mm_tn(dg0, c[:128])
    second = mm_tn(dg1, c[128:])
    db = mm_nt(txd, dsb) + jnp.concatenate([first + second[:128], second[128:]], 0)
    tail_part = txd.astype(f32) * v
    z = dyb.astype(f32) * scan - wide(XD).astype(f32) * d_intra - tail_part
    kept_sum = jnp.sum(state * dsb.astype(f32), axis=0, keepdims=True)
    boundary = last * kept_sum + jnp.sum(tail_part, axis=0, keepdims=True)
    row = lax.broadcasted_iota(jnp.int32, (L, IN), 0)
    z = jnp.where(row == L - 1, z + boundary, z)
    r = lax.broadcasted_iota(jnp.int32, (IN, 128), 0)
    cc = lax.broadcasted_iota(jnp.int32, (IN, 128), 1)
    fold = jnp.where((r // PW) == cc, 1.0, 0.0).astype(bf16)
    g_adt = exact_left(tri(False), exact_right(z, fold))
    direct = exact_right(x * dxd, fold)
    dt = kept_f[:, pl.ds(DT, N)]
    d_pre = (direct + heads[1:2] * g_adt) * kept_f[:, pl.ds(D_STEP, N)]
    decay_sum = jnp.sum(dt * g_adt, axis=0, keepdims=True)
    bias_sum = jnp.sum(d_pre, axis=0, keepdims=True)
    d_state = last * d_state + mm_tn(c, edy)
    dx = wide(STEP).astype(f32) * dxd + skip * dy
    g_pre = jnp.concatenate([dx, db, dc], 1) * wide(D_ACT, MIX).astype(f32)
    longer = jnp.concatenate([g_pre, after], 0)
    d_raw = 0.0
    tap_sums = []
    for k in range(4):
        d_raw = d_raw + taps[k : k + 1] * longer[3 - k : 3 - k + L]
        tap_sums.append(jnp.sum(g_pre * window[5 + k : 5 + k + L], axis=0, keepdims=True))
    tap_sums.append(jnp.sum(g_pre, axis=0, keepdims=True))
    g_all = jnp.concatenate([d_gates, d_raw.astype(bf16), d_pre.astype(bf16)], 1)
    sums = (jnp.concatenate(tap_sums, 0), gain_sum, skip_sum, decay_sum, bias_sum)
    return g_all, d_state, g_pre[:8], sums


class Place:
    def __init__(self):
        dp, mp = lax.axis_index("dp"), lax.axis_index("mp")
        self.dp, self.mp = dp, mp
        self.hi, self.x = mp // 4, mp % 4
        self.lo = 1 - self.hi
        self.ylo, self.z, self.core = dp // 8, (dp // 2) % 4, dp % 2
        self.other_core, self.other_ylo = 1 - self.core, 1 - self.ylo
        self.mine, self.theirs = self.hi * 4, self.lo * 4
        self.xs = [(self.x + k) % 4 for k in range(4)]
        self.row = [self.mine + x for x in self.xs]
        self.far_row = [self.theirs + x for x in self.xs]
        self.right, self.left = (dp, self.row[1]), (dp, self.row[3])
        self.across = (dp, self.far_row[0])
        self.line = [(dp, self.row[k]) for k in (1, 3, 2)]
        self.mate = (dp + 1 - 2 * self.core, mp)
        self.beside_dp = self.at(1 - self.ylo, self.z)
        self.beside = (self.beside_dp, mp)
        self.zs = [(self.z + k) % 4 for k in range(4)]
        self.near_dp = [self.at(self.ylo, z) for z in self.zs]
        self.far_dp = [self.at(1 - self.ylo, z) for z in self.zs]
        self.near_slot = [self.ylo * 4 + z for z in self.zs]
        self.far_slot = [(1 - self.ylo) * 4 + z for z in self.zs]
        self.along = [(self.near_dp[k], mp) for k in (1, 2, 3)]
        self.z_gap = [(z + 3 - self.z) % 4 for z in range(4)]
        self.z_dp = [self.at(self.ylo, z) for z in range(4)]
        self.group = [(dp, (mp + k) % GROUP) for k in range(1, GROUP)]

    def at(self, ylo, z):
        return ylo * 8 + z * 2 + self.core


def greet(peers):
    barrier = pltpu.get_barrier_semaphore()
    for peer in peers:
        pl.semaphore_signal(barrier, inc=1, device_id=peer, device_id_type=MESH)
    return lambda: pl.semaphore_wait(barrier, len(peers))


class View:
    def __init__(self, ref, *chain):
        self.ref, self.chain = ref, chain

    @property
    def at(self):
        return Indexer(self)

    def build(self):
        ref = self.ref
        for index in self.chain:
            ref = ref.at[index]
        return ref

    def __getitem__(self, index):
        return self.build()[index]

    def __setitem__(self, index, value):
        self.build()[index] = value


class Indexer:
    def __init__(self, view):
        self.view = view

    def __getitem__(self, index):
        return View(self.view.ref, *self.view.chain, index)


class Copy:
    def __init__(self, book, make):
        self.book, self.make = book, make
        book.do(lambda: make().start())

    def wait(self):
        self.book.do(lambda: self.make().wait())

    def wait_recv(self):
        self.book.do(lambda: self.make().wait_recv())

    def wait_send(self):
        self.book.do(lambda: self.make().wait_send())


class Sender:
    def __init__(self, send_sem, recv_sem, local_sem):
        self.send_sem, self.recv_sem, self.local_sem = send_sem, recv_sem, local_sem
        self.count, self.started, self.locals, self.kept = 0, [], 0, None

    def do(self, action):
        if self.kept is None:
            action()
        else:
            self.kept.append(action)

    def reserve(self, count):
        self.count += count
        return self.count - count

    def record(self, plan):
        steps = []
        while True:
            self.kept = []
            more = next(plan, self) is not self
            if self.kept:
                steps.append(self.kept)
            if not more:
                self.kept = None
                return steps

    def __call__(self, source, target, peer):
        k = self.count
        self.count += 1
        copy = Copy(
            self,
            lambda: pltpu.make_async_remote_copy(
                src_ref=source.build(),
                dst_ref=target.build(),
                send_sem=self.send_sem.at[k],
                recv_sem=self.recv_sem.at[k],
                device_id=peer,
                device_id_type=MESH,
            ),
        )
        self.started.append(copy)
        return copy

    def local(self, source, target):
        k = self.locals
        self.locals += 1
        return Copy(
            self,
            lambda: pltpu.make_async_copy(source.build(), target.build(), self.local_sem.at[k]),
        )

    def settle(self, copies):
        for copy in copies:
            copy.wait_send()
        self.started = [copy for copy in self.started if copy not in copies]

    def drain(self):
        self.settle(self.started)


def run(actions):
    for action in actions:
        action()


class Table:
    def __init__(self):
        self.rows = {}

    def add(self, block, tick, actions):
        self.rows.setdefault((block, tick), []).extend(actions)

    def ticker(self, block):
        def tick(t):
            if isinstance(block, int):
                run(self.rows.get((block, t), []))
                return
            for k in range(BLOCKS):
                if (k, t) in self.rows:
                    pl.when(block == k)(lambda k=k: run(self.rows[(k, t)]))

        return tick


def gather_unit(send, place, buf, first, second):
    me, lx, rx, ox = place.row[0], place.row[3], place.row[1], place.row[2]
    ym, lxy, rxy = place.far_row[0], place.far_row[3], place.far_row[1]
    right, left, across = place.right, place.left, place.across
    half = PIECE // 2

    def go(block, slot, h, to):
        part = buf.at[block, slot, pl.ds(half * h, half)]
        return send(part, part, to)

    c = [go(second, me, 0, across), go(second, me, 1, across)]
    a = [go(first, me, 0, right), go(first, me, 1, left)]
    a += [go(first, me, 1, right), go(first, me, 0, left)]
    b = [go(second, me, 0, right), go(second, me, 1, left)]
    b += [go(second, me, 1, right), go(second, me, 0, left)]
    y = [go(first, me, 0, across), go(first, me, 1, across)]
    yield
    a[0].wait_recv()
    f = [go(first, lx, 0, right)]
    y.append(go(first, lx, 0, across))
    a[1].wait_recv()
    f.append(go(first, rx, 1, left))
    y.append(go(first, rx, 1, across))
    yield
    a[2].wait_recv()
    y.append(go(first, lx, 1, across))
    a[3].wait_recv()
    y.append(go(first, rx, 0, across))
    yield
    b[0].wait_recv()
    k = [go(second, lx, 0, right)]
    b[1].wait_recv()
    k.append(go(second, rx, 1, left))
    c[0].wait_recv()
    c[1].wait_recv()
    d = [go(second, ym, 0, right), go(second, ym, 1, left)]
    d += [go(second, ym, 1, right), go(second, ym, 0, left)]
    yield
    f[0].wait_recv()
    y.append(go(first, ox, 0, across))
    f[1].wait_recv()
    y.append(go(first, ox, 1, across))
    for copy in b[2:] + y[:2]:
        copy.wait_recv()
    yield
    d[0].wait_recv()
    e = [go(second, lxy, 0, right)]
    d[1].wait_recv()
    e.append(go(second, rxy, 1, left))
    yield
    for copy in d[2:] + k + e + y[2:]:
        copy.wait_recv()
    yield


def row_gather_unit(send, place, buf, first):
    me, lx, rx = place.xs[0], place.xs[3], place.xs[1]

    def go(block, slot, to):
        part = buf.at[block, slot]
        return send(part, part, to)

    a = [go(first, me, place.right), go(first + 1, me, place.left)]
    a += [go(first + 1, me, place.right), go(first, me, place.left)]
    yield
    a[0].wait_recv()
    f = [go(first, lx, place.right)]
    a[1].wait_recv()
    f.append(go(first + 1, rx, place.left))
    yield
    for copy in a[2:] + f:
        copy.wait_recv()
    yield


def weight_steps(send, place, buf):
    def go(slot, peer):
        return send(buf.at[slot], buf.at[slot], peer)

    own, other = place.dp, place.beside_dp
    one = go(own, place.beside)
    near = [go(own, peer) for peer in place.along]
    mates = [go(own, place.mate)]
    yield
    one.wait_recv()
    far = [go(other, peer) for peer in place.along]
    mates.append(go(other, place.mate))
    yield
    for k in range(3):
        near[k].wait_recv()
        mates.append(go(place.near_dp[3 - k], place.mate))
    yield
    for k in range(3):
        far[k].wait_recv()
        mates.append(go(place.far_dp[3 - k], place.mate))
    yield
    for copy in mates:
        copy.wait_recv()
    yield


def add_into(send, target, other):
    def action():
        target[...] = target[...] + other[...]

    send.do(action)


def put(send, target, index, value):
    def action():
        target[index] = value()

    send.do(action)


def scatter_unit(send, place, buf, first, second, y_in, x_in, xx_in, t_out, t_in, total):
    right, left, across = place.right, place.left, place.across
    half = PIECE // 2
    mine, theirs = place.row, place.far_row
    order = (2, 1, 3, 0)

    def first_hop(k, block, side):
        slot = side[2]
        return [
            send(buf.at[block, slot, pl.ds(0, half)], x_in.at[k, 0], right),
            send(buf.at[block, slot, pl.ds(half, half)], x_in.at[k, 1], left),
        ]

    def second_hop(k, block, side, hops):
        hops[0].wait_recv()
        add_into(send, buf.at[block, side[1], pl.ds(0, half)], x_in.at[k, 0])
        one = send(buf.at[block, side[1]], xx_in.at[k, 0], right)
        hops[1].wait_recv()
        add_into(send, buf.at[block, side[3], pl.ds(half, half)], x_in.at[k, 1])
        return [one, send(buf.at[block, side[3]], xx_in.at[k, 1], left)]

    def three(k, block, side):
        return (
            buf[block, side[0]].astype(f32) + xx_in[k, 0].astype(f32) + xx_in[k, 1].astype(f32)
        )

    ahead = [send(buf.at[first, theirs[n]], y_in.at[k], across) for k, n in enumerate(order)]
    hop_t = first_hop(1, second, theirs)
    hop_m = first_hop(2, second, mine)
    yield
    two_t = second_hop(1, second, theirs, hop_t)
    yield
    ahead[0].wait_recv()
    add_into(send, buf.at[first, mine[2]], y_in.at[0])
    hop_a = first_hop(0, first, mine)
    two_m = second_hop(2, second, mine, hop_m)
    yield
    for copy in two_t:
        copy.wait_recv()
    put(send, t_out, ..., lambda: three(1, second, theirs).astype(bf16))
    last = send(t_out, t_in, across)
    yield
    for k in range(1, 4):
        ahead[k].wait_recv()
        add_into(send, buf.at[first, mine[order[k]]], y_in.at[k])
    two_a = second_hop(0, first, mine, hop_a)
    yield
    for copy in two_m + [last]:
        copy.wait_recv()
    put(send, total, second, lambda: three(2, second, mine) + t_in[...].astype(f32))
    yield
    for copy in two_a:
        copy.wait_recv()
    put(send, total, first, lambda: three(0, first, mine))
    yield


def row_scatter_unit(send, place, buf, first, x_in, xx_in, keep):
    xs = place.xs
    hops = [
        send(buf.at[first, xs[2]], x_in.at[0], place.right),
        send(buf.at[first + 1, xs[2]], x_in.at[1], place.left),
    ]
    yield
    hops[0].wait_recv()
    add_into(send, buf.at[first, xs[1]], x_in.at[0])
    two = [send(buf.at[pl.ds(first, 2), xs[1]], xx_in.at[0], place.right)]
    hops[1].wait_recv()
    add_into(send, buf.at[first + 1, xs[3]], x_in.at[1])
    two.append(send(buf.at[pl.ds(first, 2), xs[3]], xx_in.at[1], place.left))
    yield
    for copy in two:
        copy.wait_recv()

    def last(k):
        total = buf[first + k, xs[0]].astype(f32)
        keep(first + k, total + xx_in[0, k].astype(f32) + xx_in[1, k].astype(f32))

    for k in range(2):
        send.do(lambda k=k: last(k))
    yield


class Reduction:
    def __init__(self, send, place, grads, core_in, z_in, y_out, w_in, keep):
        self.send, self.place, self.grads, self.core_in = send, place, grads, core_in
        self.z_in, self.y_out, self.w_in, self.keep = z_in, y_out, w_in, keep
        self.swaps, self.base = {}, send.reserve(8)

    def swap(self, i):
        pairs = pl.ds(2 * i, 2)
        part = self.grads.at[pairs, self.place.other_core]
        self.swaps[i] = self.send(part, self.core_in.at[pairs], self.place.mate)

    def hop(self, k, y, slot, peer):
        at = self.base + 2 * k + y
        return pltpu.make_async_remote_copy(
            src_ref=self.grads.at[slot, self.place.core].build(),
            dst_ref=self.z_in.at[k, y].build(),
            send_sem=self.send.send_sem.at[at],
            recv_sem=self.send.recv_sem.at[at],
            device_id=peer,
            device_id_type=MESH,
        )

    def fold(self, i):
        place = self.place
        self.swaps[i].wait_recv()
        for slot in (2 * i, 2 * i + 1):
            add_into(self.send, self.grads.at[slot, place.core], self.core_in.at[slot])
            y, z = slot // 4, slot % 4

            def action(slot=slot, y=y, z=z):
                k, peer = place.z_gap[z], (place.z_dp[z], place.mp)
                pl.when(place.z != z)(lambda: self.hop(k, y, slot, peer).start())

            self.send.do(action)

    def arrive(self, y):
        for k in range(3):
            self.send.do(lambda k=k: self.hop(k, y, 0, self.place.along[k]).wait_recv())

    def joined(self, y, slot):
        total = self.grads[slot, self.place.core].astype(f32)
        for k in range(3):
            total = total + self.z_in[k, y].astype(f32)
        return total

    def cross(self):
        y, slot = self.place.other_ylo, self.place.far_slot[0]
        self.arrive(y)
        put(self.send, self.y_out, ..., lambda: self.joined(y, slot).astype(bf16))
        self.crossed = self.send(self.y_out, self.w_in, self.place.beside)

    def end(self):
        y, slot = self.place.ylo, self.place.near_slot[0]
        self.arrive(y)
        self.crossed.wait_recv()
        self.send.do(lambda: self.keep(self.joined(y, slot) + self.w_in[...].astype(f32)))

    def settle(self):
        for k in range(3):
            for y in range(2):
                self.hop(k, y, 0, self.place.along[k]).wait_send()


def rows(block, count=L):
    return pl.ds(pl.multiple_of(block * count, count), count)


def pick(columns, block):
    lane = lax.broadcasted_iota(jnp.int32, columns.shape, 1)
    return jnp.sum(jnp.where(lane == block, columns, 0.0), axis=1, keepdims=True)


def parameters(channel_terms, side_terms, head_terms, taps, heads, skip, gain):
    taps[pl.ds(0, CONV + 1), pl.ds(0, IN)] = channel_terms[pl.ds(0, CONV + 1)]
    taps[pl.ds(0, CONV + 1), pl.ds(IN, 2 * N)] = side_terms[...]
    taps[pl.ds(CONV + 1, 3)] = jnp.zeros((3, MIX), f32)
    gain[...] = channel_terms[pl.ds(CONV + 1, 1)]
    wide = jnp.concatenate([head_terms[...], jnp.zeros((3, N - HD), f32)], 1)
    lane = lax.broadcasted_iota(jnp.int32, (1, N), 1)
    decay = jnp.where(lane < HD, -jnp.exp(wide[1:2]), 0.0)
    heads[...] = jnp.concatenate([wide[0:1], decay, jnp.zeros((6, N), f32)], 0)
    skip[...] = spread(jnp.broadcast_to(wide[2:3], (8, N)), low_lanes(8))[0:1]


def valid_rows(seq_len, place, block):
    row = lax.broadcasted_iota(jnp.int32, (PIECE, 1), 0)
    position = row + (place.mp * PIECE + block * L)
    return jnp.where(position < seq_len[...], 1.0, 0.0)


def front_kernel(
    tokens, grad_out, seq_len, norm_gain, main_weight, side_weight, output_weight,
    channel_terms, side_terms, head_terms,
    whole_o, weights_o, out_o, back_o, raw_o, kept_o, kept_f_o, kept_h_o, states_o, g_gated_o, gated_o, sums,
    whole, weights, out, back, raw, states, g_gated, gated, gates, steps, kept, kept_f, kept_h, mixed, halves,
    taps, heads, skip, gain, squares, state, inbox, send_sem, recv_sem, local_sem,
):
    (
        tokens, grad_out, seq_len, norm_gain, main_weight, side_weight, output_weight,
        channel_terms, side_terms, head_terms, whole_o, weights_o, out_o, back_o, raw_o,
        kept_o, kept_f_o, kept_h_o, states_o, g_gated_o, gated_o, sums, whole, weights, out,
        back, raw, states, g_gated, gated, gates, steps, kept, kept_f, kept_h, mixed,
        halves, taps, heads, skip, gain, squares, state, inbox,
    ) = map(
        View,
        (
            tokens, grad_out, seq_len, norm_gain, main_weight, side_weight, output_weight,
            channel_terms, side_terms, head_terms, whole_o, weights_o, out_o, back_o, raw_o,
            kept_o, kept_f_o, kept_h_o, states_o, g_gated_o, gated_o, sums, whole, weights, out,
            back, raw, states, g_gated, gated, gates, steps, kept, kept_f, kept_h, mixed,
            halves, taps, heads, skip, gain, squares, state, inbox,
        ),
    )
    place = Place()
    meet = greet(place.group + [place.mate, place.beside] + place.along)
    scale_row = norm_gain[...].reshape(1, D)
    for i in range(BLOCKS):
        x = tokens[i].astype(f32)
        scale = lax.rsqrt(jnp.mean(x * x, axis=1, keepdims=True) + epsilon)
        whole[i, place.mp] = (x * scale * scale_row).astype(bf16)
    columns = weights.at[place.dp]
    for k in range(2):
        columns[:, pl.ds(k * IN, IN)] = main_weight[:, k].astype(bf16)
    columns[:, pl.ds(2 * IN, 2 * N)] = side_weight[:, pl.ds(0, 2 * N)]
    source = lax.broadcasted_iota(jnp.int32, (HEADS, N), 0)
    lane = lax.broadcasted_iota(jnp.int32, (HEADS, N), 1)
    spot = jnp.where((source == lane + HD * place.mp) & (lane < HD), 1.0, 0.0).astype(bf16)
    own_steps = mm(side_weight[:, pl.ds(2 * N, HEADS)], spot)
    columns[:, pl.ds(2 * IN + 2 * N, N)] = own_steps.astype(bf16)
    out[place.dp, :, pl.ds(0, IN)] = output_weight[...]
    meet()
    send = Sender(send_sem, recv_sem, local_sem)
    units = [send.record(gather_unit(send, place, whole, 2 * u, 2 * u + 1)) for u in range(4)]
    cols = send.record(weight_steps(send, place, weights))
    outs = send.record(weight_steps(send, place, out))
    backs = [send.record(row_gather_unit(send, place, back, 2 * u)) for u in range(4)]

    run(cols[0])
    own_out = out.at[place.dp, :, pl.ds(0, IN)]
    pair = send(own_out, out.at[place.dp, :, pl.ds(IN, IN)], place.across)
    for unit in units:
        run(unit[0])
    for i in range(BLOCKS):
        rounded = valid_rows(seq_len, place, i) * grad_out[i].astype(f32)
        back[i, place.xs[0]] = rounded.astype(bf16)
    parameters(channel_terms, side_terms, head_terms, taps, heads, skip, gain)
    raw[pl.ds(0, 8)] = jnp.zeros((8, MIX), f32)
    state[...] = jnp.zeros((N, IN), f32)
    squares[...] = jnp.zeros((L, 128), f32)

    def project_rows(device, first=0, count=BLOCKS):
        block = whole[pl.ds(first, count), device].reshape(count * PIECE, D)
        both = mm(block, weights[...].reshape(D, COLS))
        for i in range(count):
            part = both[i * PIECE : (i + 1) * PIECE]
            start = (first + i) * L + device * PIECE
            at = pl.ds(pl.multiple_of(start, PIECE), PIECE)
            gates[at] = part[:, :IN]
            steps[at] = part[:, IN + MIX :]
            raw[pl.ds(pl.multiple_of(start + 8, 8), PIECE)] = part[:, IN : IN + MIX]

    far = (place.row[2], place.far_row[3], place.far_row[1], place.far_row[2])

    def early(k):
        run(units[0][k] + units[1][k])

    def late(k):
        run(units[2][k] + units[3][k])

    early(1)
    run(cols[1])
    early(2)
    late(1)
    pair.wait_recv()
    run(outs[0] + cols[2])
    for back_unit in backs:
        run(back_unit[0])
    early(3)
    late(2)
    run(cols[3])
    early(4)
    late(3)
    run(cols[4])
    project_rows(place.row[0])
    early(5)
    late(4)
    project_rows(place.row[3])
    run(outs[1])
    project_rows(place.row[1])
    early(6)
    late(5)
    project_rows(place.far_row[0])
    run(backs[0][1] + backs[1][1])
    for device in far:
        project_rows(device, 0, 4)
    stored = []

    def second_half():
        for device in far:
            project_rows(device, 4, 4)

    def store_early():
        stored.append(send.local(whole, whole_o))
        stored.append(send.local(weights, weights_o))
        yield

    lane = lax.broadcasted_iota(jnp.int32, (L, 128), 1)
    crossing = [None] * 4

    def project(u):
        pairs = pl.ds(2 * u, 2)

        def action():
            both = mm(back[pairs].reshape(L, D), out[...].reshape(D, 2 * IN)).astype(bf16)
            g_gated[pairs, place.hi] = both[:, :IN].reshape(2, L // 2, IN)
            halves[pairs] = both[:, IN:].reshape(2, L // 2, IN)

        send.do(action)
        crossing[u] = send(halves.at[pairs], g_gated.at[pairs, place.hi], place.across)
        yield

    projections = [send.record(project(u))[0] for u in range(4)]
    def store_out():
        stored.append(send.local(out, out_o))
        yield

    table = Table()
    for block, tick, actions in (
        (0, 2, backs[2][1] + backs[3][1] + outs[2]),
        (0, 5, units[2][6]),
        (1, 3, units[3][6] + outs[3]),
        (2, 3, outs[4]),
        (2, 5, backs[0][2] + projections[0]),
        (3, 5, [second_half] + send.record(store_early())[0]),
        (4, 2, backs[1][2] + projections[1]),
        (5, 2, send.record(store_out())[0]),
        (6, 2, backs[2][2] + projections[2]),
    ):
        table.add(block, tick, actions)

    def block_copies(i):
        slot = lax.rem(i, 2)
        below = pl.ds(pl.multiple_of(i * L + 8, 8), L)
        pairs = [
            (raw.at[below], raw_o.at[below]),
            (kept.at[slot], kept_o.at[i]),
            (kept_f.at[slot], kept_f_o.at[i]),
            (kept_h.at[slot], kept_h_o.at[i]),
            (states.at[i], states_o.at[i]),
        ]
        return [
            pltpu.make_async_copy(source.build(), target.build(), local_sem.at[16 + 5 * slot + k])
            for k, (source, target) in enumerate(pairs)
        ]

    def block_wait(i):
        for copy in block_copies(i):
            copy.wait()

    def body(i, carry):
        tick = table.ticker(i)
        at = rows(i)
        slot = lax.rem(i, 2)
        pl.when(i >= 2)(lambda: block_wait(i - 2))
        states[i] = state[...]
        window = raw[pl.ds(pl.multiple_of(i * L, 8), L + 8)]
        outer, following = fwd_block(
            window, gates[at], steps[at], taps[...], heads[...], skip[...], state[...], tick,
            kept.at[slot], kept_f.at[slot], kept_h.at[slot],
        )
        mixed[at] = outer
        state[...] = following
        square = jnp.sum(outer * outer, axis=1, keepdims=True)
        squares[...] = jnp.where(lane == i, square, squares[...])
        for copy in block_copies(i):
            copy.start()
        tick(5)
        return carry

    lax.fori_loop(0, BLOCKS, body, 0)
    inbox[place.mp] = squares[...].T[:8]
    copies = [send(inbox.at[place.mp], inbox.at[place.mp], peer) for peer in place.group]
    stored.append(send.local(raw.at[pl.ds(0, 8)], raw_o.at[pl.ds(0, 8)]))
    run(backs[3][2] + projections[3])
    stored.append(send.local(back, back_o))
    for copy in copies:
        copy.wait_recv()
    total = inbox[0]
    for k in range(1, GROUP):
        total = total + inbox[k]
    top = lax.rsqrt(total * (1.0 / INNER) + epsilon)
    scales = jnp.concatenate([top, jnp.zeros((120, L), f32)], 0).T
    for i in range(BLOCKS):
        rounded = (mixed[pl.ds(i * L, L)] * scales[:, i : i + 1] * gain[...]).astype(bf16)
        gated[i] = rounded.reshape(2, L // 2, IN)
    stored.append(send.local(gated, gated_o))

    def products(u, scales):
        crossing[u].wait_recv()
        for i in (2 * u, 2 * u + 1):
            part = g_gated[i].reshape(L, IN).astype(f32) * gain[...] * mixed[pl.ds(i * L, L)]
            product = jnp.sum(part, axis=1, keepdims=True)
            scales = jnp.where(lane == i + 8, product, scales)
        return scales

    for u in range(4):
        scales = products(u, scales)
    sums[...] = scales
    stored.append(send.local(g_gated, g_gated_o))
    for copy in stored:
        copy.wait()

    block_wait(jnp.int32(BLOCKS - 2))
    block_wait(jnp.int32(BLOCKS - 1))
    send.drain()


def back_kernel(
    whole_i, weights_i, out_i, back_i, raw_i, kept_i, kept_f_i, kept_h_i, states_i, g_gated_i, gated_i,
    sums, tokens, grad_out, seq_len, norm_gain, channel_terms, side_terms, head_terms,
    layer_out, token_grad, gain_grad, main_grad, side_grad, out_grad, conv_grad, channel_grad, head_grad,
    weights, out, gated, raw, kept, kept_f, kept_h, states, g_gated, whole, g_all, left,
    row_parts, row_x, row_xx, parts, y_in, x_in, xx_in, t_out, t_in,
    grads, core_in, z_in, y_out, w_in, s_core, s_z, s_out, s_in, o_core, o_z, o_out, o_in, pair_out, pair_in,
    taps, heads, skip, gain, columns, totals, d_state, after, gain_part,
    products_box, share_box, side_own, side_in, side_box, sums_box, send_sem, recv_sem, local_sem,
):
    (
        whole_i, weights_i, out_i, back_i, raw_i, kept_i, kept_f_i, kept_h_i, states_i,
        g_gated_i, gated_i, sums, tokens, grad_out, seq_len, norm_gain, channel_terms,
        side_terms, head_terms, layer_out, token_grad, gain_grad, main_grad, side_grad,
        out_grad, conv_grad, channel_grad, head_grad, weights, out, gated, raw, kept,
        kept_f, kept_h, states, g_gated, whole, g_all, left, row_parts, row_x, row_xx,
        parts, y_in, x_in, xx_in, t_out, t_in, grads, core_in, z_in, y_out, w_in, s_core,
        s_z, s_out, s_in, o_core, o_z, o_out, o_in, pair_out, pair_in, taps, heads, skip,
        gain, columns, totals, d_state, after, gain_part, products_box, share_box, side_own,
        side_in, side_box, sums_box,
    ) = map(
        View,
        (
            whole_i, weights_i, out_i, back_i, raw_i, kept_i, kept_f_i, kept_h_i, states_i,
            g_gated_i, gated_i, sums, tokens, grad_out, seq_len, norm_gain, channel_terms,
            side_terms, head_terms, layer_out, token_grad, gain_grad, main_grad, side_grad,
            out_grad, conv_grad, channel_grad, head_grad, weights, out, gated, raw, kept,
            kept_f, kept_h, states, g_gated, whole, g_all, left, row_parts, row_x, row_xx,
            parts, y_in, x_in, xx_in, t_out, t_in, grads, core_in, z_in, y_out, w_in, s_core,
            s_z, s_out, s_in, o_core, o_z, o_out, o_in, pair_out, pair_in, taps, heads, skip,
            gain, columns, totals, d_state, after, gain_part, products_box, share_box, side_own,
            side_in, side_box, sums_box,
        ),
    )
    place = Place()
    meet = greet(place.group + [place.mate, place.beside] + place.along)
    send = Sender(send_sem, recv_sem, local_sem)

    def loads(i, slot):
        return [
            (raw_i.at[pl.ds(pl.multiple_of(i * L, 8), L + 8)], raw.at[slot]),
            (kept_i.at[i], kept.at[slot]),
            (kept_f_i.at[i], kept_f.at[slot]),
            (kept_h_i.at[i], kept_h.at[slot]),
            (states_i.at[i], states.at[slot]),
            (g_gated_i.at[i], g_gated.at[slot]),
        ]

    def load(i, slot, start):
        for k, (source, target) in enumerate(loads(i, slot)):
            copy = pltpu.make_async_copy(
                source.build(), target.build(), local_sem.at[16 + 6 * slot + k]
            )
            if start:
                copy.start()
            else:
                copy.wait()

    def known_rows(i):
        return pltpu.make_async_copy(whole_i.at[i].build(), whole.build(), local_sem.at[28])

    load(BLOCKS - 1, 1, True)
    known_rows(BLOCKS - 1).start()
    first = [
        send.local(gated_i.at[:, place.hi], gated.at[:, :, pl.ds(0, IN)]),
        send.local(out_i, out),
        send.local(weights_i, weights),
    ]
    load(BLOCKS - 2, 0, True)
    products_box[place.mp] = sums[...].T[8:16]
    meet()
    product_copies = [
        send(products_box.at[place.mp], products_box.at[place.mp], peer) for peer in place.group
    ]
    crossing = [
        send(
            gated_i.at[pl.ds(2 * u, 2), place.lo],
            gated.at[pl.ds(2 * u, 2), :, pl.ds(IN, IN)],
            place.across,
        )
        for u in (3, 2, 1, 0)
    ][::-1]
    parameters(channel_terms, side_terms, head_terms, taps, heads, skip, gain)
    d_state[...] = jnp.zeros((N, IN), f32)
    after[...] = jnp.zeros((8, MIX), f32)
    totals[...] = jnp.zeros((8, 2 * IN), f32)
    gain_part[...] = jnp.zeros((1, D), f32)
    columns[...] = sums[...]

    def late_products():
        for copy in product_copies:
            copy.wait_recv()
        total = products_box[0]
        for k in range(1, GROUP):
            total = total + products_box[k]
        summed = jnp.concatenate([jnp.zeros((8, L), f32), total, jnp.zeros((112, L), f32)], 0).T
        lane = lax.broadcasted_iota(jnp.int32, (L, 128), 1)
        columns[...] = jnp.where(lane >= 8, summed, columns[...])

    late_products()

    for copy in first:
        copy.wait()

    def keep_layer(i, total):
        layer_out[i] = (
            tokens[i].astype(f32) + valid_rows(seq_len, place, i) * total
        ).astype(bf16)

    def row_plan(u):
        def action():
            pairs = pl.ds(2 * u, 2)
            part = mm_nt(gated[pairs].reshape(L, 2 * IN), out[...].reshape(D, 2 * IN))
            row_parts[pairs] = part.astype(bf16).reshape(2, 4, PIECE, D)

        crossing[u].wait_recv()
        yield
        send.do(action)
        yield from row_scatter_unit(
            send, place, row_parts, 2 * u, row_x.at[u], row_xx.at[u], keep_layer
        )

    def keep_out(total):
        pair_out[...] = total[:, IN:]
        out_grad[...] = total[:, :IN]

    def keep_main(total):
        main_grad[:, 0] = total[:, :IN]
        main_grad[:, 1] = total[:, IN:]

    def keep_side(total):
        turned = total[:, 2 * N :].T[:16]
        blank = jnp.zeros((16, 2 * N - D // DP), f32)
        side_own[pl.ds(0, D // DP)] = total[:, : 2 * N].astype(bf16)
        side_own[pl.ds(D // DP, 16)] = jnp.concatenate([turned, blank], 1).astype(bf16)

    main_part = grads.at[:, :, :, pl.ds(0, 2 * IN)]
    side_part = grads.at[:, :, :, pl.ds(2 * IN, 3 * N)]
    out_sum = Reduction(send, place, main_part, o_core, o_z, o_out, o_in, keep_out)
    main_sum = Reduction(send, place, main_part, core_in, z_in, y_out, w_in, keep_main)
    side_sum = Reduction(send, place, side_part, s_core, s_z, s_out, s_in, keep_side)

    def out_plan():
        chunks = [
            send.local(
                back_i.at[:, :, :, pl.ds(i * 384, 384)], left.at[i, :, pl.ds(0, 4)]
            )
            for i in range(2)
        ]
        yield
        for i in range(4):
            chunks[i].wait()

            def action(i=i):
                side = left[i % 2, :, pl.ds(0, 4)].reshape(BLOCKS * L // 2, 384)
                pairs = pl.ds(2 * i, 2)
                part = mm_tn(side, gated[...].reshape(BLOCKS * L // 2, 2 * IN))
                grads[pairs, :, :, : 2 * IN] = part.astype(bf16).reshape(2, 2, 96, 2 * IN)

            send.do(action)
            if i < 2:
                chunks.append(
                    send.local(
                        back_i.at[:, :, :, pl.ds((i + 2) * 384, 384)],
                        left.at[i, :, pl.ds(0, 4)],
                    )
                )
            out_sum.swap(i)
            if i == 3:
                whole_loads.append(load_whole(0))
                whole_loads.append(load_whole(1))
            yield
        for i in range(4):
            out_sum.fold(i)
        yield
        out_sum.cross()
        yield
        out_sum.end()
        pair = send(pair_out, pair_in, place.across)
        yield
        pair.wait_recv()

        def finish():
            out_grad[...] += pair_in[...]

        send.do(finish)
        yield

    whole_loads = []

    def load_whole(i):
        return send.local(whole_i.at[:, :, :, pl.ds(i * 384, 384)], left.at[i % 2])

    row_units = [send.record(row_plan(u)) for u in range(4)]
    outs = send.record(out_plan())

    def final_rows(i):
        gain_row = norm_gain[...].reshape(1, D)
        x = tokens[i].astype(f32)
        s = lax.rsqrt(jnp.mean(x * x, axis=1, keepdims=True) + epsilon)
        g = token_grad[i]
        dot = jnp.sum(g * gain_row * x, axis=1, keepdims=True)
        token_grad[i] = grad_out[i].astype(f32) + s * gain_row * g - x * (s * s * s * dot * (1.0 / D))

    units = [
        send.record(
            scatter_unit(
                send, place, parts, 2 * u, 2 * u + 1,
                y_in.at[u], x_in.at[u], xx_in.at[u], t_out.at[u], t_in.at[u], token_grad,
            )
        )
        for u in range(4)
    ]
    for u in range(4):
        units[u][6] += [lambda i=2 * u + k: final_rows(i) for k in range(2)]

    table = Table()
    for block, tick, actions in (
        (0, 0, row_units[3][0]),
        (0, 0, row_units[3][1]),
        (0, 6, row_units[2][0]),
        (0, 6, row_units[2][1]),
        (1, 4, row_units[3][2]),
        (1, 6, units[3][0]),
        (1, 6, outs[0]),
        (2, 2, row_units[1][0]),
        (2, 2, row_units[0][0]),
        (2, 4, outs[1]),
        (2, 4, row_units[2][2]),
        (2, 6, outs[2]),
        (3, 2, outs[3]),
        (3, 4, units[3][1]),
        (3, 4, row_units[3][3]),
        (3, 5, units[3][2]),
        (3, 5, outs[4]),
        (3, 6, units[2][0]),
        (4, 0, row_units[2][3]),
        (4, 2, units[3][3]),
        (4, 2, outs[5]),
        (4, 6, units[3][4]),
        (4, 6, row_units[1][1]),
        (5, 4, units[2][1]),
        (5, 5, units[2][2]),
        (5, 6, units[3][5]),
        (5, 6, units[1][0]),
        (6, 0, units[2][3]),
        (6, 0, row_units[1][2]),
        (6, 5, units[3][6]),
        (6, 5, row_units[0][1]),
        (6, 6, units[2][4]),
        (6, 6, outs[6]),
        (7, 4, units[1][1]),
        (7, 5, units[1][2]),
        (7, 5, outs[7]),
        (7, 6, units[2][5]),
        (7, 6, units[0][0]),
    ):
        table.add(block, tick, actions)

    def body(j):
        tick = table.ticker(j)
        i = BLOCKS - 1 - j
        slot = i % 2
        tick(0)
        load(i, slot, False)
        g, ds, top, found = bwd_block(
            raw[slot], kept.at[slot], kept_f.at[slot], kept_h.at[slot],
            taps[...], heads[...], skip[...], gain[...],
            states[slot], pick(columns[...], i), pick(columns[...], i + 8),
            g_gated[slot].reshape(L, IN).astype(f32), d_state[...], after[...], tick,
        )
        g_all[rows(i)] = g
        d_state[...] = ds
        after[...] = top
        tap_sums, gain_sum, skip_sum, decay_sum, bias_sum = found
        blank = jnp.zeros((1, IN), f32)
        fill = jnp.zeros((1, IN - 2 * N), f32)
        totals[...] += jnp.concatenate(
            [
                jnp.concatenate([tap_sums, jnp.zeros((CONV + 1, 2 * IN - MIX), f32)], 1),
                jnp.concatenate([gain_sum, blank], 1),
                jnp.concatenate([skip_sum, blank], 1),
                jnp.concatenate([decay_sum, bias_sum, fill, blank], 1),
            ],
            0,
        )
        tick(5)
        part = mm_nt(g, weights[...].reshape(D, COLS)).astype(bf16)
        parts[i] = part.reshape(GROUP, PIECE, D)
        known_rows(i).wait()
        product = part * whole[...].reshape(L, D)
        gain_part[...] += mm(jnp.ones((8, L), bf16), product)[0:1]
        if i >= 1:
            known_rows(i - 1).start()
        if i >= 2:
            load(i - 2, slot, True)
        tick(6)

    for block in range(BLOCKS):
        body(block)

    gain_sum = gain_part[...] / norm_gain[...].reshape(1, D)
    narrow = [gain_sum[:, k * N : (k + 1) * N] for k in range(CONV + 1)]
    start = (CONV + 1) * N
    broad = [gain_sum[:, start : start + IN], gain_sum[:, start + IN : start + 2 * IN]]
    rest = gain_sum[:, start + 2 * IN :]
    broad.append(jnp.concatenate([rest, jnp.zeros((1, 3 * IN - D + start), f32)], 1))
    found = totals[...]
    upper = jnp.concatenate([found[: CONV + 1, :MIX], jnp.concatenate(narrow, 0)], 1)
    lower = jnp.concatenate([found[CONV + 1 :, :IN], jnp.concatenate(broad, 0)], 1)
    sums_box[0] = jnp.concatenate([upper, lower], 0)
    stage = [send(sums_box.at[0], sums_box.at[1], place.mate)]
    send.settle(list(out_sum.swaps.values()))
    out_sum.settle()
    late = [
        units[1][3] + row_units[0][2] + units[2][6],
        units[0][1] + units[0][2] + row_units[1][3],
        units[1][4] + units[0][3],
        units[1][5],
        units[0][4] + units[1][6],
        units[0][5] + units[0][6],
        row_units[0][3],
    ]

    def whole_chunk(load, slot):
        whole_loads[load].wait()
        return left[slot].reshape(BLOCKS * L, 384)

    def side_chunk(i):
        pairs = pl.ds(2 * i, 2)
        part = mm_tn(whole_chunk(i, i % 2), g_all[:, pl.ds(2 * IN, 3 * N)]).astype(bf16)
        grads[pairs, :, :, 2 * IN :] = part.reshape(2, 2, 96, 3 * N)
        side_sum.swap(i)

    def main_chunk(i, load=None):
        pairs = pl.ds(2 * i, 2)
        if load is not None:
            whole_loads[load].wait()
        side = left[i % 2].reshape(BLOCKS * L, 384)
        part = mm_tn(side, g_all[:, pl.ds(0, 2 * IN)]).astype(bf16)
        grads[pairs, :, :, : 2 * IN] = part.reshape(2, 2, 96, 2 * IN)
        main_sum.swap(i)

    side_chunk(0)
    whole_loads.append(load_whole(2))
    side_chunk(1)
    whole_loads.append(load_whole(3))
    run(late[0])
    side_chunk(2)
    stage[0].wait_recv()
    sums_box[2] = sums_box[0] + sums_box[1]
    stage = [send(sums_box.at[2], sums_box.at[3 + k], peer) for k, peer in enumerate(place.along)]
    side_chunk(3)
    run(late[1])
    main_chunk(2)
    whole_loads.append(load_whole(0))
    for i in range(4):
        side_sum.fold(i)
    main_chunk(3)
    whole_loads.append(load_whole(1))
    run(late[2])
    for copy in stage:
        copy.wait_recv()
    sums_box[6] = sums_box[2] + sums_box[3] + sums_box[4] + sums_box[5]
    stage = [send(sums_box.at[6], sums_box.at[7], place.beside)]
    main_chunk(0, 4)
    main_sum.fold(2)
    main_sum.fold(3)
    run(late[3])
    main_chunk(1, 5)
    main_sum.fold(0)
    side_sum.cross()
    main_sum.fold(1)
    run(late[4])
    side_sum.end()
    pair = send(side_own, side_in, place.across)
    main_sum.cross()
    pair.wait_recv()
    total = side_own[pl.ds(0, D // DP)].astype(f32) + side_in[pl.ds(0, D // DP)].astype(f32)
    side_box[place.x, pl.ds(0, D // DP)] = total.astype(bf16)
    side_box[place.x, pl.ds(D // DP, 16)] = side_own[pl.ds(D // DP, 16)]
    side_box[place.x, pl.ds(D // DP + 16, 16)] = side_in[pl.ds(D // DP, 16)]
    sides = [send(side_box.at[place.x], side_box.at[place.x], peer) for peer in place.line]
    stage[0].wait_recv()
    copied = sums_box[6] + sums_box[7]
    share_box[place.mp] = copied[:, IN:]
    shares = [send(share_box.at[place.mp], share_box.at[place.mp], peer) for peer in place.group]
    channel_grad[...] = copied[: CONV + 2, :IN]
    r = lax.broadcasted_iota(jnp.int32, (IN, N), 0)
    c = lax.broadcasted_iota(jnp.int32, (IN, N), 1)
    fold = jnp.where((r // PW) == c, 1.0, 0.0).astype(bf16)
    skips = exact_right(jnp.broadcast_to(copied[CONV + 2 : CONV + 3, :IN], (8, IN)), fold)
    decays = heads[pl.ds(1, 1)] * copied[CONV + 3 :, :N]
    biases = copied[CONV + 3 :, N : 2 * N]
    head_grad[...] = jnp.concatenate([biases, decays, skips[0:1]], 0)[:, :HD]
    run(late[5])

    for copy in shares:
        copy.wait_recv()
    shared = share_box[0]
    for k in range(1, GROUP):
        shared = shared + share_box[k]
    conv_grad[...] = shared[: CONV + 1, : 2 * N]
    for k in range(CONV + 1):
        gain_grad[pl.ds(k * N, N)] = shared[k, 2 * N :]
    for k in range(3):
        width = min(IN, D - start - k * IN)
        gain_grad[pl.ds(start + k * IN, width)] = shared[CONV + 1 + k, :width]
    run(late[6])
    run(outs[8])
    main_sum.end()
    for copy in sides:
        copy.wait_recv()
    both, steps_sum = 0.0, 0.0
    lane = lax.broadcasted_iota(jnp.int32, (16, N), 1)
    source = lax.broadcasted_iota(jnp.int32, (16, N), 0)
    for k in range(4):
        both = both + side_box[k, pl.ds(0, D // DP)].astype(f32)
        for at, first in ((D // DP, place.mine), (D // DP + 16, place.theirs)):
            spot = (lane == source + HD * (first + k)) & (source < HD)
            turned = side_box[k, pl.ds(at, 16), pl.ds(0, N)]
            picked = mm_tn(turned, jnp.where(spot, 1.0, 0.0).astype(bf16))
            steps_sum = steps_sum + picked[: D // DP]
    side_grad[...] = jnp.concatenate([both, steps_sum], 1)[:, : 2 * N + HEADS]
    send.drain()
    main_sum.settle()
    side_sum.settle()


def call(kernel, outs, scratch, sems, collective, args, flops):
    vmem, anywhere = pltpu.VMEM, pl.ANY
    spec = {True: pl.BlockSpec(memory_space=anywhere), False: pl.BlockSpec(memory_space=vmem)}
    return pl.pallas_call(
        kernel,
        out_shape=[jax.ShapeDtypeStruct(shape, dtype) for shape, dtype, _ in outs],
        in_specs=[spec[far] for _, far in args],
        out_specs=[spec[far] for _, _, far in outs],
        scratch_shapes=[pltpu.VMEM(shape, dtype) for shape, dtype in scratch]
        + [pltpu.SemaphoreType.DMA((k,)) for k in sems],
        compiler_params=pltpu.CompilerParams(
            collective_id=collective, has_side_effects=True, vmem_limit_bytes=VMEM_BYTES
        ),
        cost_estimate=pl.CostEstimate(
            flops=flops,
            bytes_accessed=sum(a.size * a.dtype.itemsize for a, _ in args),
            transcendentals=0,
        ),
        name=kernel.__name__,
    )(*[a for a, _ in args])


def deliver_kernel(*refs):
    count = (len(refs) - 2) // 3
    ins, outs, held = refs[:count], refs[count : 2 * count], refs[2 * count : 3 * count]
    sems = refs[-2:]
    copies = [
        [
            pltpu.make_async_copy(source, middle, sems[0].at[k]),
            pltpu.make_async_copy(middle, target, sems[1].at[k]),
        ]
        for k, (source, middle, target) in enumerate(zip(ins, held, outs))
    ]
    for copy, _ in copies:
        copy.start()
    for first, second in copies:
        first.wait()
        second.start()
    for _, copy in copies:
        copy.wait()


def deliver(arrays):
    anywhere = pl.BlockSpec(memory_space=pl.ANY)
    return pl.pallas_call(
        deliver_kernel,
        out_shape=[jax.ShapeDtypeStruct(a.shape, a.dtype) for a in arrays],
        in_specs=[anywhere] * len(arrays),
        out_specs=[anywhere] * len(arrays),
        scratch_shapes=[pltpu.VMEM(a.shape, a.dtype) for a in arrays]
        + [pltpu.SemaphoreType.DMA((len(arrays),))] * 2,
        compiler_params=pltpu.CompilerParams(vmem_limit_bytes=VMEM_BYTES),
        name="deliver_kernel",
    )(*arrays)


def on_device(
    tokens,
    seq_len,
    norm_gain,
    main_weight,
    side_weight,
    side_terms,
    channel_terms,
    head_terms,
    output_weight,
    cotangent,
):
    count, span = BLOCKS * L, D // DP
    saved = [
        ((BLOCKS, GROUP, PIECE, D), bf16),
        ((DP, span, COLS), bf16),
        ((DP, span, 2 * IN), bf16),
        ((BLOCKS, 4, PIECE, D), bf16),
        ((count + 8, MIX), f32),
        ((BLOCKS, L, KEPT), bf16),
        ((BLOCKS, L, KEPT_F), f32),
        ((BLOCKS, 2 * HD, IN, N), bf16),
        ((BLOCKS, N, IN), f32),
        ((BLOCKS, 2, L // 2, IN), bf16),
        ((BLOCKS, 2, L // 2, IN), bf16),
    ]
    terms = [((8, MIX), f32), ((8, N), f32), ((1, IN), f32), ((1, IN), f32)]
    blocks = [((2, L, KEPT), bf16), ((2, L, KEPT_F), f32), ((2, 2 * HD, IN, N), bf16)]
    scratch = saved[:5] + saved[8:] + [((count, IN), f32), ((count, N), f32)] + blocks
    scratch += [((count, IN), f32), ((BLOCKS, L // 2, IN), bf16)] + terms
    scratch += [((L, 128), f32), ((N, IN), f32), ((GROUP, 8, L), f32)]
    own = [tokens[0], cotangent[0], seq_len.reshape(1, 1), norm_gain]
    weights = [main_weight, side_weight, output_weight.T]
    small = [channel_terms, side_terms, head_terms]
    *passed, sums = call(
        front_kernel,
        [(shape, dtype, True) for shape, dtype in saved] + [((L, 128), f32, False)],
        scratch,
        (192, 192, 28),
        0,
        [(a, False) for a in own + weights + small],
        12 * 10**9,
    )
    outs = call(
        back_kernel,
        [
            ((BLOCKS, PIECE, D), bf16, False),
            ((BLOCKS, PIECE, D), f32, False),
            ((D,), f32, False),
            ((span, 2, IN), f32, False),
            ((span, 2 * N + HEADS), f32, False),
            ((span, IN), f32, False),
            ((CONV + 1, 2 * N), f32, False),
            ((CONV + 2, IN), f32, False),
            ((3, HD), f32, False),
        ],
        [
            ((DP, span, COLS), bf16),
            ((DP, span, 2 * IN), bf16),
            ((BLOCKS, L // 2, 2 * IN), bf16),
            ((2, L + 8, MIX), f32),
            *blocks,
            ((2, N, IN), f32),
            ((2, 2, L // 2, IN), bf16),
            ((GROUP, PIECE, D), bf16),
            ((count, COLS), bf16),
            ((2, BLOCKS, GROUP, PIECE, 384), bf16),
            ((BLOCKS, 4, PIECE, D), bf16),
            ((4, 2, PIECE, D), bf16),
            ((4, 2, 2, PIECE, D), bf16),
            ((BLOCKS, GROUP, PIECE, D), bf16),
            ((4, 4, PIECE, D), bf16),
            ((4, 3, 2, PIECE // 2, D), bf16),
            ((4, 3, 2, PIECE, D), bf16),
            ((4, PIECE, D), bf16),
            ((4, PIECE, D), bf16),
            ((8, 2, span, COLS), bf16),
        ]
        + [
            shape
            for width in (2 * IN, 3 * N, 2 * IN)
            for shape in (
                ((8, span, width), bf16),
                ((3, 2, span, width), bf16),
                ((span, width), bf16),
                ((span, width), bf16),
            )
        ]
        + [((span, IN), f32), ((span, IN), f32)]
        + terms
        + [
            ((L, 128), f32),
            ((8, 2 * IN), f32),
            ((N, IN), f32),
            ((8, MIX), f32),
            ((1, D), f32),
            ((GROUP, 8, L), f32),
            ((GROUP, 8, IN), f32),
            ((span + 16, 2 * N), bf16),
            ((span + 16, 2 * N), bf16),
            ((4, span + 32, 2 * N), bf16),
            ((8, 8, 2 * IN), f32),
        ],
        (256, 256, 30),
        1,
        [(a, True) for a in passed] + [(a, False) for a in [sums] + own + small],
        24 * 10**9,
    )
    layer_out, token_grad, gain_grad, main_grad, side_grad, out_grad, *rest = deliver(outs)
    return (
        layer_out[None],
        token_grad[None],
        gain_grad,
        main_grad,
        side_grad,
        *rest,
        out_grad.T,
    )


def solution(mesh):
    placed = (
        P("dp", None, "mp", None),
        P("dp"),
        P(),
        P("dp", None, "mp"),
        P("dp", None),
        P(),
        P(None, "mp"),
        P(None, "mp"),
        P("mp", "dp"),
        P("dp", None, "mp", None),
    )
    return jax.shard_map(
        on_device,
        mesh=mesh,
        in_specs=placed,
        out_specs=(
            P("dp", None, "mp", None),
            P("dp", None, "mp", None),
            P(),
            P("dp", None, "mp"),
            P("dp", None),
            P(),
            P(None, "mp"),
            P(None, "mp"),
            P("mp", "dp"),
        ),
        check_vma=False,
    )
```
